32 devices in a mesh: wide: 8 (over z, x), narrow: 4 (over y, core).
Axes of the slice: x: 2, y: 2, z: 4, core: 2. Of those that a mesh axis runs over, the one named last changes fastest.
Arguments:
- tokens: bfloat16 [2, 32, 384, 768], P(None, ('wide', 'narrow')), may hold values from -6 to 6
- lengths: int32 [2, 32], P(None, ('wide', 'narrow')), may hold values from 96 to 384, as said below
- w_inward: bfloat16 [2, 1769472], P(None, ('wide', 'narrow')), may hold values from -0.21875 to 0.21875
- query_bias: bfloat16 [2, 768], P(None, ('wide', 'narrow')), may hold values from -1 to 1
- value_bias: bfloat16 [2, 768], P(None, ('wide', 'narrow')), may hold values from -1 to 1
- w_outward: bfloat16 [2, 589824], P(None, ('wide', 'narrow')), may hold values from -0.625 to 0.625
- outward_bias: bfloat16 [2, 768], P(None, ('wide', 'narrow')), may hold values from -1 to 1
- attn_gain: bfloat16 [2, 768], P(None, ('wide', 'narrow')), may hold values from 0.25 to 1.75
- attn_shift: bfloat16 [2, 768], P(None, ('wide', 'narrow')), may hold values from -1 to 1
- w_expand: bfloat16 [2, 2359296], P(None, ('wide', 'narrow')), may hold values from -0.21875 to 0.21875
- expand_bias: bfloat16 [2, 3072], P(None, ('wide', 'narrow')), may hold values from -1 to 1
- w_contract: bfloat16 [2, 2359296], P(None, ('wide', 'narrow')), may hold values from -0.15625 to 0.15625
- contract_bias: bfloat16 [2, 768], P(None, ('wide', 'narrow')), may hold values from -1 to 1
- ffn_gain: bfloat16 [2, 768], P(None, ('wide', 'narrow')), may hold values from 0.25 to 1.75
- ffn_shift: bfloat16 [2, 768], P(None, ('wide', 'narrow')), may hold values from -1 to 1
- cotangent: bfloat16 [2, 32, 384, 768], P(None, ('wide', 'narrow')), may hold values from -6 to 6
Outputs:
- layer_output: float32 [2, 32, 384, 768], P(None, ('wide', 'narrow'))
- grad_tokens: float32 [2, 32, 384, 768], P(None, ('wide', 'narrow'))
- grad_w_inward: float32 [2, 1769472], P(None, ('wide', 'narrow'))
- grad_query_bias: float32 [2, 768], P(None, ('wide', 'narrow'))
- grad_value_bias: float32 [2, 768], P(None, ('wide', 'narrow'))
- grad_w_outward: float32 [2, 589824], P(None, ('wide', 'narrow'))
- grad_outward_bias: float32 [2, 768], P(None, ('wide', 'narrow'))
- grad_attn_gain: float32 [2, 768], P(None, ('wide', 'narrow'))
- grad_attn_shift: float32 [2, 768], P(None, ('wide', 'narrow'))
- grad_w_expand: float32 [2, 2359296], P(None, ('wide', 'narrow'))
- grad_expand_bias: float32 [2, 3072], P(None, ('wide', 'narrow'))
- grad_w_contract: float32 [2, 2359296], P(None, ('wide', 'narrow'))
- grad_contract_bias: float32 [2, 768], P(None, ('wide', 'narrow'))
- grad_ffn_gain: float32 [2, 768], P(None, ('wide', 'narrow'))
- grad_ffn_shift: float32 [2, 768], P(None, ('wide', 'narrow'))
The draws below stay inside these ranges and needn't reach their ends.
Inputs may be any that keep to these rules, and one draw needn't show every extreme that they name: `lengths`: each micro-batch holds one sequence of exactly 384 real tokens and one of exactly 96; the rest of a row is padding.
All inputs are finite; a program needn't handle non-finite values.
Results may differ from the reference program's by a relative error of at most 0.019.
Values may be sent and summed in bfloat16 or wider, within the bound.
No kernel may reach another device: no remote copies, remote signals or barrier semaphores. Data moves between devices by JAX's collectives and lax.ppermute only.
A program may use at most 256 MiB of HBM per device.

```python
import jax
import jax.numpy as jnp
from jax import lax

D = 768
HEAD_DIM = 64
FF = 3072
LAYERS = 2
MICRO = 2
SEQ = 384
BATCH = 32


def draw_lengths(key, part):
    key = jax.random.fold_in(key, 11)
    key_spread, key_long, key_short = jax.random.split(key, 3)
    spread = jax.random.randint(key_spread, (MICRO, BATCH), SEQ // 4, SEQ + 1)
    longest = jax.random.randint(key_long, (MICRO, 1), 0, BATCH)
    offset = jax.random.randint(key_short, (MICRO, 1), 1, BATCH)
    shortest = (longest + offset) % BATCH
    places = lax.broadcasted_iota(jnp.int32, (MICRO, BATCH), 1)
    result = jnp.where(places == longest, SEQ, jnp.where(places == shortest, SEQ // 4, spread))
    return result.astype(jnp.int32)


def spiked(values, stream_key, source, target, blocks, factor):
    def block_of(dim):
        return (jnp.arange(values.shape[dim]) // (values.shape[dim] // blocks)).reshape((-1,) + (1,) * (values.ndim - 1 - dim))

    near = jax.random.permutation(stream_key, blocks)[block_of(target)]
    far = (block_of(target) + blocks // 2) % blocks
    return jnp.where((block_of(source) == near) | (block_of(source) == far), factor * values, values)


def levels(key, extent, shards, smallest, high):
    gain, own = 1.0, jax.random.fold_in(key, 6)
    for position, parts in shards:
        steps = jnp.exp(jax.random.uniform(jax.random.fold_in(own, position), (parts,), jnp.float32, smallest / len(shards), high / len(shards)))
        gain = gain * jnp.repeat(steps, extent[position] // parts).reshape([-1 if axis == position else 1 for axis in range(len(extent))])
    return gain


def scatter_about(stream_key, shape, width, most, cuts=(), kind=jnp.bfloat16):
    loudness = levels(stream_key, shape, cuts, -0.22, 0.18) if cuts else 1.0
    entries = jax.random.normal(stream_key, shape, jnp.float32) * width * loudness
    return jnp.minimum(jnp.maximum(entries, -most), most).astype(kind)


def heavy_noise(stream_key, shape, deviation, reach, cuts, heavy, kind=jnp.bfloat16):
    values = deviation * jax.random.normal(stream_key, shape, jnp.float32)
    if cuts:
        values = values * levels(stream_key, shape, cuts, -0.22, 0.18)
    return jnp.clip(spiked(values, jax.random.fold_in(stream_key, 3), *heavy), -reach, reach).astype(kind)


def setup_inputs(seed: int = 0) -> dict:
    streams_of = jax.random.split(jax.random.key(seed), 17)
    return {
        "tokens": scatter_about(streams_of[0], (MICRO, BATCH, SEQ, D), 1.0, 6.0, ((1, 32),)),
        "lengths": draw_lengths(jax.random.fold_in(streams_of[16], 71), 0),
        "w_inward": scatter_about(streams_of[2], (LAYERS, 3 * D * D), D ** -0.5, 0.21875, ((1, 32),)),
        "query_bias": scatter_about(streams_of[3], (LAYERS, D), 0.2, 1.0, ((1, 32),)),
        "value_bias": scatter_about(streams_of[4], (LAYERS, D), 0.2, 1.0, ((1, 32),)),
        "w_outward": scatter_about(streams_of[5], (LAYERS, D * D), (D // 8) ** -0.5, 0.625, ((1, 32),)),
        "outward_bias": scatter_about(streams_of[6], (LAYERS, D), 0.2, 1.0, ((1, 32),)),
        "attn_gain": jnp.clip(1.0 + 0.15 * jax.random.normal(streams_of[7], (LAYERS, D), jnp.float32), 0.25, 1.75).astype(jnp.bfloat16),
        "attn_shift": scatter_about(streams_of[8], (LAYERS, D), 0.2, 1.0, ((1, 32),)),
        "w_expand": scatter_about(streams_of[9], (LAYERS, D * FF), D ** -0.5, 0.21875, ((1, 32),)),
        "expand_bias": scatter_about(streams_of[10], (LAYERS, FF), 0.2, 1.0, ((1, 32),)),
        "w_contract": scatter_about(streams_of[11], (LAYERS, FF * D), (FF // 2) ** -0.5, 0.15625, ((1, 32),)),
        "contract_bias": scatter_about(streams_of[12], (LAYERS, D), 0.2, 1.0, ((1, 32),)),
        "ffn_gain": jnp.clip(1.0 + 0.15 * jax.random.normal(streams_of[13], (LAYERS, D), jnp.float32), 0.25, 1.75).astype(jnp.bfloat16),
        "ffn_shift": scatter_about(streams_of[14], (LAYERS, D), 0.2, 1.0, ((1, 32),)),
        "cotangent": heavy_noise(streams_of[15], (MICRO, BATCH, SEQ, D), 1.0, 6.0, ((1, 32),), (1, 3, 32, 2.75)),
    }


@jax.custom_vjp
def low(v):
    return lax.optimization_barrier(v.astype(jnp.bfloat16)).astype(jnp.float32)

@jax.custom_vjp
def low_back(v):
    return v

def low_keep(v):
    return (low(v), None)

def low_pass(kept, grad):
    return (grad,)

def back_keep(v):
    return (v, None)

def back_low(kept, grad):
    return (low(grad),)
low.defvjp(low_keep, low_pass)
low_back.defvjp(back_keep, back_low)
epsilon = 1e-06
highest = lax.Precision.HIGHEST

def layer_norm(inputs, gain_vector, shift_vector):
    centred = inputs - lax.optimization_barrier(jnp.mean(inputs, axis=-1, keepdims=True))
    variance = lax.optimization_barrier(jnp.mean(centred * centred, axis=-1, keepdims=True))
    return centred * lax.rsqrt(variance + epsilon) * gain_vector + shift_vector

def project(inputs, matrix):
    return jnp.einsum('gsd,de->gse', inputs, matrix, precision=highest)

def one_layer(inputs, weights, valid_keys):
    w_inward, query_bias, value_bias, w_outward, outward_bias, attn_gain, attn_shift, w_expand, expand_bias, w_contract, contract_bias, ffn_gain, ffn_shift = weights
    groups, length, model_width = inputs.shape
    head_count = model_width // HEAD_DIM
    joined = project(low(inputs), w_inward)
    queries = low(low_back(joined[..., :model_width] + query_bias))
    keys_all = low(low_back(joined[..., model_width:2 * model_width]))
    values_all = low(low_back(joined[..., 2 * model_width:] + value_bias))
    shape_heads = (groups, length, head_count, HEAD_DIM)
    scores = jnp.einsum('gqhe,gkhe->ghqk', queries.reshape(shape_heads), keys_all.reshape(shape_heads), precision=highest)
    scores = low_back(scores * HEAD_DIM ** (-0.5))
    scores = jnp.where(valid_keys[:, None, None, :], scores, -1e+30)
    soft_weights = low(jax.nn.softmax(scores, axis=-1))
    attended = jnp.einsum('ghqk,gkhe->gqhe', soft_weights, values_all.reshape(shape_heads), precision=highest)
    attended = low(low_back(attended.reshape(groups, length, model_width)))
    branch = low_back(project(attended, w_outward) + outward_bias)
    first_out = layer_norm(inputs + branch, attn_gain, attn_shift)
    hidden_pre = low_back(project(low(first_out), w_expand) + expand_bias)
    hidden = low(jax.nn.gelu(hidden_pre, approximate=False))
    branch_two = low_back(project(hidden, w_contract) + contract_bias)
    return layer_norm(first_out + branch_two, ffn_gain, ffn_shift)

def reference(tokens, lengths, w_inward, query_bias, value_bias, w_outward, outward_bias, attn_gain, attn_shift, w_expand, expand_bias, w_contract, contract_bias, ffn_gain, ffn_shift, cotangent):
    shaped = (w_inward.reshape(LAYERS, D, 3 * D), query_bias, value_bias, w_outward.reshape(LAYERS, D, D), outward_bias, attn_gain, attn_shift, w_expand.reshape(LAYERS, D, FF), expand_bias, w_contract.reshape(LAYERS, FF, D), contract_bias, ffn_gain, ffn_shift)
    stacked = tuple((member.astype(jnp.float32) for member in shaped))
    bundle = 8
    rounds = MICRO * BATCH // bundle
    token_groups = tokens.astype(jnp.float32).reshape(rounds, bundle, SEQ, D)
    upstream_groups = cotangent.astype(jnp.float32).reshape(rounds, bundle, SEQ, D)
    length_groups = lengths.reshape(rounds, bundle)
    places = lax.broadcasted_iota(jnp.int32, (bundle, SEQ), 1)

    def forward(inputs, params, valid_keys):
        stream = inputs
        for layer_index in range(LAYERS):
            stream = one_layer(stream, tuple((member[layer_index] for member in params)), valid_keys)
        return stream

    def scan_step(totals, pieces):
        inputs, upstream, counts = pieces
        valid_keys = places < counts[:, None]
        result, pullback = jax.vjp(lambda supplied, params: forward(supplied, params, valid_keys), inputs, stacked)
        grad_inputs, grad_params = pullback(upstream)
        summed = jax.tree.map(lambda running, adding: running + adding, totals, grad_params)
        return (summed, (result, grad_inputs))
    zero_grads = jax.tree.map(jnp.zeros_like, stacked)
    totals, (results, grad_inputs) = lax.scan(scan_step, zero_grads, (token_groups, upstream_groups, length_groups))
    shape_full = (MICRO, BATCH, SEQ, D)
    return (results.reshape(shape_full), grad_inputs.reshape(shape_full), totals[0].reshape(LAYERS, 3 * D * D), totals[1], totals[2], totals[3].reshape(LAYERS, D * D), totals[4], totals[5], totals[6], totals[7].reshape(LAYERS, D * FF), totals[8], totals[9].reshape(LAYERS, FF * D), totals[10], totals[11], totals[12])
```

```python
import math
from functools import partial

import jax
import jax.numpy as jnp
from jax import lax
from jax.experimental import pallas as pl
from jax.experimental.pallas import tpu as pltpu
from jax.sharding import PartitionSpec as P

HEAD_DIM = 64
EPSILON = 1e-06
AXES = ("wide", "narrow")
F32 = jnp.float32
BF16 = jnp.bfloat16
ANY = pl.BlockSpec(memory_space=pl.ANY)
VMEM = pl.BlockSpec(memory_space=pltpu.VMEM)
SMEM = pl.BlockSpec(memory_space=pltpu.SMEM)
LIMIT = 60 * 2**20
SHARE = 48


def mm(left, right, over=(1, 0)):
    return lax.dot_general(
        left, right, (((over[0],), (over[1],)), ((), ())), preferred_element_type=F32
    )


def nt(left, right):
    return mm(left, right, (1, 1))


def tn(left, right):
    return mm(left, right, (0, 0))


def norm_rows(h):
    centred = h - jnp.mean(h, axis=-1, keepdims=True)
    inv = lax.rsqrt(jnp.mean(centred * centred, axis=-1, keepdims=True) + EPSILON)
    return centred * inv, inv


def norm_rows_back(g, n, inv, gain):
    t = g * gain
    return inv * (
        t
        - jnp.mean(t, axis=-1, keepdims=True)
        - n * jnp.mean(t * n, axis=-1, keepdims=True)
    )


def gelu_pair(f):
    u = jnp.abs(f)
    t = 1.0 / (1.0 + (0.3275911 / math.sqrt(2.0)) * u)
    e = jnp.exp(-0.5 * f * f)
    c = [0.5 * v for v in (0.254829592, -0.284496736, 1.421413741, -1.453152027, 1.061405429)]
    tail = e * (t * (c[0] + t * (c[1] + t * (c[2] + t * (c[3] + t * c[4])))))
    phi = jnp.where(f >= 0, 1.0 - tail, tail)
    return f * phi, phi + f * (e * (1.0 / math.sqrt(2.0 * math.pi)))


def even_lanes():
    return lax.broadcasted_iota(jnp.int32, (1, 2 * HEAD_DIM), 1) < HEAD_DIM


def place_of(idx, block, far, first_is_x):
    k, other = block % 4, block // 4
    z = idx[0] ^ (3 * (k % 2)) ^ (k // 2)
    if first_is_x:
        x, y = idx[1] ^ other, idx[2] ^ far
    else:
        x, y = idx[1] ^ far, idx[2] ^ other
    return z * 4 + x * 2 + y


def relative_of(idx, chip, first_is_x):
    r = (chip // 4) ^ idx[0]
    k = (r // 2) + 2 * ((r ^ (r // 2)) % 2)
    i = (chip // 2 % 2) ^ idx[1]
    j = (chip % 2) ^ idx[2]
    return (i * 8 + j * 4 + k) if first_is_x else (j * 8 + i * 4 + k)


def copy(src, dst, sem):
    return pltpu.make_async_copy(src, dst, sem)


def attn_forward_kernel(count, idx, x_ref, vec, *refs):
    given, refs = refs[:count], refs[count:]
    y1_ref, n1_ref, r1_ref, qkv_ref, p_ref, att_ref, w_ref, w, qkv, p, att, sem_in, sem_out = refs
    c = idx[3]

    def fetch(block, carry):
        for s, pieces in enumerate((given[:4], given[4:8])):
            for far in range(2):
                chip = place_of(idx, block, far, s == 0)
                rows = pl.ds(pl.multiple_of(chip * SHARE, SHARE), SHARE)
                for side in range(2):
                    copy(
                        pieces[2 * side + far].at[block, 0],
                        w.at[2 * s + (c ^ side), rows],
                        sem_in.at[2 * s + side],
                    ).start()
        return carry

    def fetch_whole(chip, carry):
        rows = pl.ds(pl.multiple_of(chip * SHARE, SHARE), SHARE)
        for s in range(2):
            for core in range(2):
                copy(given[0].at[2 * chip + core, 0, s], w.at[2 * s + core, rows], sem_in.at[2 * s + core]).start()
        return carry

    if count == 1:
        lax.fori_loop(0, 16, fetch_whole, 0)
    else:
        lax.fori_loop(0, 8, fetch, 0)
    for i in range(4):
        copy(w.at[0], w.at[0], sem_in.at[i]).wait()
    save_w = copy(w, w_ref, sem_out.at[0])
    save_w.start()
    length = x_ref.shape[0] // 2
    for n in range(2):
        rows = slice(n * length, (n + 1) * length)
        xr = x_ref[rows].astype(BF16)
        qkv[0, rows] = (mm(xr, w[0]) + vec[0:1]).astype(BF16)
        qkv[1, rows] = mm(xr, w[1]).astype(BF16)
        qkv[2, rows] = (mm(xr, w[2]) + vec[1:2]).astype(BF16)
    save_qkv = copy(qkv, qkv_ref, sem_out.at[1])
    save_qkv.start()
    pairs = x_ref.shape[1] // (2 * HEAD_DIM)
    places = lax.broadcasted_iota(jnp.int32, (1, length), 1)

    def pair(step, carry):
        n, j = step // pairs, step % pairs
        rows = pl.ds(pl.multiple_of(n * length, length), length)
        lanes = pl.ds(pl.multiple_of(j * 2 * HEAD_DIM, 2 * HEAD_DIM), 2 * HEAD_DIM)
        even = even_lanes()
        hidden = jnp.where(places < idx[4 + n], 0.0, -1e30)
        q2 = qkv[0, rows, lanes] * jnp.asarray(HEAD_DIM**-0.5, BF16)
        k2 = qkv[1, rows, lanes]
        v2 = qkv[2, rows, lanes]
        parts = []
        for h in range(2):
            mine = even if h == 0 else jnp.logical_not(even)
            s = nt(jnp.where(mine, q2, jnp.zeros_like(q2)), k2) + hidden
            e = jnp.exp(s - jnp.max(s, axis=-1, keepdims=True))
            soft = (e * (1.0 / jnp.sum(e, axis=-1, keepdims=True))).astype(BF16)
            p[2 * step + h] = soft
            parts.append(mm(soft, v2))
        att[rows, lanes] = jnp.where(even, parts[0], parts[1]).astype(BF16)
        copy(p.at[pl.ds(2 * step, 2)], p_ref.at[pl.ds(2 * step, 2)], sem_out.at[2]).start()
        return carry

    lax.fori_loop(0, 2 * pairs, pair, 0)
    save_att = copy(att, att_ref, sem_out.at[3])
    save_att.start()
    for n in range(2):
        rows = slice(n * length, (n + 1) * length)
        h = x_ref[rows].astype(F32) + (mm(att[rows], w[3]) + vec[2:3])
        normed, inv = norm_rows(h)
        n1_ref[rows] = normed
        r1_ref[rows] = inv
        y1_ref[rows] = normed * vec[3:4] + vec[4:5]
    save_w.wait()
    save_qkv.wait()
    copy(p, p_ref, sem_out.at[2]).wait()
    save_att.wait()


def attn_forward(idx, x, vec, pieces):
    t, d = x.shape
    heads = d // HEAD_DIM
    length = t // 2
    return pl.pallas_call(
        partial(attn_forward_kernel, len(pieces)),
        in_specs=[SMEM, VMEM, VMEM] + [ANY] * len(pieces),
        out_specs=[VMEM, VMEM, VMEM, ANY, ANY, ANY, ANY],
        out_shape=[
            jax.ShapeDtypeStruct((t, d), F32),
            jax.ShapeDtypeStruct((t, d), F32),
            jax.ShapeDtypeStruct((t, 1), F32),
            jax.ShapeDtypeStruct((3, t, d), BF16),
            jax.ShapeDtypeStruct((2 * heads, length, length), BF16),
            jax.ShapeDtypeStruct((t, d), BF16),
            jax.ShapeDtypeStruct((4, d, d), BF16),
        ],
        scratch_shapes=[
            pltpu.VMEM((4, d, d), BF16),
            pltpu.VMEM((3, t, d), BF16),
            pltpu.VMEM((2 * heads, length, length), BF16),
            pltpu.VMEM((t, d), BF16),
            pltpu.SemaphoreType.DMA((4,)),
            pltpu.SemaphoreType.DMA((4,)),
        ],
        compiler_params=pltpu.CompilerParams(vmem_limit_bytes=LIMIT),
        cost_estimate=pl.CostEstimate(flops=8 * t * d * d + 4 * t * length * d, bytes_accessed=40 * 2**20, transcendentals=2 * heads * length * length),
        name="attn_forward",
    )(idx, x, vec, *pieces)


def ffn_forward_kernel(count, idx, y1_ref, vec, *refs):
    given, refs = refs[:count], refs[count:]
    x_ref, n2_ref, r2_ref, ur_ref, gp_ref, we_ref, wc_ref, we, wc, ur, gp, acc, sem_in, sem_out = refs
    c = idx[3]

    def fetch(block, carry):
        for s, pieces in enumerate((given[:4], given[4:8])):
            for far in range(2):
                chip = place_of(idx, block, far, s == 0)
                rows = pl.ds(pl.multiple_of(chip * SHARE, SHARE), SHARE)
                for side in range(2):
                    core = c ^ side
                    piece = pieces[2 * side + far]
                    copy(piece.at[block, 0], we.at[2 * core + s, rows], sem_in.at[2 * s + side]).start()
                    down = pl.ds(pl.multiple_of(chip * 4 * SHARE + core * 2 * SHARE + s * SHARE, SHARE), SHARE)
                    copy(piece.at[block, 1], wc.at[down], sem_in.at[4 + 2 * s + side]).start()
        return carry

    def fetch_whole(chip, carry):
        rows = pl.ds(pl.multiple_of(chip * SHARE, SHARE), SHARE)
        for s in range(2):
            for core in range(2):
                share = given[0].at[2 * chip + core]
                copy(share.at[1, s], we.at[2 * core + s, rows], sem_in.at[2 * s + core]).start()
                down = pl.ds(pl.multiple_of(chip * 4 * SHARE + core * 2 * SHARE + s * SHARE, SHARE), SHARE)
                copy(share.at[2, s], wc.at[down], sem_in.at[4 + 2 * s + core]).start()
        return carry

    if count == 1:
        lax.fori_loop(0, 16, fetch_whole, 0)
    else:
        lax.fori_loop(0, 8, fetch, 0)
    for i in range(4):
        copy(we.at[0], we.at[0], sem_in.at[i]).wait()
    save_we = copy(we, we_ref, sem_out.at[0])
    save_we.start()
    d = y1_ref.shape[1]
    length = y1_ref.shape[0] // 2
    save_wc = copy(wc, wc_ref, sem_out.at[1])
    for j in range(4):
        cols = slice(j * d, (j + 1) * d)
        for n in range(2):
            rows = slice(n * length, (n + 1) * length)
            f = mm(y1_ref[rows].astype(BF16), we[j]) + vec[5 + j : 6 + j]
            u, slope = gelu_pair(f)
            u = u.astype(BF16)
            ur[j, rows] = u
            gp[j, rows] = slope.astype(BF16)
            if j == 0 and n == 0:
                for i in range(4):
                    copy(we.at[0], we.at[0], sem_in.at[4 + i]).wait()
                save_wc.start()
            part = mm(u, wc[cols])
            if j == 0:
                acc[rows] = part
            else:
                acc[rows] += part
        copy(ur.at[j], ur_ref.at[j], sem_out.at[2]).start()
        copy(gp.at[j], gp_ref.at[j], sem_out.at[3]).start()
    for n in range(2):
        rows = slice(n * length, (n + 1) * length)
        normed, inv = norm_rows(y1_ref[rows] + (acc[rows] + vec[9:10]))
        n2_ref[rows] = normed
        r2_ref[rows] = inv
        x_ref[rows] = normed * vec[10:11] + vec[11:12]
    save_we.wait()
    save_wc.wait()
    copy(ur, ur_ref, sem_out.at[2]).wait()
    copy(gp, gp_ref, sem_out.at[3]).wait()


def ffn_forward(idx, y1, vec, pieces):
    t, d = y1.shape
    hidden = 4 * d
    return pl.pallas_call(
        partial(ffn_forward_kernel, len(pieces)),
        in_specs=[SMEM, VMEM, VMEM] + [ANY] * len(pieces),
        out_specs=[VMEM, VMEM, VMEM, ANY, ANY, ANY, ANY],
        out_shape=[
            jax.ShapeDtypeStruct((t, d), F32),
            jax.ShapeDtypeStruct((t, d), F32),
            jax.ShapeDtypeStruct((t, 1), F32),
            jax.ShapeDtypeStruct((4, t, d), BF16),
            jax.ShapeDtypeStruct((4, t, d), BF16),
            jax.ShapeDtypeStruct((4, d, d), BF16),
            jax.ShapeDtypeStruct((hidden, d), BF16),
        ],
        scratch_shapes=[
            pltpu.VMEM((4, d, d), BF16),
            pltpu.VMEM((hidden, d), BF16),
            pltpu.VMEM((4, t, d), BF16),
            pltpu.VMEM((4, t, d), BF16),
            pltpu.VMEM((t, d), F32),
            pltpu.SemaphoreType.DMA((8,)),
            pltpu.SemaphoreType.DMA((4,)),
        ],
        compiler_params=pltpu.CompilerParams(vmem_limit_bytes=LIMIT),
        cost_estimate=pl.CostEstimate(flops=4 * t * d * hidden, bytes_accessed=40 * 2**20, transcendentals=2 * t * hidden),
        name="ffn_forward",
    )(idx, y1, vec, *pieces)


def send_rows(idx, block, chip, core, s, m, sums, sem):
    if len(sums) == 1:
        copy(block, sums[0].at[2 * chip + core, s, m], sem).start()
        return
    keep, give = sums
    to = jnp.where(s == 1, relative_of(idx, chip, True), relative_of(idx, chip, False))

    @pl.when(core == idx[3])
    def _():
        copy(block, keep.at[s, to, m], sem).start()

    @pl.when(core != idx[3])
    def _():
        copy(block, give.at[s, to, m], sem).start()


def send_square(idx, stage, core, s, m, sums, sem):
    def go(chip, carry):
        rows = pl.ds(pl.multiple_of(chip * SHARE, SHARE), SHARE)
        send_rows(idx, stage.at[rows], chip, core, s, m, sums, sem)
        return carry

    lax.fori_loop(0, 16, go, 0)


def sums_shapes(d, whole, m=1):
    if whole:
        return [jax.ShapeDtypeStruct((32, 2, m, SHARE, d), BF16)]
    return [jax.ShapeDtypeStruct((2, 16, 1, SHARE, d), BF16)] * 2


def halves_of(ref):
    length = ref.shape[0] // 2
    return [slice(n * length, (n + 1) * length) for n in range(2)]


def add_small(ref, row, value):
    ref[row : row + 1] += jnp.sum(value.astype(F32), axis=0, keepdims=True)


def contract_backward_kernel(count, idx, g_ref, n2_ref, r2_ref, vec, ur_ref, gp_ref, wc_ref, *refs):
    dh2_ref, small_ref, ef_ref = refs[:3]
    sums, refs = refs[3 : 3 + count], refs[3 + count :]
    wc, ur, gp, stage, e2, sem_in, sem_out = refs
    d = g_ref.shape[1]
    loads = []
    for j in range(4):
        cols = pl.ds(j * d, d)
        loads.append([
            copy(ur_ref.at[j], ur.at[j], sem_in.at[3 * j]),
            copy(wc_ref.at[cols], wc.at[cols], sem_in.at[3 * j + 1]),
            copy(gp_ref.at[j], gp.at[j], sem_in.at[3 * j + 2]),
        ])
        for load in loads[j]:
            load.start()
    small_ref[...] = jnp.zeros_like(small_ref)
    for rows in halves_of(g_ref):
        g, normed = g_ref[rows].astype(F32), n2_ref[rows]
        add_small(small_ref, 5, g * normed)
        add_small(small_ref, 6, g)
        dh2 = norm_rows_back(g, normed, r2_ref[rows], vec[10:11])
        low = dh2.astype(BF16)
        add_small(small_ref, 4, low)
        dh2_ref[rows] = dh2
        e2[rows] = low
    for j in range(4):
        cols = slice(j * d, (j + 1) * d)
        for load in loads[j]:
            load.wait()
        stage[j] = tn(ur[j], e2[...]).astype(BF16)

        def go(b, carry):
            rows = pl.ds(pl.multiple_of(b * SHARE, SHARE), SHARE)
            send_rows(idx, stage.at[j, rows], 4 * j + b // 4, b // 2 % 2, b % 2, len(sums) % 2, sums, sem_out.at[0])
            return carry

        lax.fori_loop(0, 16, go, 0)
        for rows in halves_of(g_ref):
            ef = (nt(e2[rows], wc[cols]) * gp[j, rows].astype(F32)).astype(BF16)
            gp[j, rows] = ef
            add_small(small_ref, j, ef)
        copy(gp.at[j], ef_ref.at[j], sem_out.at[1]).start()
    copy(stage, stage, sem_out.at[0]).wait()
    copy(gp, ef_ref, sem_out.at[1]).wait()


def contract_backward(whole, idx, g, n2, r2, vec, ur, gp, wc):
    t, d = n2.shape
    sums = sums_shapes(d, whole, 2)
    return pl.pallas_call(
        partial(contract_backward_kernel, len(sums)),
        in_specs=[SMEM] + [VMEM] * 4 + [ANY] * 3,
        out_specs=[VMEM, VMEM, ANY] + [ANY] * len(sums),
        out_shape=[
            jax.ShapeDtypeStruct((t, d), F32),
            jax.ShapeDtypeStruct((8, d), F32),
            jax.ShapeDtypeStruct((4, t, d), BF16),
            *sums,
        ],
        scratch_shapes=[
            pltpu.VMEM((4 * d, d), BF16),
            pltpu.VMEM((4, t, d), BF16),
            pltpu.VMEM((4, t, d), BF16),
            pltpu.VMEM((4, d, d), BF16),
            pltpu.VMEM((t, d), BF16),
            pltpu.SemaphoreType.DMA((12,)),
            pltpu.SemaphoreType.DMA((2,)),
        ],
        compiler_params=pltpu.CompilerParams(vmem_limit_bytes=LIMIT),
        cost_estimate=pl.CostEstimate(flops=16 * t * d * d, bytes_accessed=40 * 2**20, transcendentals=0),
        name="contract_backward",
    )(idx, g, n2, r2, vec, ur, gp, wc)


def expand_backward_kernel(count, idx, dh2_ref, n1_ref, r1_ref, vec, ef_ref, we_ref, w_ref, *refs):
    if count == 1:
        refs = refs[1:]
    dh1_ref, small_ref, da_ref = refs[:3]
    sums, refs = refs[3 : 3 + count], refs[3 + count :]
    we, ef, wo, stage, y1r, dy1, sem_in, sem_out = refs
    loads = []
    for j in range(4):
        loads.append([copy(ef_ref.at[j], ef.at[j], sem_in.at[2 * j]), copy(we_ref.at[j], we.at[j], sem_in.at[2 * j + 1])])
        for load in loads[j]:
            load.start()
    last = copy(w_ref.at[3], wo, sem_in.at[8])
    last.start()
    small_ref[...] = jnp.zeros_like(small_ref)
    for rows in halves_of(dh2_ref):
        y1r[rows] = (n1_ref[rows] * vec[3:4] + vec[4:5]).astype(BF16)
    for j in range(4):
        for load in loads[j]:
            load.wait()
        stage[j] = tn(y1r[...], ef[j]).astype(BF16)
        send_square(idx, stage.at[j], j // 2, j % 2, 0, sums, sem_out.at[0])
        for rows in halves_of(dh2_ref):
            part = nt(ef[j, rows], we[j])
            dy1[rows] = (dh2_ref[rows] if j == 0 else dy1[rows]) + part
    last.wait()
    for rows in halves_of(dh2_ref):
        g, normed = dy1[rows], n1_ref[rows]
        add_small(small_ref, 1, g * normed)
        add_small(small_ref, 2, g)
        dh1 = norm_rows_back(g, normed, r1_ref[rows], vec[3:4])
        dh1_ref[rows] = dh1
        e1 = dh1.astype(BF16)
        add_small(small_ref, 0, e1)
        da_ref[rows] = nt(e1, wo[...]).astype(BF16)
    copy(stage, stage, sem_out.at[0]).wait()


def expand_backward(whole, idx, dh2, n1, r1, vec, ef, we, w, *passed):
    t, d = dh2.shape
    sums = sums_shapes(d, whole, 2)
    return pl.pallas_call(
        partial(expand_backward_kernel, len(sums)),
        in_specs=[SMEM] + [VMEM] * 4 + [ANY] * (3 + len(passed)),
        out_specs=[VMEM, VMEM, VMEM] + [ANY] * len(sums),
        input_output_aliases={8: 3} if passed else {},
        out_shape=[
            jax.ShapeDtypeStruct((t, d), F32),
            jax.ShapeDtypeStruct((8, d), F32),
            jax.ShapeDtypeStruct((t, d), BF16),
            *sums,
        ],
        scratch_shapes=[
            pltpu.VMEM((4, d, d), BF16),
            pltpu.VMEM((4, t, d), BF16),
            pltpu.VMEM((d, d), BF16),
            pltpu.VMEM((4, d, d), BF16),
            pltpu.VMEM((t, d), BF16),
            pltpu.VMEM((t, d), F32),
            pltpu.SemaphoreType.DMA((9,)),
            pltpu.SemaphoreType.DMA((1,)),
        ],
        compiler_params=pltpu.CompilerParams(vmem_limit_bytes=LIMIT),
        cost_estimate=pl.CostEstimate(flops=18 * t * d * d, bytes_accessed=40 * 2**20, transcendentals=0),
        name="expand_backward",
    )(idx, dh2, n1, r1, vec, ef, we, w, *passed)


def heads_backward_kernel(da_ref, qkv_ref, p_ref, back_ref, small_ref, p, sem_in):
    t, d = da_ref.shape
    length = t // 2
    pairs = d // (2 * HEAD_DIM)
    factor = HEAD_DIM**-0.5
    steps = 2 * pairs

    def load(step, slot):
        return copy(p_ref.at[pl.ds(2 * step, 2)], p.at[slot], sem_in.at[slot])

    load(0, 0).start()

    def pair(step, carry):
        slot = step % 2

        @pl.when(step + 1 < steps)
        def _():
            load(step + 1, 1 - slot).start()

        load(step, slot).wait()
        n, j = step // pairs, step % pairs
        rows = pl.ds(pl.multiple_of(n * length, length), length)
        lanes = pl.ds(pl.multiple_of(j * 2 * HEAD_DIM, 2 * HEAD_DIM), 2 * HEAD_DIM)
        even = even_lanes()
        q2, k2, v2 = (qkv_ref[i, rows, lanes] for i in range(3))
        da2 = da_ref[rows, lanes]
        dqs, dks, dvs = [], [], []
        for h in range(2):
            mine = even if h == 0 else jnp.logical_not(even)
            soft = p[slot, h]
            dp = nt(jnp.where(mine, da2, jnp.zeros_like(da2)), v2)
            dvs.append(tn(soft, da2))
            soft = soft.astype(F32)
            inner = jnp.sum(soft * dp, axis=-1, keepdims=True)
            ds = (soft * (dp - inner)).astype(BF16)
            dqs.append(mm(ds, k2))
            dks.append(tn(ds, q2))
        dq, dk, dv = (jnp.where(even, m[0], m[1]) for m in (dqs, dks, dvs))
        back_ref[0, rows, lanes] = (dq * factor).astype(BF16)
        back_ref[1, rows, lanes] = (dk * factor).astype(BF16)
        back_ref[2, rows, lanes] = dv.astype(BF16)
        return carry

    lax.fori_loop(0, steps, pair, 0)
    small_ref[0:1] = jnp.sum(back_ref[0].astype(F32), axis=0, keepdims=True)
    small_ref[1:2] = jnp.sum(back_ref[2].astype(F32), axis=0, keepdims=True)


def heads_backward(da, qkv, p):
    t, d = da.shape
    length = t // 2
    return pl.pallas_call(
        heads_backward_kernel,
        in_specs=[VMEM, VMEM, ANY],
        out_specs=[VMEM, VMEM],
        out_shape=[jax.ShapeDtypeStruct((3, t, d), BF16), jax.ShapeDtypeStruct((8, d), F32)],
        scratch_shapes=[pltpu.VMEM((2, 2, length, length), BF16), pltpu.SemaphoreType.DMA((2,))],
        compiler_params=pltpu.CompilerParams(vmem_limit_bytes=LIMIT),
        cost_estimate=pl.CostEstimate(flops=30 * t * length * d, bytes_accessed=20 * 2**20, transcendentals=0),
        name="heads_backward",
    )(da, qkv, p)


def inward_backward_kernel(count, idx, dh1_ref, x_ref, att_ref, back, w_ref, *refs):
    dx_ref = refs[0]
    sums, refs = refs[1 : 1 + count], refs[1 + count :]
    w, stage, sem_in, sem_out = refs
    load = copy(w_ref, w, sem_in.at[0])
    load.start()
    xr = x_ref[...].astype(BF16)
    for i, (core, s) in enumerate(((0, 0), (1, 0), (0, 1))):
        stage[i] = tn(xr, back[i]).astype(BF16)
        send_square(idx, stage.at[i], core, s, 0, sums, sem_out.at[0])
    stage[3] = tn(att_ref[...], dh1_ref[...].astype(BF16)).astype(BF16)
    send_square(idx, stage.at[3], 1, 1, 0, sums, sem_out.at[0])
    load.wait()
    for rows in halves_of(dh1_ref):
        dx_ref[rows] = dh1_ref[rows] + (nt(back[0, rows], w[0]) + nt(back[1, rows], w[1]) + nt(back[2, rows], w[2]))
    copy(stage, stage, sem_out.at[0]).wait()


def inward_backward(whole, idx, dh1, x, att, back, w):
    t, d = dh1.shape
    sums = sums_shapes(d, whole)
    return pl.pallas_call(
        partial(inward_backward_kernel, len(sums)),
        in_specs=[SMEM] + [VMEM] * 4 + [ANY],
        out_specs=[VMEM] + [ANY] * len(sums),
        out_shape=[jax.ShapeDtypeStruct((t, d), F32), *sums],
        scratch_shapes=[
            pltpu.VMEM((4, d, d), BF16),
            pltpu.VMEM((4, d, d), BF16),
            pltpu.SemaphoreType.DMA((1,)),
            pltpu.SemaphoreType.DMA((1,)),
        ],
        compiler_params=pltpu.CompilerParams(vmem_limit_bytes=LIMIT),
        cost_estimate=pl.CostEstimate(flops=14 * t * d * d, bytes_accessed=30 * 2**20, transcendentals=0),
        name="inward_backward",
    )(idx, dh1, x, att, back, w)


BITS = {"c": 1, "y": 2, "x": 4, "z1": 8, "z2": 16, "z3": 24}


def swap(array, by):
    return lax.ppermute(array, AXES, [(i, i ^ BITS[by]) for i in range(32)])


def tie(values, *others):
    return lax.optimization_barrier((values, others))[0]


def pair_up(share):
    return jnp.stack([share, swap(share, "z3")])


def column_up(pair):
    return jnp.concatenate([pair, swap(pair, "z1")])


def near_up(cols):
    return tuple(jnp.concatenate([col, swap(col, by)]) for col, by in zip(cols, "xy"))


def far_up(near):
    return tuple(swap(piece, by) for piece, by in zip(near, "yx"))


def other_core(pieces):
    return tuple(swap(piece, "c") for piece in pieces)


def in_order(near, far, near_c, far_c):
    return sum(((near[s], far[s], near_c[s], far_c[s]) for s in range(2)), ())


def place_small(qb, vb, ob, ag, ash, eb, cb, fg, fs, width, device):
    layers, rows = qb.shape
    lanes = lax.broadcasted_iota(jnp.int32, (1, 1, width), 2)
    thin = jnp.stack([qb, vb, ob, ag, ash, cb, fg, fs], axis=1).astype(F32)
    thin = jnp.where(lanes // rows == device, jnp.tile(thin, (1, 1, width // rows)), 0.0)
    lines = lax.broadcasted_iota(jnp.int32, (1, 4, width), 1)
    wide = jnp.tile(eb.astype(F32)[:, None], (1, 4, width // eb.shape[1]))
    wide = jnp.where(lines * (width // eb.shape[1]) + lanes // eb.shape[1] == device, wide, 0.0)
    return jnp.concatenate([thin[:, 0:5], wide, thin[:, 5:8], jnp.zeros((layers, 4, width), F32)], axis=1)


def own_small(total, rows, device):
    layers, _, width = total.shape
    thin = lax.dynamic_slice_in_dim(total, device * rows, rows, 2)
    count = width // (4 * rows)
    wide = lax.dynamic_slice(total, (0, 5 + device // count, device % count * 4 * rows), (layers, 1, 4 * rows))
    return [thin[:, i] for i in range(5)] + [wide[:, 0]] + [thin[:, i] for i in range(9, 12)]


def add_swap(array, by):
    return array + swap(array, by)


class Sums:
    def __init__(self, keep, give):
        self.both = [keep]
        self.parts = [[], []]
        self.give = give

    def total(self, s, lo, hi):
        whole = None
        for a in [b[s] for b in self.both] + self.parts[s]:
            a = a[lo:hi].astype(F32)
            whole = a if whole is None else whole + a
        return whole

    def latest(self):
        return self.parts if self.parts[0] else self.both

    def hold(self, *others):
        if self.parts[0]:
            self.parts = tie(self.parts, *others)
        else:
            self.both = tie(self.both, *others)

    def core(self):
        self.both = self.both + [swap(self.give, "c")]

    def plane(self, lo, bys):
        arrived = [swap(self.total(s, lo, 2 * lo).astype(BF16), bys[s]) for s in range(2)]
        for s in range(2):
            self.parts[s] = self.parts[s] + [arrived[s]]

    def first(self):
        self.plane(8, "yx")

    def second(self):
        self.plane(4, "xy")

    def line(self, lo, by):
        arrived = swap(jnp.stack([self.total(s, lo, 2 * lo) for s in range(2)]).astype(BF16), by)
        for s in range(2):
            self.parts[s] = self.parts[s] + [arrived[s]]

    def third(self):
        self.line(2, "z1")

    def fourth(self):
        self.line(1, "z3")

    def result(self):
        return jnp.stack([self.total(s, 0, 1)[0] for s in range(2)])


def front(first, last, rows, width, c, attention):
    layers = first.shape[0]
    first = first.reshape(layers, rows, -1)
    cut = lambda i: first[:, :, i * width : (i + 1) * width]
    if attention:
        zero, one = (cut(0), cut(2)), (cut(1), last.reshape(layers, rows, width))
    else:
        zero, one = (cut(0), cut(1)), (cut(2), cut(3))
    zero, one = jnp.stack(zero, 1), jnp.stack(one, 1)
    return jnp.where(c == 0, zero, one), jnp.where(c == 0, one, zero)


def both_cores(mine, got, c):
    return jnp.where(c == 0, jnp.concatenate([mine, got], 2), jnp.concatenate([got, mine], 2))


def gather_any(w_inward, w_outward, w_expand, w_contract, width):
    whole = lambda m, n: lax.all_gather(m, AXES, axis=0, tiled=True).reshape(-1, n)
    inward, outward = whole(w_inward, 3 * width), whole(w_outward, width)
    expand, contract = whole(w_expand, 4 * width), whole(w_contract, width)
    cut = lambda m, i: m[:, i * width : (i + 1) * width].reshape(16, SHARE, width)
    squares = [cut(inward, i) for i in range(3)] + [cut(outward, 0)] + [cut(expand, i) for i in range(4)]
    down = contract.reshape(16, 2, 2, SHARE, width)
    sides = []
    for core in range(2):
        pick = (core, 2 + core, 4 + 2 * core, 5 + 2 * core)
        pairs = [squares[i] for i in pick] + [down[:, core, s] for s in range(2)]
        sides.append(jnp.stack(pairs, 1).reshape(16, 3, 2, SHARE, width))
    return jnp.stack(sides, 1).reshape(32, 3, 2, SHARE, width)


def collect_any(attn, ffn, width):
    attn = attn.reshape(16, 2, 2, SHARE, width)
    ffn = ffn.reshape(16, 2, 2, 2, SHARE, width)
    expand, contract = ffn[:, :, :, 0], ffn[:, :, :, 1]
    inward = jnp.concatenate([attn[:, 0, 0], attn[:, 1, 0], attn[:, 0, 1]], axis=-1)
    expand = jnp.concatenate([expand[:, core, s] for core in range(2) for s in range(2)], axis=-1)
    return tuple(
        lax.psum_scatter(m.reshape(-1).astype(F32), AXES, scatter_dimension=0, tiled=True)
        for m in (inward, attn[:, 1, 1], expand, contract)
    )


def local(blocked, tokens, lengths, w_inward, qb, vb, w_outward, ob, ag, ash, w_expand, eb, w_contract, cb, fg, fs, cotangent):
    layers = w_inward.shape[0]
    width = tokens.shape[-1]
    rows = qb.shape[1]
    device = lax.axis_index("wide") * lax.axis_size("narrow") + lax.axis_index("narrow")
    me = device if blocked else jnp.int32(0)
    c = me & 1
    place = jnp.stack([me >> 3, (me >> 2) & 1, (me >> 1) & 1, c]).astype(jnp.int32)
    idx = jnp.concatenate([place, lengths.reshape(-1), jnp.zeros((2,), jnp.int32)])
    small = place_small(qb, vb, ob, ag, ash, eb, cb, fg, fs, width, device)
    x = tokens.reshape(-1, width)
    kept = []

    def keep_layer(x, attn, ffn):
        y1, n1, r1, qkv, p, att, w = attn
        out, n2, r2, ur, gp, we, wc = ffn
        kept.append((x, n1, r1, qkv, p, att, w, n2, r2, ur, gp, we, wc))
        return out

    if blocked:
        mine, got = front(w_inward, w_outward, rows, width, c, True)
        halves = lambda col: (col[:, 0, None], col[:, 1, None])
        halves2 = lambda col: (col[:, :, 0], col[:, :, 1])
        share_a = both_cores(mine, swap(got, "c"), c)
        small = add_swap(small, "c")
        mine, got = front(w_expand, None, rows, width, c, False)
        share_e = both_cores(mine, swap(got, "c"), c)
        contract = w_contract.reshape(layers, 2, SHARE, width)
        share_f = [jnp.stack([share_e[l], contract[l]]) for l in range(layers)]
        a_pair = pair_up(share_a[0])
        share, a_pair, small = tie((share_f[0], a_pair, small))
        f_pair = pair_up(share)
        a_col = column_up(a_pair)
        small = add_swap(small, "z1")
        f_pair, a_col, small = tie((f_pair, a_col, small))
        f_col = column_up(f_pair)
        a_near = near_up(halves(a_col))
        small = add_swap(small, "z2")
        a_near, small = tie((a_near, small))
        a_far = far_up(a_near)
        a_core = other_core(a_near)
        f_col, a_far, small = tie((f_col, a_far, small))
        f_near = near_up(halves2(f_col))
        small = add_swap(small, "x")
        a1_pair = pair_up(tie((share_a[1], a_far))[0])
        a_core += other_core(a_far)
        x, f_near, a1_pair, small = tie((x, f_near, a1_pair, small))
        f_far = far_up(f_near)
        small = add_swap(small, "y")
        a1_col = column_up(a1_pair)
        f_core = other_core(f_near)
        vecs = [small[l] for l in range(layers)]
        attn = attn_forward(idx, x, vecs[0], in_order(a_near, a_far, a_core[:2], a_core[2:]))
        f_far, a1_col, f_core, y1, share = tie((f_far, a1_col, f_core, attn[0], share_f[1]))
        f_core += other_core(f_far)
        a1_near = near_up(halves(a1_col))
        f1_pair = pair_up(share)
        y1, a1_near, f1_pair = tie((y1, a1_near, f1_pair))
        a1_far = far_up(a1_near)
        f1_col = column_up(f1_pair)
        ffn = ffn_forward(idx, y1, vecs[0], in_order(f_near, f_far, f_core[:2], f_core[2:]))
        x1 = keep_layer(x, (y1,) + tuple(attn[1:]), ffn)
        a1_far, f1_col, x1 = tie((a1_far, f1_col, x1))
        a1_core = other_core(a1_near + a1_far)
        f1_near = near_up(halves2(f1_col))
        x1, f1_near = tie((x1, f1_near))
        f1_far = far_up(f1_near)
        f1_core = other_core(f1_near)
        attn = attn_forward(idx, x1, vecs[1], in_order(a1_near, a1_far, a1_core[:2], a1_core[2:]))
        f1_far, f1_core, y1 = tie((f1_far, f1_core, attn[0]))
        f1_core += other_core(f1_far)
        ffn = ffn_forward(idx, y1, vecs[1], in_order(f1_near, f1_far, f1_core[:2], f1_core[2:]))
        output = keep_layer(x1, attn, ffn)
    else:
        small = lax.psum(small, AXES)
        vecs = [small[l] for l in range(layers)]
        for l in range(layers):
            pieces = (gather_any(w_inward[l], w_outward[l], w_expand[l], w_contract[l], width),)
            attn = attn_forward(idx, x, vecs[l], pieces)
            x = keep_layer(x, attn, ffn_forward(idx, attn[0], vecs[l], pieces))
        output = x
    g = cotangent.reshape(-1, width)
    w_sums, smalls = [None] * layers, [None] * layers

    def contract_back(l, g):
        x, n1, r1, qkv, p, att, w, n2, r2, ur, gp, we, wc = kept[l]
        return contract_backward(not blocked or l > 0, idx, g, n2, r2, vecs[l], ur, gp, wc)

    def expand_back(l, dh2, ef, *passed):
        x, n1, r1, qkv, p, att, w, n2, r2, ur, gp, we, wc = kept[l]
        return expand_backward(not blocked or l > 0, idx, dh2, n1, r1, vecs[l], ef, we, w, *passed)

    def heads_back(l, da):
        x, n1, r1, qkv, p, att, w, n2, r2, ur, gp, we, wc = kept[l]
        return heads_backward(da, qkv, p)

    def inward_back(l, dh1, back):
        x, n1, r1, qkv, p, att, w, n2, r2, ur, gp, we, wc = kept[l]
        return inward_backward(not blocked, idx, dh1, x, att, back, w)

    def small_rows(small_c, small_e, small_h):
        return jnp.concatenate([small_h[0:2], small_e[0:3], small_c[0:7]])

    if blocked:
        dh2, small_c, ef, whole = contract_back(1, g)
        dh1, small_e, da, whole = expand_back(1, dh2, ef, whole)
        f1 = lax.psum_scatter(whole, AXES, scatter_dimension=0, tiled=True)
        back, small_h = heads_back(1, da)
        smalls[1] = small_rows(small_c, small_e, small_h)
        g, *sums = inward_back(1, dh1, back)
        a1 = Sums(*sums)
        a1.core()
        dh2, small_c, ef, *sums = contract_back(0, g)
        c0 = Sums(*sums)
        ef, c0.give, a1.both = tie((ef, c0.give, a1.both))
        c0.core()
        a1.first()
        dh1, small_e, da, *sums = expand_back(0, dh2, ef)
        e0 = Sums(*sums)
        da, e0.give, a1.parts, c0.both = tie((da, e0.give, a1.parts, c0.both))
        e0.core()
        a1.second()
        c0.first()
        back, small_h = heads_back(0, da)
        smalls[0] = small_rows(small_c, small_e, small_h)
        back, a1.parts, c0.parts, e0.both = tie((back, a1.parts, c0.parts, e0.both))
        a1.third()
        c0.second()
        e0.first()
        g, *sums = inward_back(0, dh1, back)
        a0 = Sums(*sums)
        small, a0.give, a1.parts, c0.parts, e0.parts = tie((jnp.stack(smalls), a0.give, a1.parts, c0.parts, e0.parts))
        a0.core()
        e0.second()
        c0.third()
        a1.fourth()
        small = add_swap(small, "z2")
        small, a0.both, e0.parts, c0.parts = tie((small, a0.both, e0.parts, c0.parts))
        a0.first()
        e0.third()
        c0.fourth()
        small = add_swap(small, "z1")
        small, a0.parts, e0.parts, f1 = tie((small, a0.parts, e0.parts, f1))
        a0.second()
        e0.fourth()
        small = add_swap(small, "x")
        small, a0.parts, e0.parts = tie((small, a0.parts, e0.parts))
        a0.third()
        small = add_swap(small, "y")
        small, a0.parts = tie((small, a0.parts))
        a0.fourth()
        small = add_swap(small, "c")
        f1 = f1[0].astype(F32)
        a0, e0, c0, a1 = (m.result()[:, 0] for m in (a0, e0, c0, a1))
        w_sums = [(a0, e0, c0), (a1, f1[:, 0], f1[:, 1])]
    else:
        for l in reversed(range(layers)):
            dh2, small_c, ef, whole = contract_back(l, g)
            dh1, small_e, da, whole = expand_back(l, dh2, ef, whole)
            back, small_h = heads_back(l, da)
            g, sums_a = inward_back(l, dh1, back)
            smalls[l] = small_rows(small_c, small_e, small_h)
            w_sums[l] = collect_any(sums_a, whole, width)
        small = lax.psum(jnp.stack(smalls), AXES)
    names = ("qb", "vb", "ob", "ag", "as", "eb", "cb", "fg", "fs")
    outs = dict(zip(names, own_small(small, rows, device)))
    flat = {"in": [], "out": [], "ex": [], "co": []}
    for l in range(layers):
        if not blocked:
            for name, share in zip(("in", "out", "ex", "co"), w_sums[l]):
                flat[name].append(share)
            continue
        attn, expand, contract = w_sums[l]
        squares = jnp.stack([attn[0], attn[1], expand[0], expand[1]])
        low, high = squares[:, :rows], squares[:, rows:]
        mine = jnp.where(c == 0, low, high)
        got = swap(jnp.where(c == 0, high, low), "c")
        zero, one = jnp.where(c == 0, mine, got), jnp.where(c == 0, got, mine)
        flat["in"].append(jnp.concatenate([zero[0], one[0], zero[1]], axis=1).reshape(-1))
        flat["out"].append(one[1].reshape(-1))
        flat["ex"].append(jnp.concatenate([zero[2], zero[3], one[2], one[3]], axis=1).reshape(-1))
        flat["co"].append(contract.reshape(-1))
    flat = {k: jnp.stack(v) for k, v in flat.items()}
    shape = tokens.shape
    return (
        output.reshape(shape), g.reshape(shape), flat["in"], outs["qb"], outs["vb"], flat["out"], outs["ob"],
        outs["ag"], outs["as"], flat["ex"], outs["eb"], flat["co"], outs["cb"], outs["fg"], outs["fs"],
    )


def solution(mesh):
    flat = P(None, AXES)
    deep = P(None, AXES, None, None)
    blocked = mesh.shape["wide"] == 8 and mesh.shape["narrow"] == 4
    return jax.shard_map(
        partial(local, blocked),
        mesh=mesh,
        in_specs=(deep,) + (flat,) * 14 + (deep,),
        out_specs=(deep, deep) + (flat,) * 13,
        check_vma=False,
    )
```

```python
import math
from functools import partial

import jax
import jax.numpy as jnp
from jax import lax
from jax.experimental import pallas as pl
from jax.experimental.pallas import tpu as pltpu
from jax.sharding import PartitionSpec as P

HEAD_DIM = 64
EPSILON = 1e-06
AXES = ("wide", "narrow")
F32 = jnp.float32
BF16 = jnp.bfloat16
ANY = pl.BlockSpec(memory_space=pl.ANY)
VMEM = pl.BlockSpec(memory_space=pltpu.VMEM)
SMEM = pl.BlockSpec(memory_space=pltpu.SMEM)
LIMIT = 60 * 2**20
SHARE = 48


def mm(left, right, over=(1, 0)):
    return lax.dot_general(
        left, right, (((over[0],), (over[1],)), ((), ())), preferred_element_type=F32
    )


def nt(left, right):
    return mm(left, right, (1, 1))


def tn(left, right):
    return mm(left, right, (0, 0))


def norm_rows(h):
    centred = h - jnp.mean(h, axis=-1, keepdims=True)
    inv = lax.rsqrt(jnp.mean(centred * centred, axis=-1, keepdims=True) + EPSILON)
    return centred * inv, inv


def norm_rows_back(g, n, inv, gain):
    t = g * gain
    return inv * (
        t
        - jnp.mean(t, axis=-1, keepdims=True)
        - n * jnp.mean(t * n, axis=-1, keepdims=True)
    )


def gelu_pair(f):
    u = jnp.abs(f)
    t = 1.0 / (1.0 + (0.3275911 / math.sqrt(2.0)) * u)
    e = jnp.exp(-0.5 * f * f)
    c = [0.5 * v for v in (0.254829592, -0.284496736, 1.421413741, -1.453152027, 1.061405429)]
    tail = e * (t * (c[0] + t * (c[1] + t * (c[2] + t * (c[3] + t * c[4])))))
    phi = jnp.where(f >= 0, 1.0 - tail, tail)
    return f * phi, phi + f * (e * (1.0 / math.sqrt(2.0 * math.pi)))


def even_lanes():
    return lax.broadcasted_iota(jnp.int32, (1, 2 * HEAD_DIM), 1) < HEAD_DIM


def place_of(idx, block, far, first_is_x):
    k, other = block % 4, block // 4
    z = idx[0] ^ (3 * (k % 2)) ^ (k // 2)
    if first_is_x:
        x, y = idx[1] ^ other, idx[2] ^ far
    else:
        x, y = idx[1] ^ far, idx[2] ^ other
    return z * 4 + x * 2 + y


def relative_of(idx, chip, first_is_x):
    r = (chip // 4) ^ idx[0]
    k = (r // 2) + 2 * ((r ^ (r // 2)) % 2)
    i = (chip // 2 % 2) ^ idx[1]
    j = (chip % 2) ^ idx[2]
    return (i * 8 + j * 4 + k) if first_is_x else (j * 8 + i * 4 + k)


def copy(src, dst, sem):
    return pltpu.make_async_copy(src, dst, sem)


def halves_of(ref):
    length = ref.shape[0] // 2
    return [slice(n * length, (n + 1) * length) for n in range(2)]


def add_small(ref, row, value):
    ref[row : row + 1] += jnp.sum(value.astype(F32), axis=0, keepdims=True)


def load_halves(src, dst, sems, at):
    loads = [copy(src.at[rows], dst.at[rows], sems.at[at + n]) for n, rows in enumerate(halves_of(src))]
    for load in loads:
        load.start()
    return loads


def rows_of(chip):
    return pl.ds(pl.multiple_of(chip * SHARE, SHARE), SHARE)


def fetch_attn(idx, given, w, sem, cores=(None, None)):
    if len(given) == 1:

        def whole(chip, carry):
            for s in range(2):
                for core in (0, 1) if cores[s] is None else (cores[s],):
                    square = 2 * s + core
                    copy(given[0].at[2 * chip + core, 0, s], w.at[square, rows_of(chip)], sem.at[square]).start()
            return carry

        lax.fori_loop(0, 16, whole, 0)
        return

    def go(block, carry):
        for s in range(2):
            if cores[s] == -1:
                continue
            for side in range(2):
                core = idx[3] ^ side

                def start(s=s, side=side, core=core):
                    for far in range(2):
                        rows = rows_of(place_of(idx, block, far, s == 0))
                        copy(given[4 * s + 2 * side + far].at[block, 0], w.at[2 * s + core, rows], sem.at[2 * s + core]).start()

                if cores[s] is None:
                    start()
                else:
                    pl.when(core == cores[s])(start)
        return carry

    lax.fori_loop(0, 8, go, 0)


def wait_square(w, sem, square):
    copy(w.at[square], w.at[square], sem.at[square]).wait()


def fetch_ffn(idx, given, m, w, sem):
    def place(chip, core, s):
        if m == 0:
            return w.at[2 * core + s, rows_of(chip)]
        return w.at[pl.ds(pl.multiple_of((chip * 4 + core * 2 + s) * SHARE, SHARE), SHARE)]

    def whole(chip, carry):
        for s in range(2):
            for core in range(2):
                copy(given[0].at[2 * chip + core, 1 + m, s], place(chip, core, s), sem.at[2 * core + s]).start()
        return carry

    def go(block, carry):
        for s in range(2):
            for side in range(2):
                core = idx[3] ^ side
                for far in range(2):
                    chip = place_of(idx, block, far, s == 0)
                    copy(given[4 * s + 2 * side + far].at[block, m], place(chip, core, s), sem.at[2 * core + s]).start()
        return carry

    if len(given) == 1:
        lax.fori_loop(0, 16, whole, 0)
    else:
        lax.fori_loop(0, 8, go, 0)


def wait_rows(w, sem):
    quarter = w.shape[0] // 4
    for i in range(4):
        copy(w.at[pl.ds(0, quarter)], w.at[pl.ds(0, quarter)], sem.at[i]).wait()


def call(kernel, name, operands, out_shape, scratch, flops, sems, aliases=None):
    return pl.pallas_call(
        kernel,
        in_specs=[SMEM] + [ANY] * (len(operands) - 1),
        out_specs=[ANY] * len(out_shape),
        out_shape=out_shape,
        scratch_shapes=scratch + [pltpu.SemaphoreType.DMA((n,)) for n in sems],
        input_output_aliases=aliases or {},
        compiler_params=pltpu.CompilerParams(vmem_limit_bytes=LIMIT),
        cost_estimate=pl.CostEstimate(flops=flops, bytes_accessed=30 * 2**20, transcendentals=0),
        name=name,
    )(*operands)


def shape(*dims, dtype=F32):
    return jax.ShapeDtypeStruct(dims, dtype)


def attn_forward_kernel(idx, x_ref, vec_ref, *refs):
    given, refs = refs[:-20], refs[-20:]
    y1_ref, r1_ref, qkv_ref, p_ref, att_ref = refs[:5]
    x, vec, w, qkv, p, att, y1, r1, sem_x, sem_vec, sem_w, sem_y, sem_r, sem_q, sem_p = refs[5:]
    loads = load_halves(x_ref, x, sem_x, 0)
    load_vec = copy(vec_ref, vec, sem_vec.at[0])
    load_vec.start()
    fetch_attn(idx, given, w, sem_w)
    load_vec.wait()
    halves = halves_of(x)
    length = halves[0].stop
    for n, rows in enumerate(halves):
        loads[n].wait()
        xr = x[rows].astype(BF16)
        for i in range(3):
            if n == 0:
                wait_square(w, sem_w, i)
            joined = mm(xr, w[i])
            if i != 1:
                joined = joined + vec[i // 2 : i // 2 + 1]
            qkv[i, rows] = joined.astype(BF16)
    save_qkv = copy(qkv, qkv_ref, sem_q.at[0])
    save_qkv.start()
    pairs = x.shape[1] // (2 * HEAD_DIM)
    places = lax.broadcasted_iota(jnp.int32, (1, length), 1)
    even = even_lanes()

    def pair(step, carry):
        n, j = step // pairs, step % pairs
        rows = pl.ds(pl.multiple_of(n * length, length), length)
        lanes = pl.ds(pl.multiple_of(j * 2 * HEAD_DIM, 2 * HEAD_DIM), 2 * HEAD_DIM)
        hidden = jnp.where(places < idx[4 + n], 0.0, -1e30)
        q2 = qkv[0, rows, lanes] * jnp.asarray(HEAD_DIM**-0.5, BF16)
        k2 = qkv[1, rows, lanes]
        v2 = qkv[2, rows, lanes]
        parts = []
        for h in range(2):
            mine = even if h == 0 else jnp.logical_not(even)
            s = nt(jnp.where(mine, q2, jnp.zeros_like(q2)), k2) + hidden
            e = jnp.exp(s - jnp.max(s, axis=-1, keepdims=True))
            soft = (e * (1.0 / jnp.sum(e, axis=-1, keepdims=True))).astype(BF16)
            p[2 * step + h] = soft
            parts.append(mm(soft, v2))
        att[rows, lanes] = jnp.where(even, parts[0], parts[1]).astype(BF16)
        copy(p.at[pl.ds(2 * step, 2)], p_ref.at[pl.ds(2 * step, 2)], sem_p.at[0]).start()
        return carry

    lax.fori_loop(0, 2 * pairs, pair, 0)
    save_att = copy(att, att_ref, sem_q.at[1])
    save_att.start()
    wait_square(w, sem_w, 3)
    saves = [save_qkv, save_att]
    for n, rows in enumerate(halves):
        h = x[rows].astype(F32) + (mm(att[rows], w[3]) + vec[2:3])
        normed, inv = norm_rows(h)
        y1[rows] = normed * vec[3:4] + vec[4:5]
        r1[rows] = inv
        saves += [copy(y1.at[rows], y1_ref.at[rows], sem_y.at[n]), copy(r1.at[rows], r1_ref.at[rows], sem_r.at[n])]
        saves[-2].start()
        saves[-1].start()
    for save in saves:
        save.wait()
    copy(p, p_ref, sem_p.at[0]).wait()


def attn_forward(idx, x, vec, pieces):
    t, d = x.shape
    heads = d // HEAD_DIM
    length = t // 2
    return call(
        attn_forward_kernel,
        "attn_forward",
        (idx, x, vec) + tuple(pieces),
        [shape(t, d), shape(t, 1), shape(3, t, d, dtype=BF16), shape(2 * heads, length, length, dtype=BF16), shape(t, d, dtype=BF16)],
        [
            pltpu.VMEM((t, d), x.dtype),
            pltpu.VMEM(vec.shape, F32),
            pltpu.VMEM((4, d, d), BF16),
            pltpu.VMEM((3, t, d), BF16),
            pltpu.VMEM((2 * heads, length, length), BF16),
            pltpu.VMEM((t, d), BF16),
            pltpu.VMEM((t, d), F32),
            pltpu.VMEM((t, 1), F32),
        ],
        8 * t * d * d + 4 * t * length * d,
        (2, 1, 4, 2, 2, 2, 1),
    )


def ffn_forward_kernel(idx, y1_ref, vec_ref, *refs):
    given, refs = refs[:-22], refs[-22:]
    x_ref, r2_ref, ur_ref, gp_ref = refs[:4]
    y1, vec, we, wc, ur, gp, acc, x, r2, sem_y, sem_vec, sem_e, sem_c, sem_x, sem_r, sem_u, sem_g, sem_z = refs[4:]
    del sem_z
    loads = load_halves(y1_ref, y1, sem_y, 0)
    load_vec = copy(vec_ref, vec, sem_vec.at[0])
    load_vec.start()
    fetch_ffn(idx, given, 0, we, sem_e)
    fetch_ffn(idx, given, 1, wc, sem_c)
    load_vec.wait()
    d = y1.shape[1]
    halves = halves_of(y1)
    for j in range(4):
        cols = slice(j * d, (j + 1) * d)
        wait_square(we, sem_e, j)
        for n, rows in enumerate(halves):
            if j == 0:
                loads[n].wait()
            f = mm(y1[rows].astype(BF16), we[j]) + vec[5 + j : 6 + j]
            u, slope = gelu_pair(f)
            u = u.astype(BF16)
            ur[j, rows] = u
            gp[j, rows] = slope.astype(BF16)
            if j == 0 and n == 0:
                wait_rows(wc, sem_c)
            part = mm(u, wc[cols])
            if j == 0:
                acc[rows] = part
            else:
                acc[rows] += part
        copy(ur.at[j], ur_ref.at[j], sem_u.at[0]).start()
        copy(gp.at[j], gp_ref.at[j], sem_g.at[0]).start()
    saves = []
    for n, rows in enumerate(halves):
        normed, inv = norm_rows(y1[rows] + (acc[rows] + vec[9:10]))
        x[rows] = normed * vec[10:11] + vec[11:12]
        r2[rows] = inv
        saves += [copy(x.at[rows], x_ref.at[rows], sem_x.at[n]), copy(r2.at[rows], r2_ref.at[rows], sem_r.at[n])]
        saves[-2].start()
        saves[-1].start()
    for save in saves:
        save.wait()
    copy(ur, ur_ref, sem_u.at[0]).wait()
    copy(gp, gp_ref, sem_g.at[0]).wait()


def ffn_forward(idx, y1, vec, pieces):
    t, d = y1.shape
    return call(
        ffn_forward_kernel,
        "ffn_forward",
        (idx, y1, vec) + tuple(pieces),
        [shape(t, d), shape(t, 1), shape(4, t, d, dtype=BF16), shape(4, t, d, dtype=BF16)],
        [
            pltpu.VMEM((t, d), F32),
            pltpu.VMEM(vec.shape, F32),
            pltpu.VMEM((4, d, d), BF16),
            pltpu.VMEM((4 * d, d), BF16),
            pltpu.VMEM((4, t, d), BF16),
            pltpu.VMEM((4, t, d), BF16),
            pltpu.VMEM((t, d), F32),
            pltpu.VMEM((t, d), F32),
            pltpu.VMEM((t, 1), F32),
        ],
        16 * t * d * d,
        (2, 1, 4, 4, 2, 2, 1, 1, 1),
    )


def send_rows(idx, block, chip, core, s, m, sums, sem):
    if len(sums) == 1:
        copy(block, sums[0].at[2 * chip + core, s, m], sem).start()
        return
    keep, give = sums
    to = jnp.where(s == 1, relative_of(idx, chip, True), relative_of(idx, chip, False))

    @pl.when(core == idx[3])
    def _():
        copy(block, keep.at[s, to, m], sem).start()

    @pl.when(core != idx[3])
    def _():
        copy(block, give.at[s, to, m], sem).start()


def send_square(idx, stage, core, s, m, sums, sem):
    def go(chip, carry):
        send_rows(idx, stage.at[rows_of(chip)], chip, core, s, m, sums, sem)
        return carry

    lax.fori_loop(0, 16, go, 0)


def sums_shapes(d, whole, m=1):
    if whole:
        return [shape(32, 2, m, SHARE, d, dtype=BF16)]
    return [shape(2, 16, m, SHARE, d, dtype=BF16)] * 2


def ffn_backward_kernel(count, idx, g_ref, x_ref, r2_ref, y1_ref, r1_ref, vec_ref, ur_ref, gp_ref, *refs):
    given, refs = refs[: -(30 + count)], refs[-(30 + count) :]
    attn, given = (given[:1], given[:1]) if len(given) < 16 else (given[8:16], given[:8])
    dh1_ref, small_ref, da_ref = refs[:3]
    sums, refs = refs[3 : 3 + count], refs[3 + count :]
    g, x, r2, y1, r1, vec, we, wc, w, ur, gp, acc, e2, y1r, stage, da, small = refs[:17]
    sem_g, sem_x, sem_y, sem_r, sem_e, sem_c, sem_w, sem_u, sem_d, sem_a = refs[17:]
    d = y1.shape[1]
    halves = halves_of(y1)
    load_vec = copy(vec_ref, vec, sem_r.at[4])
    load_vec.start()
    loads = list(zip(load_halves(g_ref, g, sem_g, 0), load_halves(x_ref, x, sem_x, 0), load_halves(r2_ref, r2, sem_r, 0)))
    load_u = [copy(ur_ref.at[j], ur.at[j], sem_u.at[j]) for j in range(4)]
    load_g = [copy(gp_ref.at[j], gp.at[j], sem_u.at[4 + j]) for j in range(4)]
    load_u[0].start()
    fetch_ffn(idx, given, 1, wc, sem_c)
    load_g[0].start()
    load_y = load_halves(y1_ref, y1, sem_y, 0)
    load_r = load_halves(r1_ref, r1, sem_r, 2)
    fetch_ffn(idx, given, 0, we, sem_e)
    for j in range(1, 4):
        load_u[j].start()
        load_g[j].start()
    fetch_attn(idx, attn, w, sem_w, (-1, 1))
    small[...] = jnp.zeros_like(small)
    load_vec.wait()
    inv_gain = 1.0 / vec[10:11]
    for n, rows in enumerate(halves):
        for load in loads[n]:
            load.wait()
        grad = g[rows].astype(F32)
        normed = (x[rows] - vec[11:12]) * inv_gain
        add_small(small, 8, grad * normed)
        add_small(small, 9, grad)
        back = norm_rows_back(grad, normed, r2[rows], vec[10:11])
        low = back.astype(BF16)
        add_small(small, 7, low)
        acc[rows] = back
        e2[rows] = low
    for j in range(4):
        cols = slice(j * d, (j + 1) * d)
        load_u[j].wait()
        stage[4 + j] = tn(ur[j], e2[...]).astype(BF16)

        def go(b, carry):
            send_rows(idx, stage.at[4 + j, rows_of(b)], 4 * j + b // 4, b // 2 % 2, b % 2, 1, sums, sem_a.at[0])
            return carry

        lax.fori_loop(0, 16, go, 0)
        if j == 0:
            wait_rows(wc, sem_c)
            for n, rows in enumerate(halves):
                load_y[n].wait()
                y1r[rows] = y1[rows].astype(BF16)
        load_g[j].wait()
        for rows in halves:
            ef = (nt(e2[rows], wc[cols]) * gp[j, rows].astype(F32)).astype(BF16)
            gp[j, rows] = ef
            add_small(small, 3 + j, ef)
        stage[j] = tn(y1r[...], gp[j]).astype(BF16)
        send_square(idx, stage.at[j], j // 2, j % 2, 0, sums, sem_a.at[1])
        wait_square(we, sem_e, j)
        for rows in halves:
            acc[rows] += nt(gp[j, rows], we[j])
    wait_square(w, sem_w, 3)
    inv_gain = 1.0 / vec[3:4]
    saves = []
    for n, rows in enumerate(halves):
        load_r[n].wait()
        grad, normed = acc[rows], (y1[rows] - vec[4:5]) * inv_gain
        add_small(small, 1, grad * normed)
        add_small(small, 2, grad)
        back = norm_rows_back(grad, normed, r1[rows], vec[3:4])
        x[rows] = back
        low = back.astype(BF16)
        add_small(small, 0, low)
        da[rows] = nt(low, w[3]).astype(BF16)
        saves += [copy(x.at[rows], dh1_ref.at[rows], sem_d.at[n]), copy(da.at[rows], da_ref.at[rows], sem_d.at[2 + n])]
        saves[-2].start()
        saves[-1].start()
    saves.append(copy(small, small_ref, sem_d.at[4]))
    saves[-1].start()
    for save in saves:
        save.wait()
    copy(stage.at[4:8], stage.at[4:8], sem_a.at[0]).wait()
    copy(stage.at[0:4], stage.at[0:4], sem_a.at[1]).wait()


def ffn_backward(whole, idx, g, x, r2, y1, r1, vec, ur, gp, ffn_pieces, attn_pieces):
    t, d = x.shape
    sums = sums_shapes(d, whole, 2)
    pieces = tuple(ffn_pieces) + tuple(attn_pieces) if len(ffn_pieces) == 8 else tuple(ffn_pieces)
    return call(
        partial(ffn_backward_kernel, len(sums)),
        "ffn_backward",
        (idx, g, x, r2, y1, r1, vec, ur, gp) + pieces,
        [shape(t, d), shape(16, d), shape(t, d, dtype=BF16)] + sums,
        [
            pltpu.VMEM((t, d), g.dtype),
            pltpu.VMEM((t, d), F32),
            pltpu.VMEM((t, 1), F32),
            pltpu.VMEM((t, d), F32),
            pltpu.VMEM((t, 1), F32),
            pltpu.VMEM(vec.shape, F32),
            pltpu.VMEM((4, d, d), BF16),
            pltpu.VMEM((4 * d, d), BF16),
            pltpu.VMEM((4, d, d), BF16),
            pltpu.VMEM((4, t, d), BF16),
            pltpu.VMEM((4, t, d), BF16),
            pltpu.VMEM((t, d), F32),
            pltpu.VMEM((t, d), BF16),
            pltpu.VMEM((t, d), BF16),
            pltpu.VMEM((8, d, d), BF16),
            pltpu.VMEM((t, d), BF16),
            pltpu.VMEM((16, d), F32),
        ],
        32 * t * d * d,
        (2, 2, 2, 5, 4, 4, 4, 8, 5, 2),
    )


def ffn_both_kernel(idx, y1_ref, r1_ref, g_ref, vec_ref, *refs):
    given, refs = refs[:-32], refs[-32:]
    attn, given = (given[:1], given[:1]) if len(given) < 16 else (given[8:16], given[:8])
    x_ref, dh1_ref, small_ref, da_ref, sums = refs[:5]
    y1, r1, g, vec, we, wc, w, ur, gp, acc, x, n2, e2, y1r, stage, da, small = refs[5:22]
    sem_y, sem_r, sem_g, sem_vec, sem_e, sem_c, sem_w, sem_x, sem_d, sem_a = refs[22:]
    d = y1.shape[1]
    halves = halves_of(y1)
    load_y = load_halves(y1_ref, y1, sem_y, 0)
    load_vec = copy(vec_ref, vec, sem_vec.at[0])
    load_vec.start()
    fetch_ffn(idx, given, 0, we, sem_e)
    fetch_ffn(idx, given, 1, wc, sem_c)
    load_g = load_halves(g_ref, g, sem_g, 0)
    load_r = load_halves(r1_ref, r1, sem_r, 0)
    fetch_attn(idx, attn, w, sem_w, (-1, 1))
    small[...] = jnp.zeros_like(small)
    load_vec.wait()
    for n, rows in enumerate(halves):
        load_y[n].wait()
        y1r[rows] = y1[rows].astype(BF16)
    for j in range(4):
        cols = slice(j * d, (j + 1) * d)
        wait_square(we, sem_e, j)
        for n, rows in enumerate(halves):
            u, slope = gelu_pair(mm(y1r[rows], we[j]) + vec[5 + j : 6 + j])
            u = u.astype(BF16)
            ur[j, rows] = u
            gp[j, rows] = slope.astype(BF16)
            if j == 0 and n == 0:
                wait_rows(wc, sem_c)
            part = mm(u, wc[cols])
            if j == 0:
                acc[rows] = part
            else:
                acc[rows] += part
    saves = []
    for n, rows in enumerate(halves):
        normed, inv = norm_rows(y1[rows] + (acc[rows] + vec[9:10]))
        x[rows] = normed * vec[10:11] + vec[11:12]
        saves.append(copy(x.at[rows], x_ref.at[rows], sem_x.at[n]))
        saves[-1].start()
        load_g[n].wait()
        grad = g[rows].astype(F32)
        add_small(small, 8, grad * normed)
        add_small(small, 9, grad)
        back = norm_rows_back(grad, normed, inv, vec[10:11])
        low = back.astype(BF16)
        add_small(small, 7, low)
        acc[rows] = back
        e2[rows] = low
    for j in range(4):
        cols = slice(j * d, (j + 1) * d)
        stage[4 + j] = tn(ur[j], e2[...]).astype(BF16)

        def go(b, carry):
            send_rows(idx, stage.at[4 + j, rows_of(b)], 4 * j + b // 4, b // 2 % 2, b % 2, 1, (sums,), sem_a.at[0])
            return carry

        lax.fori_loop(0, 16, go, 0)
        for rows in halves:
            ef = (nt(e2[rows], wc[cols]) * gp[j, rows].astype(F32)).astype(BF16)
            gp[j, rows] = ef
            add_small(small, 3 + j, ef)
        stage[j] = tn(y1r[...], gp[j]).astype(BF16)
        send_square(idx, stage.at[j], j // 2, j % 2, 0, (sums,), sem_a.at[1])
        for rows in halves:
            acc[rows] += nt(gp[j, rows], we[j])
    wait_square(w, sem_w, 3)
    inv_gain = 1.0 / vec[3:4]
    for n, rows in enumerate(halves):
        load_r[n].wait()
        grad, normed = acc[rows], (y1[rows] - vec[4:5]) * inv_gain
        add_small(small, 1, grad * normed)
        add_small(small, 2, grad)
        back = norm_rows_back(grad, normed, r1[rows], vec[3:4])
        n2[rows] = back
        low = back.astype(BF16)
        add_small(small, 0, low)
        da[rows] = nt(low, w[3]).astype(BF16)
        saves += [copy(n2.at[rows], dh1_ref.at[rows], sem_d.at[n]), copy(da.at[rows], da_ref.at[rows], sem_d.at[2 + n])]
        saves[-2].start()
        saves[-1].start()
    saves.append(copy(small, small_ref, sem_d.at[4]))
    saves[-1].start()
    for save in saves:
        save.wait()
    copy(stage.at[4:8], stage.at[4:8], sem_a.at[0]).wait()
    copy(stage.at[0:4], stage.at[0:4], sem_a.at[1]).wait()


def ffn_both(idx, y1, r1, g, vec, ffn_pieces, attn_pieces):
    t, d = y1.shape
    pieces = tuple(ffn_pieces) + tuple(attn_pieces) if len(ffn_pieces) == 8 else tuple(ffn_pieces)
    return call(
        ffn_both_kernel,
        "ffn_both",
        (idx, y1, r1, g, vec) + pieces,
        [shape(t, d), shape(t, d), shape(16, d), shape(t, d, dtype=BF16)] + sums_shapes(d, True, 2),
        [
            pltpu.VMEM((t, d), F32),
            pltpu.VMEM((t, 1), F32),
            pltpu.VMEM((t, d), g.dtype),
            pltpu.VMEM(vec.shape, F32),
            pltpu.VMEM((4, d, d), BF16),
            pltpu.VMEM((4 * d, d), BF16),
            pltpu.VMEM((4, d, d), BF16),
            pltpu.VMEM((4, t, d), BF16),
            pltpu.VMEM((4, t, d), BF16),
            pltpu.VMEM((t, d), F32),
            pltpu.VMEM((t, d), F32),
            pltpu.VMEM((t, d), F32),
            pltpu.VMEM((t, d), BF16),
            pltpu.VMEM((t, d), BF16),
            pltpu.VMEM((8, d, d), BF16),
            pltpu.VMEM((t, d), BF16),
            pltpu.VMEM((16, d), F32),
        ],
        48 * t * d * d,
        (2, 2, 2, 1, 4, 4, 4, 2, 5, 2),
    )


def heads_backward_kernel(idx, da_ref, qkv_ref, p_ref, back_ref, small_ref, da, qkv, back, small, p, sem_in, sem_p, sem_out):
    t, d = da.shape
    length = t // 2
    pairs = d // (2 * HEAD_DIM)
    factor = HEAD_DIM**-0.5
    even = even_lanes()

    def load(step, slot):
        return copy(p_ref.at[pl.ds(2 * step, 2)], p.at[slot], sem_p.at[slot])

    load(0, 0).start()
    loads = load_halves(da_ref, da, sem_in, 0)
    for n, rows in enumerate(halves_of(da)):
        loads.append(copy(qkv_ref.at[:, rows], qkv.at[:, rows], sem_in.at[2 + n]))
        loads[-1].start()
    for n, rows in enumerate(halves_of(da)):
        loads[n].wait()
        loads[2 + n].wait()

        def pair(j, carry, n=n):
            step = n * pairs + j
            slot = step % 2

            @pl.when(step + 1 < 2 * pairs)
            def _():
                load(step + 1, 1 - slot).start()

            load(step, slot).wait()
            lanes = pl.ds(pl.multiple_of(j * 2 * HEAD_DIM, 2 * HEAD_DIM), 2 * HEAD_DIM)
            q2, k2, v2 = (qkv[i, n * length : (n + 1) * length, lanes] for i in range(3))
            da2 = da[n * length : (n + 1) * length, lanes]
            dqs, dks, dvs = [], [], []
            for h in range(2):
                mine = even if h == 0 else jnp.logical_not(even)
                soft = p[slot, h]
                dp = nt(jnp.where(mine, da2, jnp.zeros_like(da2)), v2)
                dvs.append(tn(soft, da2))
                soft = soft.astype(F32)
                inner = jnp.sum(soft * dp, axis=-1, keepdims=True)
                ds = (soft * (dp - inner)).astype(BF16)
                dqs.append(mm(ds, k2))
                dks.append(tn(ds, q2))
            dq, dk, dv = (jnp.where(even, m[0], m[1]) for m in (dqs, dks, dvs))
            back[0, n * length : (n + 1) * length, lanes] = (dq * factor).astype(BF16)
            back[1, n * length : (n + 1) * length, lanes] = (dk * factor).astype(BF16)
            back[2, n * length : (n + 1) * length, lanes] = dv.astype(BF16)
            return carry

        lax.fori_loop(0, pairs, pair, 0)
        copy(back.at[:, rows], back_ref.at[:, rows], sem_out.at[n]).start()
    small[0:1] = jnp.sum(back[0].astype(F32), axis=0, keepdims=True)
    small[1:2] = jnp.sum(back[2].astype(F32), axis=0, keepdims=True)
    save = copy(small, small_ref, sem_out.at[2])
    save.start()
    for n, rows in enumerate(halves_of(da)):
        copy(back.at[:, rows], back_ref.at[:, rows], sem_out.at[n]).wait()
    save.wait()


def heads_backward(idx, da, qkv, p):
    t, d = da.shape
    length = t // 2
    return call(
        heads_backward_kernel,
        "heads_backward",
        (idx, da, qkv, p),
        [shape(3, t, d, dtype=BF16), shape(8, d)],
        [
            pltpu.VMEM((t, d), BF16),
            pltpu.VMEM((3, t, d), BF16),
            pltpu.VMEM((3, t, d), BF16),
            pltpu.VMEM((8, d), F32),
            pltpu.VMEM((2, 2, length, length), BF16),
        ],
        30 * t * length * d,
        (4, 2, 3),
    )


def inward_backward_kernel(count, idx, dh1_ref, x_ref, att_ref, back_ref, *refs):
    given, refs = refs[: -(16 + count)], refs[-(16 + count) :]
    dx_ref = refs[0]
    sums, refs = refs[1 : 1 + count], refs[1 + count :]
    dh1, x, att, back, w, stage, dx, sem_d, sem_x, sem_a, sem_b, sem_w, sem_out, sem_s, _ = refs[:15]
    halves = halves_of(x)
    load_x = load_halves(x_ref, x, sem_x, 0)
    load_b = [copy(back_ref.at[i], back.at[i], sem_b.at[i]) for i in range(3)]
    for load in load_b:
        load.start()
    fetch_attn(idx, given, w, sem_w, (None, 0))
    load_d = load_halves(dh1_ref, dh1, sem_d, 0)
    load_a = copy(att_ref, att, sem_a.at[0])
    load_a.start()
    for load in load_x:
        load.wait()
    xr = x[...].astype(BF16)
    for i, (core, s) in enumerate(((0, 0), (1, 0), (0, 1))):
        load_b[i].wait()
        stage[i] = tn(xr, back[i]).astype(BF16)
        send_square(idx, stage.at[i], core, s, 0, sums, sem_s.at[0])
    for load in load_d:
        load.wait()
    load_a.wait()
    stage[3] = tn(att[...], dh1[...].astype(BF16)).astype(BF16)
    send_square(idx, stage.at[3], 1, 1, 0, sums, sem_s.at[0])
    for i in range(3):
        wait_square(w, sem_w, i)
    saves = []
    for n, rows in enumerate(halves):
        dx[rows] = dh1[rows] + (nt(back[0, rows], w[0]) + nt(back[1, rows], w[1]) + nt(back[2, rows], w[2]))
        saves.append(copy(dx.at[rows], dx_ref.at[rows], sem_out.at[n]))
        saves[-1].start()
    for save in saves:
        save.wait()
    copy(stage, stage, sem_s.at[0]).wait()


def inward_backward(whole, idx, dh1, x, att, back, pieces):
    t, d = dh1.shape
    sums = sums_shapes(d, whole)
    return call(
        partial(inward_backward_kernel, len(sums)),
        "inward_backward",
        (idx, dh1, x, att, back) + tuple(pieces),
        [shape(t, d)] + sums,
        [
            pltpu.VMEM((t, d), F32),
            pltpu.VMEM((t, d), x.dtype),
            pltpu.VMEM((t, d), BF16),
            pltpu.VMEM((3, t, d), BF16),
            pltpu.VMEM((4, d, d), BF16),
            pltpu.VMEM((4, d, d), BF16),
            pltpu.VMEM((t, d), F32),
        ],
        14 * t * d * d,
        (2, 2, 1, 3, 4, 2, 1, 1),
    )


BITS = {"c": 1, "y": 2, "x": 4, "z1": 8, "z2": 16, "z3": 24}


def swap(array, by):
    return lax.ppermute(array, AXES, [(i, i ^ BITS[by]) for i in range(32)])


def tie(values, *others):
    return lax.optimization_barrier((values, others))[0]


def pair_up(share):
    return jnp.stack([share, swap(share, "z3")])


def column_up(pair):
    return jnp.concatenate([pair, swap(pair, "z1")])


def near_up(cols):
    return tuple(jnp.concatenate([col, swap(col, by)]) for col, by in zip(cols, "xy"))


def far_up(near):
    return tuple(swap(piece, by) for piece, by in zip(near, "yx"))


def other_core(pieces):
    return tuple(swap(piece, "c") for piece in pieces)


def in_order(near, far, near_c, far_c):
    return sum(((near[s], far[s], near_c[s], far_c[s]) for s in range(2)), ())


def place_small(qb, vb, ob, ag, ash, eb, cb, fg, fs, width, device):
    layers, rows = qb.shape
    lanes = lax.broadcasted_iota(jnp.int32, (1, 1, width), 2)
    thin = jnp.stack([qb, vb, ob, ag, ash, cb, fg, fs], axis=1).astype(F32)
    thin = jnp.where(lanes // rows == device, jnp.tile(thin, (1, 1, width // rows)), 0.0)
    lines = lax.broadcasted_iota(jnp.int32, (1, 4, width), 1)
    wide = jnp.tile(eb.astype(F32)[:, None], (1, 4, width // eb.shape[1]))
    wide = jnp.where(lines * (width // eb.shape[1]) + lanes // eb.shape[1] == device, wide, 0.0)
    return jnp.concatenate([thin[:, 0:5], wide, thin[:, 5:8], jnp.zeros((layers, 4, width), F32)], axis=1)


def own_small(total, rows, device):
    layers, _, width = total.shape
    thin = lax.dynamic_slice_in_dim(total, device * rows, rows, 2)
    count = width // (4 * rows)
    wide = lax.dynamic_slice(total, (0, 5 + device // count, device % count * 4 * rows), (layers, 1, 4 * rows))
    return [thin[:, i] for i in range(5)] + [wide[:, 0]] + [thin[:, i] for i in range(9, 12)]


def add_swap(array, by):
    return array + swap(array, by)


class Sums:
    def __init__(self, keep, give):
        self.both = [keep]
        self.parts = [[], []]
        self.give = give

    def total(self, s, lo, hi):
        whole = None
        for a in [b[s] for b in self.both] + self.parts[s]:
            a = a[lo:hi].astype(F32)
            whole = a if whole is None else whole + a
        return whole

    def latest(self):
        return self.parts if self.parts[0] else self.both

    def hold(self, *others):
        if self.parts[0]:
            self.parts = tie(self.parts, *others)
        else:
            self.both = tie(self.both, *others)

    def core(self):
        self.both = self.both + [swap(self.give, "c")]

    def plane(self, lo, bys):
        arrived = [swap(self.total(s, lo, 2 * lo).astype(BF16), bys[s]) for s in range(2)]
        for s in range(2):
            self.parts[s] = self.parts[s] + [arrived[s]]

    def first(self):
        self.plane(8, "yx")

    def second(self):
        self.plane(4, "xy")

    def line(self, lo, by):
        arrived = swap(jnp.stack([self.total(s, lo, 2 * lo) for s in range(2)]).astype(BF16), by)
        for s in range(2):
            self.parts[s] = self.parts[s] + [arrived[s]]

    def third(self):
        self.line(2, "z1")

    def fourth(self):
        self.line(1, "z3")

    def result(self):
        return jnp.stack([self.total(s, 0, 1)[0] for s in range(2)])


def front(first, last, rows, width, c, attention):
    layers = first.shape[0]
    first = first.reshape(layers, rows, -1)
    cut = lambda i: first[:, :, i * width : (i + 1) * width]
    if attention:
        zero, one = (cut(0), cut(2)), (cut(1), last.reshape(layers, rows, width))
    else:
        zero, one = (cut(0), cut(1)), (cut(2), cut(3))
    zero, one = jnp.stack(zero, 1), jnp.stack(one, 1)
    return jnp.where(c == 0, zero, one), jnp.where(c == 0, one, zero)


def both_cores(mine, got, c):
    return jnp.where(c == 0, jnp.concatenate([mine, got], 2), jnp.concatenate([got, mine], 2))


def gather_any(w_inward, w_outward, w_expand, w_contract, width):
    whole = lambda m, n: lax.all_gather(m, AXES, axis=0, tiled=True).reshape(-1, n)
    inward, outward = whole(w_inward, 3 * width), whole(w_outward, width)
    expand, contract = whole(w_expand, 4 * width), whole(w_contract, width)
    cut = lambda m, i: m[:, i * width : (i + 1) * width].reshape(16, SHARE, width)
    squares = [cut(inward, i) for i in range(3)] + [cut(outward, 0)] + [cut(expand, i) for i in range(4)]
    down = contract.reshape(16, 2, 2, SHARE, width)
    sides = []
    for core in range(2):
        pick = (core, 2 + core, 4 + 2 * core, 5 + 2 * core)
        pairs = [squares[i] for i in pick] + [down[:, core, s] for s in range(2)]
        sides.append(jnp.stack(pairs, 1).reshape(16, 3, 2, SHARE, width))
    return jnp.stack(sides, 1).reshape(32, 3, 2, SHARE, width)


def collect_any(attn, ffn, width):
    attn = attn.reshape(16, 2, 2, SHARE, width)
    ffn = ffn.reshape(16, 2, 2, 2, SHARE, width)
    expand, contract = ffn[:, :, :, 0], ffn[:, :, :, 1]
    inward = jnp.concatenate([attn[:, 0, 0], attn[:, 1, 0], attn[:, 0, 1]], axis=-1)
    expand = jnp.concatenate([expand[:, core, s] for core in range(2) for s in range(2)], axis=-1)
    return tuple(
        lax.psum_scatter(m.reshape(-1).astype(F32), AXES, scatter_dimension=0, tiled=True)
        for m in (inward, attn[:, 1, 1], expand, contract)
    )


def local(blocked, tokens, lengths, w_inward, qb, vb, w_outward, ob, ag, ash, w_expand, eb, w_contract, cb, fg, fs, cotangent):
    layers = w_inward.shape[0]
    width = tokens.shape[-1]
    rows = qb.shape[1]
    device = lax.axis_index("wide") * lax.axis_size("narrow") + lax.axis_index("narrow")
    me = device if blocked else jnp.int32(0)
    c = me & 1
    place = jnp.stack([me >> 3, (me >> 2) & 1, (me >> 1) & 1, c]).astype(jnp.int32)
    idx = jnp.concatenate([place, lengths.reshape(-1), jnp.zeros((2,), jnp.int32)])
    small = place_small(qb, vb, ob, ag, ash, eb, cb, fg, fs, width, device)
    x = tokens.reshape(-1, width)
    kept = []

    def keep_layer(x, y1, attn, ffn, attn_pieces, ffn_pieces):
        kept.append((x, y1) + tuple(attn[1:]) + tuple(ffn) + (attn_pieces, ffn_pieces))
        return ffn[0]

    if blocked:
        mine, got = front(w_inward, w_outward, rows, width, c, True)
        halves = lambda col: (col[:, 0, None], col[:, 1, None])
        halves2 = lambda col: (col[:, :, 0], col[:, :, 1])
        share_a = both_cores(mine, swap(got, "c"), c)
        small = add_swap(small, "c")
        mine, got = front(w_expand, None, rows, width, c, False)
        share_e = both_cores(mine, swap(got, "c"), c)
        contract = w_contract.reshape(layers, 2, SHARE, width)
        share_f = [jnp.stack([share_e[l], contract[l]]) for l in range(layers)]
        a_pair = pair_up(share_a[0])
        share, a_pair, small = tie((share_f[0], a_pair, small))
        f_pair = pair_up(share)
        a_col = column_up(a_pair)
        small = add_swap(small, "z1")
        f_pair, a_col, small = tie((f_pair, a_col, small))
        f_col = column_up(f_pair)
        a_near = near_up(halves(a_col))
        small = add_swap(small, "z2")
        a_near, small = tie((a_near, small))
        a_far = far_up(a_near)
        a_core = other_core(a_near)
        f_col, a_far, small = tie((f_col, a_far, small))
        f_near = near_up(halves2(f_col))
        small = add_swap(small, "x")
        a1_pair = pair_up(tie((share_a[1], a_far))[0])
        a_core += other_core(a_far)
        x, f_near, a1_pair, small = tie((x, f_near, a1_pair, small))
        f_far = far_up(f_near)
        small = add_swap(small, "y")
        a1_col = column_up(a1_pair)
        f_core = other_core(f_near)
        vecs = [small[l] for l in range(layers)]
        a_pieces = in_order(a_near, a_far, a_core[:2], a_core[2:])
        attn = attn_forward(idx, x, vecs[0], a_pieces)
        f_far, a1_col, f_core, y1, share = tie((f_far, a1_col, f_core, attn[0], share_f[1]))
        f_core += other_core(f_far)
        a1_near = near_up(halves(a1_col))
        f1_pair = pair_up(share)
        y1, a1_near, f1_pair = tie((y1, a1_near, f1_pair))
        a1_far = far_up(a1_near)
        f1_col = column_up(f1_pair)
        f_pieces = in_order(f_near, f_far, f_core[:2], f_core[2:])
        ffn = ffn_forward(idx, y1, vecs[0], f_pieces)
        x1 = keep_layer(x, y1, attn, ffn, a_pieces, f_pieces)
        a1_far, f1_col, x1 = tie((a1_far, f1_col, x1))
        a1_core = other_core(a1_near + a1_far)
        f1_near = near_up(halves2(f1_col))
        x1, f1_near = tie((x1, f1_near))
        f1_far = far_up(f1_near)
        f1_core = other_core(f1_near)
        a1_pieces = in_order(a1_near, a1_far, a1_core[:2], a1_core[2:])
        attn = attn_forward(idx, x1, vecs[1], a1_pieces)
        f1_far, f1_core, y1 = tie((f1_far, f1_core, attn[0]))
        f1_core += other_core(f1_far)
        f1_pieces = in_order(f1_near, f1_far, f1_core[:2], f1_core[2:])
        output, dh1, small, da, whole = ffn_both(idx, y1, attn[1], cotangent.reshape(-1, width), vecs[1], f1_pieces, a1_pieces)
        keep_layer(x1, y1, attn, (output, None, None, None), a1_pieces, f1_pieces)
    else:
        small = lax.psum(small, AXES)
        vecs = [small[l] for l in range(layers)]
        for l in range(layers):
            pieces = (gather_any(w_inward[l], w_outward[l], w_expand[l], w_contract[l], width),)
            attn = attn_forward(idx, x, vecs[l], pieces)
            if l + 1 < layers:
                x = keep_layer(x, attn[0], attn, ffn_forward(idx, attn[0], vecs[l], pieces), pieces, pieces)
        output, dh1, small, da, whole = ffn_both(idx, attn[0], attn[1], cotangent.reshape(-1, width), vecs[l], pieces, pieces)
        keep_layer(x, attn[0], attn, (output, None, None, None), pieces, pieces)
    w_sums, smalls = [None] * layers, [None] * layers

    def ffn_back(l, g):
        x, y1, r1, qkv, p, att, out, r2, ur, gp, attn_pieces, ffn_pieces = kept[l]
        return ffn_backward(not blocked, idx, g, out, r2, y1, r1, vecs[l], ur, gp, ffn_pieces, attn_pieces)

    def heads_back(l, da):
        x, y1, r1, qkv, p, att, out, r2, ur, gp, attn_pieces, ffn_pieces = kept[l]
        return heads_backward(idx, da, qkv, p)

    def inward_back(l, dh1, back):
        x, y1, r1, qkv, p, att, out, r2, ur, gp, attn_pieces, ffn_pieces = kept[l]
        return inward_backward(not blocked, idx, dh1, x, att, back, attn_pieces)

    if blocked:
        f1 = lax.psum_scatter(whole, AXES, scatter_dimension=0, tiled=True)
        back, small_h = heads_back(1, da)
        smalls[1] = jnp.concatenate([small_h[0:2], small[0:10]])
        g, *sums = inward_back(1, dh1, back)
        a1 = Sums(*sums)
        a1.core()
        dh1, small, da, *sums = ffn_back(0, g)
        f0 = Sums(*sums)
        da, f0.give, a1.both = tie((da, f0.give, a1.both))
        f0.core()
        a1.first()
        back, small_h = heads_back(0, da)
        smalls[0] = jnp.concatenate([small_h[0:2], small[0:10]])
        back, a1.parts, f0.both = tie((back, a1.parts, f0.both))
        f0.first()
        a1.second()
        g, *sums = inward_back(0, dh1, back)
        a0 = Sums(*sums)
        a0.give, a1.parts, f0.parts = tie((a0.give, a1.parts, f0.parts))
        a0.core()
        f0.second()
        a1.third()
        a0.both, a1.parts = tie((a0.both, a1.parts))
        a0.first()
        a1.fourth()
        small, f0.parts = tie((jnp.stack(smalls), f0.parts))
        f0.third()
        small = add_swap(small, "z2")
        small, a0.parts, f1 = tie((small, a0.parts, f1))
        a0.second()
        small = add_swap(small, "x")
        small, a0.parts, f0.parts = tie((small, a0.parts, f0.parts))
        a0.third()
        f0.fourth()
        small = add_swap(small, "y")
        small, a0.parts, f0.parts = tie((small, a0.parts, f0.parts))
        a0.fourth()
        small = add_swap(small, "z1")
        small, a0.parts = tie((small, a0.parts))
        small = add_swap(small, "c")
        f1 = f1[0].astype(F32)
        f0 = f0.result()
        a0, a1 = (m.result()[:, 0] for m in (a0, a1))
        w_sums = [(a0, f0[:, 0], f0[:, 1]), (a1, f1[:, 0], f1[:, 1])]
    else:
        for l in reversed(range(layers)):
            if l + 1 < layers:
                dh1, small, da, whole = ffn_back(l, g)
            back, small_h = heads_back(l, da)
            g, sums_a = inward_back(l, dh1, back)
            smalls[l] = jnp.concatenate([small_h[0:2], small[0:10]])
            w_sums[l] = collect_any(sums_a, whole, width)
        small = lax.psum(jnp.stack(smalls), AXES)
    names = ("qb", "vb", "ob", "ag", "as", "eb", "cb", "fg", "fs")
    outs = dict(zip(names, own_small(small, rows, device)))
    flat = {"in": [], "out": [], "ex": [], "co": []}
    for l in range(layers):
        if not blocked:
            for name, share in zip(("in", "out", "ex", "co"), w_sums[l]):
                flat[name].append(share)
            continue
        attn, expand, contract = w_sums[l]
        squares = jnp.stack([attn[0], attn[1], expand[0], expand[1]])
        low, high = squares[:, :rows], squares[:, rows:]
        mine = jnp.where(c == 0, low, high)
        got = swap(jnp.where(c == 0, high, low), "c")
        zero, one = jnp.where(c == 0, mine, got), jnp.where(c == 0, got, mine)
        flat["in"].append(jnp.concatenate([zero[0], one[0], zero[1]], axis=1).reshape(-1))
        flat["out"].append(one[1].reshape(-1))
        flat["ex"].append(jnp.concatenate([zero[2], zero[3], one[2], one[3]], axis=1).reshape(-1))
        flat["co"].append(contract.reshape(-1))
    flat = {k: jnp.stack(v) for k, v in flat.items()}
    shape = tokens.shape
    return (
        output.reshape(shape), g.reshape(shape), flat["in"], outs["qb"], outs["vb"], flat["out"], outs["ob"],
        outs["ag"], outs["as"], flat["ex"], outs["eb"], flat["co"], outs["cb"], outs["fg"], outs["fs"],
    )


def solution(mesh):
    flat = P(None, AXES)
    deep = P(None, AXES, None, None)
    blocked = mesh.shape["wide"] == 8 and mesh.shape["narrow"] == 4
    return jax.shard_map(
        partial(local, blocked),
        mesh=mesh,
        in_specs=(deep,) + (flat,) * 14 + (deep,),
        out_specs=(deep, deep) + (flat,) * 13,
        check_vma=False,
    )
```

```python
import math
from functools import partial

import jax
import jax.numpy as jnp
from jax import lax
from jax.experimental import pallas as pl
from jax.experimental.pallas import tpu as pltpu
from jax.sharding import PartitionSpec as P

HEAD_DIM = 64
EPSILON = 1e-06
AXES = ("wide", "narrow")
F32 = jnp.float32
BF16 = jnp.bfloat16
ANY = pl.BlockSpec(memory_space=pl.ANY)
VMEM = pl.BlockSpec(memory_space=pltpu.VMEM)
SMEM = pl.BlockSpec(memory_space=pltpu.SMEM)
LIMIT = 60 * 2**20
SHARE = 48


def mm(left, right, over=(1, 0)):
    return lax.dot_general(
        left, right, (((over[0],), (over[1],)), ((), ())), preferred_element_type=F32
    )


def nt(left, right):
    return mm(left, right, (1, 1))


def tn(left, right):
    return mm(left, right, (0, 0))


def norm_rows(h):
    centred = h - jnp.mean(h, axis=-1, keepdims=True)
    inv = lax.rsqrt(jnp.mean(centred * centred, axis=-1, keepdims=True) + EPSILON)
    return centred * inv, inv


def norm_rows_back(g, n, inv, gain):
    t = g * gain
    return inv * (
        t
        - jnp.mean(t, axis=-1, keepdims=True)
        - n * jnp.mean(t * n, axis=-1, keepdims=True)
    )


def gelu_pair(f):
    u = jnp.abs(f)
    t = 1.0 / (1.0 + (0.3275911 / math.sqrt(2.0)) * u)
    e = jnp.exp(-0.5 * f * f)
    c = [0.5 * v for v in (0.254829592, -0.284496736, 1.421413741, -1.453152027, 1.061405429)]
    tail = e * (t * (c[0] + t * (c[1] + t * (c[2] + t * (c[3] + t * c[4])))))
    phi = jnp.where(f >= 0, 1.0 - tail, tail)
    return f * phi, phi + f * (e * (1.0 / math.sqrt(2.0 * math.pi)))


def even_lanes():
    return lax.broadcasted_iota(jnp.int32, (1, 2 * HEAD_DIM), 1) < HEAD_DIM


def place_of(idx, block, far, first_is_x):
    k, other = block % 4, block // 4
    z = idx[0] ^ (3 * (k % 2)) ^ (k // 2)
    if first_is_x:
        x, y = idx[1] ^ other, idx[2] ^ far
    else:
        x, y = idx[1] ^ far, idx[2] ^ other
    return z * 4 + x * 2 + y


def relative_of(idx, chip, first_is_x):
    r = (chip // 4) ^ idx[0]
    k = (r // 2) + 2 * ((r ^ (r // 2)) % 2)
    i = (chip // 2 % 2) ^ idx[1]
    j = (chip % 2) ^ idx[2]
    return (i * 8 + j * 4 + k) if first_is_x else (j * 8 + i * 4 + k)


def copy(src, dst, sem):
    return pltpu.make_async_copy(src, dst, sem)


def halves_of(ref):
    length = ref.shape[0] // 2
    return [slice(n * length, (n + 1) * length) for n in range(2)]


def add_small(ref, row, value):
    ref[row : row + 1] += jnp.sum(value.astype(F32), axis=0, keepdims=True)


def load_halves(src, dst, sems, at):
    loads = [copy(src.at[rows], dst.at[rows], sems.at[at + n]) for n, rows in enumerate(halves_of(src))]
    for load in loads:
        load.start()
    return loads


def rows_of(chip):
    return pl.ds(pl.multiple_of(chip * SHARE, SHARE), SHARE)


def fetch_attn(idx, given, w, sem, cores=(None, None)):
    if len(given) == 1:

        def whole(chip, carry):
            for s in range(2):
                for core in (0, 1) if cores[s] is None else (cores[s],):
                    square = 2 * s + core
                    copy(given[0].at[2 * chip + core, 0, s], w.at[square, rows_of(chip)], sem.at[square]).start()
            return carry

        lax.fori_loop(0, 16, whole, 0)
        return

    def go(block, carry):
        for s in range(2):
            if cores[s] == -1:
                continue
            for side in range(2):
                core = idx[3] ^ side

                def start(s=s, side=side, core=core):
                    for far in range(2):
                        rows = rows_of(place_of(idx, block, far, s == 0))
                        copy(given[4 * s + 2 * side + far].at[block, 0], w.at[2 * s + core, rows], sem.at[2 * s + core]).start()

                if cores[s] is None:
                    start()
                else:
                    pl.when(core == cores[s])(start)
        return carry

    lax.fori_loop(0, 8, go, 0)


def wait_square(w, sem, square):
    copy(w.at[square], w.at[square], sem.at[square]).wait()


def fetch_ffn(idx, given, m, w, sem):
    def place(chip, core, s):
        if m == 0:
            return w.at[2 * core + s, rows_of(chip)]
        return w.at[pl.ds(pl.multiple_of((chip * 4 + core * 2 + s) * SHARE, SHARE), SHARE)]

    def whole(chip, carry):
        for s in range(2):
            for core in range(2):
                copy(given[0].at[2 * chip + core, 1 + m, s], place(chip, core, s), sem.at[2 * core + s]).start()
        return carry

    def go(block, carry):
        for s in range(2):
            for side in range(2):
                core = idx[3] ^ side
                for far in range(2):
                    chip = place_of(idx, block, far, s == 0)
                    copy(given[4 * s + 2 * side + far].at[block, m], place(chip, core, s), sem.at[2 * core + s]).start()
        return carry

    if len(given) == 1:
        lax.fori_loop(0, 16, whole, 0)
    else:
        lax.fori_loop(0, 8, go, 0)


def wait_rows(w, sem):
    quarter = w.shape[0] // 4
    for i in range(4):
        copy(w.at[pl.ds(0, quarter)], w.at[pl.ds(0, quarter)], sem.at[i]).wait()


def call(kernel, name, operands, out_shape, scratch, flops, sems, aliases=None):
    return pl.pallas_call(
        kernel,
        in_specs=[SMEM] + [ANY] * (len(operands) - 1),
        out_specs=[ANY] * len(out_shape),
        out_shape=out_shape,
        scratch_shapes=scratch + [pltpu.SemaphoreType.DMA((n,)) for n in sems],
        input_output_aliases=aliases or {},
        compiler_params=pltpu.CompilerParams(vmem_limit_bytes=LIMIT),
        cost_estimate=pl.CostEstimate(flops=flops, bytes_accessed=30 * 2**20, transcendentals=0),
        name=name,
    )(*operands)


def shape(*dims, dtype=F32):
    return jax.ShapeDtypeStruct(dims, dtype)


def attn_forward_kernel(idx, x_ref, vec_ref, *refs):
    given, refs = refs[:-20], refs[-20:]
    y1_ref, r1_ref, qkv_ref, p_ref, att_ref = refs[:5]
    x, vec, w, qkv, p, att, y1, r1, sem_x, sem_vec, sem_w, sem_y, sem_r, sem_q, sem_p = refs[5:]
    loads = load_halves(x_ref, x, sem_x, 0)
    load_vec = copy(vec_ref, vec, sem_vec.at[0])
    load_vec.start()
    fetch_attn(idx, given, w, sem_w)
    load_vec.wait()
    halves = halves_of(x)
    length = halves[0].stop
    for n, rows in enumerate(halves):
        loads[n].wait()
        xr = x[rows].astype(BF16)
        for i in range(3):
            if n == 0:
                wait_square(w, sem_w, i)
            joined = mm(xr, w[i])
            if i != 1:
                joined = joined + vec[i // 2 : i // 2 + 1]
            qkv[i, rows] = joined.astype(BF16)
    save_qkv = copy(qkv, qkv_ref, sem_q.at[0])
    save_qkv.start()
    pairs = x.shape[1] // (2 * HEAD_DIM)
    places = lax.broadcasted_iota(jnp.int32, (length, 1), 0)
    even = even_lanes()

    def pair(step, carry):
        n, j = step // pairs, step % pairs
        rows = pl.ds(pl.multiple_of(n * length, length), length)
        lanes = pl.ds(pl.multiple_of(j * 2 * HEAD_DIM, 2 * HEAD_DIM), 2 * HEAD_DIM)
        hidden = jnp.where(places < idx[4 + n], 0.0, -1e30)
        q2 = qkv[0, rows, lanes] * jnp.asarray(HEAD_DIM**-0.5, BF16)
        k2 = qkv[1, rows, lanes]
        v2 = qkv[2, rows, lanes].T
        masks = (even, jnp.logical_not(even))
        scores = [nt(k2, jnp.where(mine, q2, jnp.zeros_like(q2))) + hidden for mine in masks]
        parts = []
        for h, s in enumerate(scores):
            e = jnp.exp(s - jnp.max(s, axis=0, keepdims=True))
            soft = (e * (1.0 / jnp.sum(e, axis=0, keepdims=True))).astype(BF16)
            p[2 * step + h] = soft
            parts.append(mm(v2[h * HEAD_DIM : (h + 1) * HEAD_DIM], soft))
        att[rows, lanes] = jnp.concatenate(parts, axis=0).T.astype(BF16)
        copy(p.at[pl.ds(2 * step, 2)], p_ref.at[pl.ds(2 * step, 2)], sem_p.at[0]).start()
        return carry

    lax.fori_loop(0, 2 * pairs, pair, 0, unroll=3)
    save_att = copy(att, att_ref, sem_q.at[1])
    save_att.start()
    wait_square(w, sem_w, 3)
    saves = [save_qkv, save_att]
    for n, rows in enumerate(halves):
        h = x[rows].astype(F32) + (mm(att[rows], w[3]) + vec[2:3])
        normed, inv = norm_rows(h)
        y1[rows] = normed * vec[3:4] + vec[4:5]
        r1[rows] = inv
        saves += [copy(y1.at[rows], y1_ref.at[rows], sem_y.at[n]), copy(r1.at[rows], r1_ref.at[rows], sem_r.at[n])]
        saves[-2].start()
        saves[-1].start()
    for save in saves:
        save.wait()
    copy(p, p_ref, sem_p.at[0]).wait()


def attn_forward(idx, x, vec, pieces):
    t, d = x.shape
    heads = d // HEAD_DIM
    length = t // 2
    return call(
        attn_forward_kernel,
        "attn_forward",
        (idx, x, vec) + tuple(pieces),
        [shape(t, d), shape(t, 1), shape(3, t, d, dtype=BF16), shape(2 * heads, length, length, dtype=BF16), shape(t, d, dtype=BF16)],
        [
            pltpu.VMEM((t, d), x.dtype),
            pltpu.VMEM(vec.shape, F32),
            pltpu.VMEM((4, d, d), BF16),
            pltpu.VMEM((3, t, d), BF16),
            pltpu.VMEM((2 * heads, length, length), BF16),
            pltpu.VMEM((t, d), BF16),
            pltpu.VMEM((t, d), F32),
            pltpu.VMEM((t, 1), F32),
        ],
        8 * t * d * d + 4 * t * length * d,
        (2, 1, 4, 2, 2, 2, 1),
    )


def ffn_forward_kernel(idx, y1_ref, vec_ref, *refs):
    given, refs = refs[:-22], refs[-22:]
    x_ref, r2_ref, ur_ref, gp_ref = refs[:4]
    y1, vec, we, wc, ur, gp, acc, x, r2, sem_y, sem_vec, sem_e, sem_c, sem_x, sem_r, sem_u, sem_g, sem_z = refs[4:]
    del sem_z
    loads = load_halves(y1_ref, y1, sem_y, 0)
    load_vec = copy(vec_ref, vec, sem_vec.at[0])
    load_vec.start()
    fetch_ffn(idx, given, 0, we, sem_e)
    fetch_ffn(idx, given, 1, wc, sem_c)
    load_vec.wait()
    d = y1.shape[1]
    halves = halves_of(y1)
    for j in range(4):
        cols = slice(j * d, (j + 1) * d)
        wait_square(we, sem_e, j)
        for n, rows in enumerate(halves):
            if j == 0:
                loads[n].wait()
            f = mm(y1[rows].astype(BF16), we[j]) + vec[5 + j : 6 + j]
            u, slope = gelu_pair(f)
            u = u.astype(BF16)
            ur[j, rows] = u
            gp[j, rows] = slope.astype(BF16)
            if j == 0 and n == 0:
                wait_rows(wc, sem_c)
            part = mm(u, wc[cols])
            if j == 0:
                acc[rows] = part
            else:
                acc[rows] += part
        copy(ur.at[j], ur_ref.at[j], sem_u.at[0]).start()
        copy(gp.at[j], gp_ref.at[j], sem_g.at[0]).start()
    saves = []
    for n, rows in enumerate(halves):
        normed, inv = norm_rows(y1[rows] + (acc[rows] + vec[9:10]))
        x[rows] = normed * vec[10:11] + vec[11:12]
        r2[rows] = inv
        saves += [copy(x.at[rows], x_ref.at[rows], sem_x.at[n]), copy(r2.at[rows], r2_ref.at[rows], sem_r.at[n])]
        saves[-2].start()
        saves[-1].start()
    for save in saves:
        save.wait()
    copy(ur, ur_ref, sem_u.at[0]).wait()
    copy(gp, gp_ref, sem_g.at[0]).wait()


def ffn_forward(idx, y1, vec, pieces):
    t, d = y1.shape
    return call(
        ffn_forward_kernel,
        "ffn_forward",
        (idx, y1, vec) + tuple(pieces),
        [shape(t, d), shape(t, 1), shape(4, t, d, dtype=BF16), shape(4, t, d, dtype=BF16)],
        [
            pltpu.VMEM((t, d), F32),
            pltpu.VMEM(vec.shape, F32),
            pltpu.VMEM((4, d, d), BF16),
            pltpu.VMEM((4 * d, d), BF16),
            pltpu.VMEM((4, t, d), BF16),
            pltpu.VMEM((4, t, d), BF16),
            pltpu.VMEM((t, d), F32),
            pltpu.VMEM((t, d), F32),
            pltpu.VMEM((t, 1), F32),
        ],
        16 * t * d * d,
        (2, 1, 4, 4, 2, 2, 1, 1, 1),
    )


def send_rows(idx, block, chip, core, s, m, sums, sem):
    if len(sums) == 1:
        copy(block, sums[0].at[2 * chip + core, s, m], sem).start()
        return
    keep, give = sums
    to = jnp.where(s == 1, relative_of(idx, chip, True), relative_of(idx, chip, False))

    @pl.when(core == idx[3])
    def _():
        copy(block, keep.at[s, to, m], sem).start()

    @pl.when(core != idx[3])
    def _():
        copy(block, give.at[s, to, m], sem).start()


def send_square(idx, stage, core, s, m, sums, sem):
    def go(chip, carry):
        send_rows(idx, stage.at[rows_of(chip)], chip, core, s, m, sums, sem)
        return carry

    lax.fori_loop(0, 16, go, 0)


def sums_shapes(d, whole, m=1):
    if whole:
        return [shape(32, 2, m, SHARE, d, dtype=BF16)]
    return [shape(2, 16, m, SHARE, d, dtype=BF16)] * 2


def ffn_backward_kernel(count, idx, g_ref, x_ref, r2_ref, y1_ref, r1_ref, vec_ref, ur_ref, gp_ref, *refs):
    given, refs = refs[: -(30 + count)], refs[-(30 + count) :]
    attn, given = (given[:1], given[:1]) if len(given) < 16 else (given[8:16], given[:8])
    dh1_ref, small_ref, da_ref = refs[:3]
    sums, refs = refs[3 : 3 + count], refs[3 + count :]
    g, x, r2, y1, r1, vec, we, wc, w, ur, gp, acc, e2, y1r, stage, da, small = refs[:17]
    sem_g, sem_x, sem_y, sem_r, sem_e, sem_c, sem_w, sem_u, sem_d, sem_a = refs[17:]
    d = y1.shape[1]
    halves = halves_of(y1)
    load_vec = copy(vec_ref, vec, sem_r.at[4])
    load_vec.start()
    loads = list(zip(load_halves(g_ref, g, sem_g, 0), load_halves(x_ref, x, sem_x, 0), load_halves(r2_ref, r2, sem_r, 0)))
    load_u = [copy(ur_ref.at[j], ur.at[j], sem_u.at[j]) for j in range(4)]
    load_g = [copy(gp_ref.at[j], gp.at[j], sem_u.at[4 + j]) for j in range(4)]
    load_u[0].start()
    fetch_ffn(idx, given, 1, wc, sem_c)
    load_g[0].start()
    load_y = load_halves(y1_ref, y1, sem_y, 0)
    load_r = load_halves(r1_ref, r1, sem_r, 2)
    fetch_ffn(idx, given, 0, we, sem_e)
    for j in range(1, 4):
        load_u[j].start()
        load_g[j].start()
    fetch_attn(idx, attn, w, sem_w, (-1, 1))
    small[...] = jnp.zeros_like(small)
    load_vec.wait()
    inv_gain = 1.0 / vec[10:11]
    for n, rows in enumerate(halves):
        for load in loads[n]:
            load.wait()
        grad = g[rows].astype(F32)
        normed = (x[rows] - vec[11:12]) * inv_gain
        add_small(small, 8, grad * normed)
        add_small(small, 9, grad)
        back = norm_rows_back(grad, normed, r2[rows], vec[10:11])
        low = back.astype(BF16)
        add_small(small, 7, low)
        acc[rows] = back
        e2[rows] = low
    for j in range(4):
        cols = slice(j * d, (j + 1) * d)
        load_u[j].wait()
        stage[4 + j] = tn(ur[j], e2[...]).astype(BF16)

        def go(b, carry):
            send_rows(idx, stage.at[4 + j, rows_of(b)], 4 * j + b // 4, b // 2 % 2, b % 2, 1, sums, sem_a.at[0])
            return carry

        lax.fori_loop(0, 16, go, 0)
        if j == 0:
            wait_rows(wc, sem_c)
            for n, rows in enumerate(halves):
                load_y[n].wait()
                y1r[rows] = y1[rows].astype(BF16)
        load_g[j].wait()
        for rows in halves:
            ef = (nt(e2[rows], wc[cols]) * gp[j, rows].astype(F32)).astype(BF16)
            gp[j, rows] = ef
            add_small(small, 3 + j, ef)
        stage[j] = tn(y1r[...], gp[j]).astype(BF16)
        send_square(idx, stage.at[j], j // 2, j % 2, 0, sums, sem_a.at[1])
        wait_square(we, sem_e, j)
        for rows in halves:
            acc[rows] += nt(gp[j, rows], we[j])
    wait_square(w, sem_w, 3)
    inv_gain = 1.0 / vec[3:4]
    saves = []
    for n, rows in enumerate(halves):
        load_r[n].wait()
        grad, normed = acc[rows], (y1[rows] - vec[4:5]) * inv_gain
        add_small(small, 1, grad * normed)
        add_small(small, 2, grad)
        back = norm_rows_back(grad, normed, r1[rows], vec[3:4])
        x[rows] = back
        low = back.astype(BF16)
        add_small(small, 0, low)
        da[rows] = nt(low, w[3]).astype(BF16)
        saves += [copy(x.at[rows], dh1_ref.at[rows], sem_d.at[n]), copy(da.at[rows], da_ref.at[rows], sem_d.at[2 + n])]
        saves[-2].start()
        saves[-1].start()
    saves.append(copy(small, small_ref, sem_d.at[4]))
    saves[-1].start()
    for save in saves:
        save.wait()
    copy(stage.at[4:8], stage.at[4:8], sem_a.at[0]).wait()
    copy(stage.at[0:4], stage.at[0:4], sem_a.at[1]).wait()


def ffn_backward(whole, idx, g, x, r2, y1, r1, vec, ur, gp, ffn_pieces, attn_pieces):
    t, d = x.shape
    sums = sums_shapes(d, whole, 2)
    pieces = tuple(ffn_pieces) + tuple(attn_pieces) if len(ffn_pieces) == 8 else tuple(ffn_pieces)
    return call(
        partial(ffn_backward_kernel, len(sums)),
        "ffn_backward",
        (idx, g, x, r2, y1, r1, vec, ur, gp) + pieces,
        [shape(t, d), shape(16, d), shape(t, d, dtype=BF16)] + sums,
        [
            pltpu.VMEM((t, d), g.dtype),
            pltpu.VMEM((t, d), F32),
            pltpu.VMEM((t, 1), F32),
            pltpu.VMEM((t, d), F32),
            pltpu.VMEM((t, 1), F32),
            pltpu.VMEM(vec.shape, F32),
            pltpu.VMEM((4, d, d), BF16),
            pltpu.VMEM((4 * d, d), BF16),
            pltpu.VMEM((4, d, d), BF16),
            pltpu.VMEM((4, t, d), BF16),
            pltpu.VMEM((4, t, d), BF16),
            pltpu.VMEM((t, d), F32),
            pltpu.VMEM((t, d), BF16),
            pltpu.VMEM((t, d), BF16),
            pltpu.VMEM((8, d, d), BF16),
            pltpu.VMEM((t, d), BF16),
            pltpu.VMEM((16, d), F32),
        ],
        32 * t * d * d,
        (2, 2, 2, 5, 4, 4, 4, 8, 5, 2),
    )


def ffn_both_kernel(idx, y1_ref, r1_ref, g_ref, vec_ref, *refs):
    given, refs = refs[:-32], refs[-32:]
    attn, given = (given[:1], given[:1]) if len(given) < 16 else (given[8:16], given[:8])
    x_ref, dh1_ref, small_ref, da_ref, sums = refs[:5]
    y1, r1, g, vec, we, wc, w, ur, gp, acc, x, n2, e2, y1r, stage, da, small = refs[5:22]
    sem_y, sem_r, sem_g, sem_vec, sem_e, sem_c, sem_w, sem_x, sem_d, sem_a = refs[22:]
    d = y1.shape[1]
    halves = halves_of(y1)
    load_y = load_halves(y1_ref, y1, sem_y, 0)
    load_vec = copy(vec_ref, vec, sem_vec.at[0])
    load_vec.start()
    fetch_ffn(idx, given, 0, we, sem_e)
    fetch_ffn(idx, given, 1, wc, sem_c)
    load_g = load_halves(g_ref, g, sem_g, 0)
    load_r = load_halves(r1_ref, r1, sem_r, 0)
    fetch_attn(idx, attn, w, sem_w, (-1, 1))
    small[...] = jnp.zeros_like(small)
    load_vec.wait()
    for n, rows in enumerate(halves):
        load_y[n].wait()
        y1r[rows] = y1[rows].astype(BF16)
    for j in range(4):
        cols = slice(j * d, (j + 1) * d)
        wait_square(we, sem_e, j)
        for n, rows in enumerate(halves):
            u, slope = gelu_pair(mm(y1r[rows], we[j]) + vec[5 + j : 6 + j])
            u = u.astype(BF16)
            ur[j, rows] = u
            gp[j, rows] = slope.astype(BF16)
            if j == 0 and n == 0:
                wait_rows(wc, sem_c)
            part = mm(u, wc[cols])
            if j == 0:
                acc[rows] = part
            else:
                acc[rows] += part
    saves = []
    for n, rows in enumerate(halves):
        normed, inv = norm_rows(y1[rows] + (acc[rows] + vec[9:10]))
        x[rows] = normed * vec[10:11] + vec[11:12]
        saves.append(copy(x.at[rows], x_ref.at[rows], sem_x.at[n]))
        saves[-1].start()
        load_g[n].wait()
        grad = g[rows].astype(F32)
        add_small(small, 8, grad * normed)
        add_small(small, 9, grad)
        back = norm_rows_back(grad, normed, inv, vec[10:11])
        low = back.astype(BF16)
        add_small(small, 7, low)
        acc[rows] = back
        e2[rows] = low
    for j in range(4):
        cols = slice(j * d, (j + 1) * d)
        stage[4 + j] = tn(ur[j], e2[...]).astype(BF16)

        def go(b, carry):
            send_rows(idx, stage.at[4 + j, rows_of(b)], 4 * j + b // 4, b // 2 % 2, b % 2, 1, (sums,), sem_a.at[0])
            return carry

        lax.fori_loop(0, 16, go, 0)
        for rows in halves:
            ef = (nt(e2[rows], wc[cols]) * gp[j, rows].astype(F32)).astype(BF16)
            gp[j, rows] = ef
            add_small(small, 3 + j, ef)
        stage[j] = tn(y1r[...], gp[j]).astype(BF16)
        send_square(idx, stage.at[j], j // 2, j % 2, 0, (sums,), sem_a.at[1])
        for rows in halves:
            acc[rows] += nt(gp[j, rows], we[j])
    wait_square(w, sem_w, 3)
    inv_gain = 1.0 / vec[3:4]
    for n, rows in enumerate(halves):
        load_r[n].wait()
        grad, normed = acc[rows], (y1[rows] - vec[4:5]) * inv_gain
        add_small(small, 1, grad * normed)
        add_small(small, 2, grad)
        back = norm_rows_back(grad, normed, r1[rows], vec[3:4])
        n2[rows] = back
        low = back.astype(BF16)
        add_small(small, 0, low)
        da[rows] = nt(low, w[3]).astype(BF16)
        saves += [copy(n2.at[rows], dh1_ref.at[rows], sem_d.at[n]), copy(da.at[rows], da_ref.at[rows], sem_d.at[2 + n])]
        saves[-2].start()
        saves[-1].start()
    saves.append(copy(small, small_ref, sem_d.at[4]))
    saves[-1].start()
    for save in saves:
        save.wait()
    copy(stage.at[4:8], stage.at[4:8], sem_a.at[0]).wait()
    copy(stage.at[0:4], stage.at[0:4], sem_a.at[1]).wait()


def ffn_both(idx, y1, r1, g, vec, ffn_pieces, attn_pieces):
    t, d = y1.shape
    pieces = tuple(ffn_pieces) + tuple(attn_pieces) if len(ffn_pieces) == 8 else tuple(ffn_pieces)
    return call(
        ffn_both_kernel,
        "ffn_both",
        (idx, y1, r1, g, vec) + pieces,
        [shape(t, d), shape(t, d), shape(16, d), shape(t, d, dtype=BF16)] + sums_shapes(d, True, 2),
        [
            pltpu.VMEM((t, d), F32),
            pltpu.VMEM((t, 1), F32),
            pltpu.VMEM((t, d), g.dtype),
            pltpu.VMEM(vec.shape, F32),
            pltpu.VMEM((4, d, d), BF16),
            pltpu.VMEM((4 * d, d), BF16),
            pltpu.VMEM((4, d, d), BF16),
            pltpu.VMEM((4, t, d), BF16),
            pltpu.VMEM((4, t, d), BF16),
            pltpu.VMEM((t, d), F32),
            pltpu.VMEM((t, d), F32),
            pltpu.VMEM((t, d), F32),
            pltpu.VMEM((t, d), BF16),
            pltpu.VMEM((t, d), BF16),
            pltpu.VMEM((8, d, d), BF16),
            pltpu.VMEM((t, d), BF16),
            pltpu.VMEM((16, d), F32),
        ],
        48 * t * d * d,
        (2, 2, 2, 1, 4, 4, 4, 2, 5, 2),
    )


def heads_backward_kernel(idx, da_ref, qkv_ref, p_ref, back_ref, small_ref, da, qkv, back, small, p, sem_in, sem_p, sem_out):
    t, d = da.shape
    length = t // 2
    pairs = d // (2 * HEAD_DIM)
    factor = HEAD_DIM**-0.5
    even = even_lanes()

    def load(step, slot):
        return copy(p_ref.at[pl.ds(2 * step, 2)], p.at[slot], sem_p.at[slot])

    load(0, 0).start()
    loads = load_halves(da_ref, da, sem_in, 0)
    for n, rows in enumerate(halves_of(da)):
        loads.append(copy(qkv_ref.at[:, rows], qkv.at[:, rows], sem_in.at[2 + n]))
        loads[-1].start()
    for n, rows in enumerate(halves_of(da)):
        loads[n].wait()
        loads[2 + n].wait()

        def pair(j, carry, n=n):
            step = n * pairs + j
            slot = step % 2

            @pl.when(step + 1 < 2 * pairs)
            def _():
                load(step + 1, 1 - slot).start()

            load(step, slot).wait()
            lanes = pl.ds(pl.multiple_of(j * 2 * HEAD_DIM, 2 * HEAD_DIM), 2 * HEAD_DIM)
            q2, k2, v2 = (qkv[i, n * length : (n + 1) * length, lanes] for i in range(3))
            da2 = da[n * length : (n + 1) * length, lanes]
            masks = (even, jnp.logical_not(even))
            k2t = k2.T
            dps = [nt(v2, jnp.where(mine, da2, jnp.zeros_like(da2))) for mine in masks]
            softs = [p[slot, h] for h in range(2)]
            dss = []
            for soft, dp in zip(softs, dps):
                soft = soft.astype(F32)
                inner = jnp.sum(soft * dp, axis=0, keepdims=True)
                dss.append((soft * (dp - inner)).astype(BF16))
            dv = jnp.where(even, mm(softs[0], da2), mm(softs[1], da2))
            dk = jnp.where(even, mm(dss[0], q2), mm(dss[1], q2))
            dq = jnp.concatenate([mm(k2t[h * HEAD_DIM : (h + 1) * HEAD_DIM], dss[h]) for h in range(2)], axis=0).T
            back[0, n * length : (n + 1) * length, lanes] = (dq * factor).astype(BF16)
            back[1, n * length : (n + 1) * length, lanes] = (dk * factor).astype(BF16)
            back[2, n * length : (n + 1) * length, lanes] = dv.astype(BF16)
            return carry

        lax.fori_loop(0, pairs, pair, 0)
        copy(back.at[:, rows], back_ref.at[:, rows], sem_out.at[n]).start()
    small[0:1] = jnp.sum(back[0].astype(F32), axis=0, keepdims=True)
    small[1:2] = jnp.sum(back[2].astype(F32), axis=0, keepdims=True)
    save = copy(small, small_ref, sem_out.at[2])
    save.start()
    for n, rows in enumerate(halves_of(da)):
        copy(back.at[:, rows], back_ref.at[:, rows], sem_out.at[n]).wait()
    save.wait()


def heads_backward(idx, da, qkv, p):
    t, d = da.shape
    length = t // 2
    return call(
        heads_backward_kernel,
        "heads_backward",
        (idx, da, qkv, p),
        [shape(3, t, d, dtype=BF16), shape(8, d)],
        [
            pltpu.VMEM((t, d), BF16),
            pltpu.VMEM((3, t, d), BF16),
            pltpu.VMEM((3, t, d), BF16),
            pltpu.VMEM((8, d), F32),
            pltpu.VMEM((2, 2, length, length), BF16),
        ],
        30 * t * length * d,
        (4, 2, 3),
    )


def inward_backward_kernel(count, idx, dh1_ref, x_ref, att_ref, back_ref, *refs):
    given, refs = refs[: -(16 + count)], refs[-(16 + count) :]
    dx_ref = refs[0]
    sums, refs = refs[1 : 1 + count], refs[1 + count :]
    dh1, x, att, back, w, stage, dx, sem_d, sem_x, sem_a, sem_b, sem_w, sem_out, sem_s, _ = refs[:15]
    halves = halves_of(x)
    load_x = load_halves(x_ref, x, sem_x, 0)
    load_b = [copy(back_ref.at[i], back.at[i], sem_b.at[i]) for i in range(3)]
    for load in load_b:
        load.start()
    fetch_attn(idx, given, w, sem_w, (None, 0))
    load_d = load_halves(dh1_ref, dh1, sem_d, 0)
    load_a = copy(att_ref, att, sem_a.at[0])
    load_a.start()
    for load in load_x:
        load.wait()
    xr = x[...].astype(BF16)
    for i, (core, s) in enumerate(((0, 0), (1, 0), (0, 1))):
        load_b[i].wait()
        stage[i] = tn(xr, back[i]).astype(BF16)
        send_square(idx, stage.at[i], core, s, 0, sums, sem_s.at[0])
    for load in load_d:
        load.wait()
    load_a.wait()
    stage[3] = tn(att[...], dh1[...].astype(BF16)).astype(BF16)
    send_square(idx, stage.at[3], 1, 1, 0, sums, sem_s.at[0])
    for i in range(3):
        wait_square(w, sem_w, i)
    saves = []
    for n, rows in enumerate(halves):
        dx[rows] = dh1[rows] + (nt(back[0, rows], w[0]) + nt(back[1, rows], w[1]) + nt(back[2, rows], w[2]))
        saves.append(copy(dx.at[rows], dx_ref.at[rows], sem_out.at[n]))
        saves[-1].start()
    for save in saves:
        save.wait()
    copy(stage, stage, sem_s.at[0]).wait()


def inward_backward(whole, idx, dh1, x, att, back, pieces):
    t, d = dh1.shape
    sums = sums_shapes(d, whole)
    return call(
        partial(inward_backward_kernel, len(sums)),
        "inward_backward",
        (idx, dh1, x, att, back) + tuple(pieces),
        [shape(t, d)] + sums,
        [
            pltpu.VMEM((t, d), F32),
            pltpu.VMEM((t, d), x.dtype),
            pltpu.VMEM((t, d), BF16),
            pltpu.VMEM((3, t, d), BF16),
            pltpu.VMEM((4, d, d), BF16),
            pltpu.VMEM((4, d, d), BF16),
            pltpu.VMEM((t, d), F32),
        ],
        14 * t * d * d,
        (2, 2, 1, 3, 4, 2, 1, 1),
    )


BITS = {"c": 1, "y": 2, "x": 4, "z1": 8, "z2": 16, "z3": 24}


def swap(array, by):
    return lax.ppermute(array, AXES, [(i, i ^ BITS[by]) for i in range(32)])


def tie(values, *others):
    return lax.optimization_barrier((values, others))[0]


def pair_up(share):
    return jnp.stack([share, swap(share, "z3")])


def column_up(pair):
    return jnp.concatenate([pair, swap(pair, "z1")])


def near_up(cols):
    return tuple(jnp.concatenate([col, swap(col, by)]) for col, by in zip(cols, "xy"))


def far_up(near):
    return tuple(swap(piece, by) for piece, by in zip(near, "yx"))


def other_core(pieces):
    return tuple(swap(piece, "c") for piece in pieces)


def in_order(near, far, near_c, far_c):
    return sum(((near[s], far[s], near_c[s], far_c[s]) for s in range(2)), ())


def place_small(qb, vb, ob, ag, ash, eb, cb, fg, fs, width, device):
    layers, rows = qb.shape
    lanes = lax.broadcasted_iota(jnp.int32, (1, 1, width), 2)
    thin = jnp.stack([qb, vb, ob, ag, ash, cb, fg, fs], axis=1).astype(F32)
    thin = jnp.where(lanes // rows == device, jnp.tile(thin, (1, 1, width // rows)), 0.0)
    lines = lax.broadcasted_iota(jnp.int32, (1, 4, width), 1)
    wide = jnp.tile(eb.astype(F32)[:, None], (1, 4, width // eb.shape[1]))
    wide = jnp.where(lines * (width // eb.shape[1]) + lanes // eb.shape[1] == device, wide, 0.0)
    return jnp.concatenate([thin[:, 0:5], wide, thin[:, 5:8], jnp.zeros((layers, 4, width), F32)], axis=1)


def own_small(total, rows, device):
    layers, _, width = total.shape
    thin = lax.dynamic_slice_in_dim(total, device * rows, rows, 2)
    count = width // (4 * rows)
    wide = lax.dynamic_slice(total, (0, 5 + device // count, device % count * 4 * rows), (layers, 1, 4 * rows))
    return [thin[:, i] for i in range(5)] + [wide[:, 0]] + [thin[:, i] for i in range(9, 12)]


def add_swap(array, by):
    return array + swap(array, by)


class Sums:
    def __init__(self, keep, give):
        self.both = [keep]
        self.parts = [[], []]
        self.give = give

    def total(self, s, lo, hi):
        whole = None
        for a in [b[s] for b in self.both] + self.parts[s]:
            a = a[lo:hi].astype(F32)
            whole = a if whole is None else whole + a
        return whole

    def latest(self):
        return self.parts if self.parts[0] else self.both

    def hold(self, *others):
        if self.parts[0]:
            self.parts = tie(self.parts, *others)
        else:
            self.both = tie(self.both, *others)

    def core(self):
        self.both = self.both + [swap(self.give, "c")]

    def plane(self, lo, bys):
        arrived = [swap(self.total(s, lo, 2 * lo).astype(BF16), bys[s]) for s in range(2)]
        for s in range(2):
            self.parts[s] = self.parts[s] + [arrived[s]]

    def first(self):
        self.plane(8, "yx")

    def second(self):
        self.plane(4, "xy")

    def line(self, lo, by):
        arrived = swap(jnp.stack([self.total(s, lo, 2 * lo) for s in range(2)]).astype(BF16), by)
        for s in range(2):
            self.parts[s] = self.parts[s] + [arrived[s]]

    def third(self):
        self.line(2, "z1")

    def fourth(self):
        self.line(1, "z3")

    def result(self):
        return jnp.stack([self.total(s, 0, 1)[0] for s in range(2)])


def front(first, last, rows, width, c, attention):
    layers = first.shape[0]
    first = first.reshape(layers, rows, -1)
    cut = lambda i: first[:, :, i * width : (i + 1) * width]
    if attention:
        zero, one = (cut(0), cut(2)), (cut(1), last.reshape(layers, rows, width))
    else:
        zero, one = (cut(0), cut(1)), (cut(2), cut(3))
    zero, one = jnp.stack(zero, 1), jnp.stack(one, 1)
    return jnp.where(c == 0, zero, one), jnp.where(c == 0, one, zero)


def both_cores(mine, got, c):
    return jnp.where(c == 0, jnp.concatenate([mine, got], 2), jnp.concatenate([got, mine], 2))


def gather_any(w_inward, w_outward, w_expand, w_contract, width):
    whole = lambda m, n: lax.all_gather(m, AXES, axis=0, tiled=True).reshape(-1, n)
    inward, outward = whole(w_inward, 3 * width), whole(w_outward, width)
    expand, contract = whole(w_expand, 4 * width), whole(w_contract, width)
    cut = lambda m, i: m[:, i * width : (i + 1) * width].reshape(16, SHARE, width)
    squares = [cut(inward, i) for i in range(3)] + [cut(outward, 0)] + [cut(expand, i) for i in range(4)]
    down = contract.reshape(16, 2, 2, SHARE, width)
    sides = []
    for core in range(2):
        pick = (core, 2 + core, 4 + 2 * core, 5 + 2 * core)
        pairs = [squares[i] for i in pick] + [down[:, core, s] for s in range(2)]
        sides.append(jnp.stack(pairs, 1).reshape(16, 3, 2, SHARE, width))
    return jnp.stack(sides, 1).reshape(32, 3, 2, SHARE, width)


def collect_any(attn, ffn, width):
    attn = attn.reshape(16, 2, 2, SHARE, width)
    ffn = ffn.reshape(16, 2, 2, 2, SHARE, width)
    expand, contract = ffn[:, :, :, 0], ffn[:, :, :, 1]
    inward = jnp.concatenate([attn[:, 0, 0], attn[:, 1, 0], attn[:, 0, 1]], axis=-1)
    expand = jnp.concatenate([expand[:, core, s] for core in range(2) for s in range(2)], axis=-1)
    return tuple(
        lax.psum_scatter(m.reshape(-1).astype(F32), AXES, scatter_dimension=0, tiled=True)
        for m in (inward, attn[:, 1, 1], expand, contract)
    )


def local(blocked, tokens, lengths, w_inward, qb, vb, w_outward, ob, ag, ash, w_expand, eb, w_contract, cb, fg, fs, cotangent):
    layers = w_inward.shape[0]
    width = tokens.shape[-1]
    rows = qb.shape[1]
    device = lax.axis_index("wide") * lax.axis_size("narrow") + lax.axis_index("narrow")
    me = device if blocked else jnp.int32(0)
    c = me & 1
    place = jnp.stack([me >> 3, (me >> 2) & 1, (me >> 1) & 1, c]).astype(jnp.int32)
    idx = jnp.concatenate([place, lengths.reshape(-1), jnp.zeros((2,), jnp.int32)])
    small = place_small(qb, vb, ob, ag, ash, eb, cb, fg, fs, width, device)
    x = tokens.reshape(-1, width)
    kept = []

    def keep_layer(x, y1, attn, ffn, attn_pieces, ffn_pieces):
        kept.append((x, y1) + tuple(attn[1:]) + tuple(ffn) + (attn_pieces, ffn_pieces))
        return ffn[0]

    if blocked:
        mine, got = front(w_inward, w_outward, rows, width, c, True)
        halves = lambda col: (col[:, 0, None], col[:, 1, None])
        halves2 = lambda col: (col[:, :, 0], col[:, :, 1])
        share_a = both_cores(mine, swap(got, "c"), c)
        small = add_swap(small, "c")
        mine, got = front(w_expand, None, rows, width, c, False)
        share_e = both_cores(mine, swap(got, "c"), c)
        contract = w_contract.reshape(layers, 2, SHARE, width)
        share_f = [jnp.stack([share_e[l], contract[l]]) for l in range(layers)]
        a_pair = pair_up(share_a[0])
        share, a_pair, small = tie((share_f[0], a_pair, small))
        f_pair = pair_up(share)
        a_col = column_up(a_pair)
        small = add_swap(small, "z1")
        f_pair, a_col, small = tie((f_pair, a_col, small))
        f_col = column_up(f_pair)
        a_near = near_up(halves(a_col))
        small = add_swap(small, "z2")
        a_near, small = tie((a_near, small))
        a_far = far_up(a_near)
        a_core = other_core(a_near)
        f_col, a_far, small = tie((f_col, a_far, small))
        f_near = near_up(halves2(f_col))
        small = add_swap(small, "x")
        a1_pair = pair_up(tie((share_a[1], a_far))[0])
        a_core += other_core(a_far)
        x, f_near, a1_pair, small = tie((x, f_near, a1_pair, small))
        f_far = far_up(f_near)
        small = add_swap(small, "y")
        a1_col = column_up(a1_pair)
        f_core = other_core(f_near)
        vecs = [small[l] for l in range(layers)]
        a_pieces = in_order(a_near, a_far, a_core[:2], a_core[2:])
        attn = attn_forward(idx, x, vecs[0], a_pieces)
        f_far, a1_col, f_core, y1, share = tie((f_far, a1_col, f_core, attn[0], share_f[1]))
        f_core += other_core(f_far)
        a1_near = near_up(halves(a1_col))
        f1_pair = pair_up(share)
        y1, a1_near, f1_pair = tie((y1, a1_near, f1_pair))
        a1_far = far_up(a1_near)
        f1_col = column_up(f1_pair)
        f_pieces = in_order(f_near, f_far, f_core[:2], f_core[2:])
        ffn = ffn_forward(idx, y1, vecs[0], f_pieces)
        x1 = keep_layer(x, y1, attn, ffn, a_pieces, f_pieces)
        a1_far, f1_col, x1 = tie((a1_far, f1_col, x1))
        a1_core = other_core(a1_near + a1_far)
        f1_near = near_up(halves2(f1_col))
        x1, f1_near = tie((x1, f1_near))
        f1_far = far_up(f1_near)
        f1_core = other_core(f1_near)
        a1_pieces = in_order(a1_near, a1_far, a1_core[:2], a1_core[2:])
        attn = attn_forward(idx, x1, vecs[1], a1_pieces)
        f1_far, f1_core, y1 = tie((f1_far, f1_core, attn[0]))
        f1_core += other_core(f1_far)
        f1_pieces = in_order(f1_near, f1_far, f1_core[:2], f1_core[2:])
        output, dh1, small, da, whole = ffn_both(idx, y1, attn[1], cotangent.reshape(-1, width), vecs[1], f1_pieces, a1_pieces)
        keep_layer(x1, y1, attn, (output, None, None, None), a1_pieces, f1_pieces)
    else:
        small = lax.psum(small, AXES)
        vecs = [small[l] for l in range(layers)]
        for l in range(layers):
            pieces = (gather_any(w_inward[l], w_outward[l], w_expand[l], w_contract[l], width),)
            attn = attn_forward(idx, x, vecs[l], pieces)
            if l + 1 < layers:
                x = keep_layer(x, attn[0], attn, ffn_forward(idx, attn[0], vecs[l], pieces), pieces, pieces)
        output, dh1, small, da, whole = ffn_both(idx, attn[0], attn[1], cotangent.reshape(-1, width), vecs[l], pieces, pieces)
        keep_layer(x, attn[0], attn, (output, None, None, None), pieces, pieces)
    w_sums, smalls = [None] * layers, [None] * layers

    def ffn_back(l, g):
        x, y1, r1, qkv, p, att, out, r2, ur, gp, attn_pieces, ffn_pieces = kept[l]
        return ffn_backward(not blocked, idx, g, out, r2, y1, r1, vecs[l], ur, gp, ffn_pieces, attn_pieces)

    def heads_back(l, da):
        x, y1, r1, qkv, p, att, out, r2, ur, gp, attn_pieces, ffn_pieces = kept[l]
        return heads_backward(idx, da, qkv, p)

    def inward_back(l, dh1, back):
        x, y1, r1, qkv, p, att, out, r2, ur, gp, attn_pieces, ffn_pieces = kept[l]
        return inward_backward(not blocked, idx, dh1, x, att, back, attn_pieces)

    if blocked:
        f1 = lax.psum_scatter(whole, AXES, scatter_dimension=0, tiled=True)
        back, small_h = heads_back(1, da)
        smalls[1] = jnp.concatenate([small_h[0:2], small[0:10]])
        g, *sums = inward_back(1, dh1, back)
        a1 = Sums(*sums)
        a1.core()
        dh1, small, da, *sums = ffn_back(0, g)
        f0 = Sums(*sums)
        da, f0.give, a1.both = tie((da, f0.give, a1.both))
        f0.core()
        a1.first()
        back, small_h = heads_back(0, da)
        smalls[0] = jnp.concatenate([small_h[0:2], small[0:10]])
        back, a1.parts, f0.both = tie((back, a1.parts, f0.both))
        f0.first()
        a1.second()
        g, *sums = inward_back(0, dh1, back)
        a0 = Sums(*sums)
        a0.give, a1.parts, f0.parts = tie((a0.give, a1.parts, f0.parts))
        a0.core()
        f0.second()
        a1.third()
        a0.both, a1.parts = tie((a0.both, a1.parts))
        a0.first()
        a1.fourth()
        small, f0.parts = tie((jnp.stack(smalls), f0.parts))
        f0.third()
        small = add_swap(small, "z2")
        small, a0.parts, f1 = tie((small, a0.parts, f1))
        a0.second()
        small = add_swap(small, "x")
        small, a0.parts, f0.parts = tie((small, a0.parts, f0.parts))
        a0.third()
        f0.fourth()
        small = add_swap(small, "y")
        small, a0.parts, f0.parts = tie((small, a0.parts, f0.parts))
        a0.fourth()
        small = add_swap(small, "z1")
        small, a0.parts = tie((small, a0.parts))
        small = add_swap(small, "c")
        f1 = f1[0].astype(F32)
        f0 = f0.result()
        a0, a1 = (m.result()[:, 0] for m in (a0, a1))
        w_sums = [(a0, f0[:, 0], f0[:, 1]), (a1, f1[:, 0], f1[:, 1])]
    else:
        for l in reversed(range(layers)):
            if l + 1 < layers:
                dh1, small, da, whole = ffn_back(l, g)
            back, small_h = heads_back(l, da)
            g, sums_a = inward_back(l, dh1, back)
            smalls[l] = jnp.concatenate([small_h[0:2], small[0:10]])
            w_sums[l] = collect_any(sums_a, whole, width)
        small = lax.psum(jnp.stack(smalls), AXES)
    names = ("qb", "vb", "ob", "ag", "as", "eb", "cb", "fg", "fs")
    outs = dict(zip(names, own_small(small, rows, device)))
    flat = {"in": [], "out": [], "ex": [], "co": []}
    for l in range(layers):
        if not blocked:
            for name, share in zip(("in", "out", "ex", "co"), w_sums[l]):
                flat[name].append(share)
            continue
        attn, expand, contract = w_sums[l]
        squares = jnp.stack([attn[0], attn[1], expand[0], expand[1]])
        low, high = squares[:, :rows], squares[:, rows:]
        mine = jnp.where(c == 0, low, high)
        got = swap(jnp.where(c == 0, high, low), "c")
        zero, one = jnp.where(c == 0, mine, got), jnp.where(c == 0, got, mine)
        flat["in"].append(jnp.concatenate([zero[0], one[0], zero[1]], axis=1).reshape(-1))
        flat["out"].append(one[1].reshape(-1))
        flat["ex"].append(jnp.concatenate([zero[2], zero[3], one[2], one[3]], axis=1).reshape(-1))
        flat["co"].append(contract.reshape(-1))
    flat = {k: jnp.stack(v) for k, v in flat.items()}
    shape = tokens.shape
    return (
        output.reshape(shape), g.reshape(shape), flat["in"], outs["qb"], outs["vb"], flat["out"], outs["ob"],
        outs["ag"], outs["as"], flat["ex"], outs["eb"], flat["co"], outs["cb"], outs["fg"], outs["fs"],
    )


def solution(mesh):
    flat = P(None, AXES)
    deep = P(None, AXES, None, None)
    blocked = mesh.shape["wide"] == 8 and mesh.shape["narrow"] == 4
    return jax.shard_map(
        partial(local, blocked),
        mesh=mesh,
        in_specs=(deep,) + (flat,) * 14 + (deep,),
        out_specs=(deep, deep) + (flat,) * 13,
        check_vma=False,
    )
```

```python
import math
from functools import partial

import jax
import jax.numpy as jnp
from jax import lax
from jax.experimental import pallas as pl
from jax.experimental.pallas import tpu as pltpu
from jax.sharding import PartitionSpec as P

HEAD_DIM = 64
EPSILON = 1e-06
AXES = ("wide", "narrow")
F32 = jnp.float32
BF16 = jnp.bfloat16
ANY = pl.BlockSpec(memory_space=pl.ANY)
VMEM = pl.BlockSpec(memory_space=pltpu.VMEM)
SMEM = pl.BlockSpec(memory_space=pltpu.SMEM)
LIMIT = 60 * 2**20
SHARE = 48


def mm(left, right, over=(1, 0)):
    return lax.dot_general(
        left, right, (((over[0],), (over[1],)), ((), ())), preferred_element_type=F32
    )


def nt(left, right):
    return mm(left, right, (1, 1))


def tn(left, right):
    return mm(left, right, (0, 0))


def norm_rows(h):
    centred = h - jnp.mean(h, axis=-1, keepdims=True)
    inv = lax.rsqrt(jnp.mean(centred * centred, axis=-1, keepdims=True) + EPSILON)
    return centred * inv, inv


def norm_rows_back(g, n, inv, gain):
    t = g * gain
    return inv * (
        t
        - jnp.mean(t, axis=-1, keepdims=True)
        - n * jnp.mean(t * n, axis=-1, keepdims=True)
    )


def gelu_pair(f):
    u = jnp.abs(f)
    t = 1.0 / (1.0 + (0.3275911 / math.sqrt(2.0)) * u)
    e = jnp.exp(-0.5 * f * f)
    c = [0.5 * v for v in (0.254829592, -0.284496736, 1.421413741, -1.453152027, 1.061405429)]
    tail = e * (t * (c[0] + t * (c[1] + t * (c[2] + t * (c[3] + t * c[4])))))
    phi = jnp.where(f >= 0, 1.0 - tail, tail)
    return f * phi, phi + f * (e * (1.0 / math.sqrt(2.0 * math.pi)))


def even_lanes():
    return lax.broadcasted_iota(jnp.int32, (1, 2 * HEAD_DIM), 1) < HEAD_DIM


def place_of(idx, block, far, first_is_x):
    k, other = block % 4, block // 4
    z = idx[0] ^ (3 * (k % 2)) ^ (k // 2)
    if first_is_x:
        x, y = idx[1] ^ other, idx[2] ^ far
    else:
        x, y = idx[1] ^ far, idx[2] ^ other
    return z * 4 + x * 2 + y


def relative_of(idx, chip, first_is_x):
    r = (chip // 4) ^ idx[0]
    k = (r // 2) + 2 * ((r ^ (r // 2)) % 2)
    i = (chip // 2 % 2) ^ idx[1]
    j = (chip % 2) ^ idx[2]
    return (i * 8 + j * 4 + k) if first_is_x else (j * 8 + i * 4 + k)


def copy(src, dst, sem):
    return pltpu.make_async_copy(src, dst, sem)


def halves_of(ref):
    length = ref.shape[0] // 2
    return [slice(n * length, (n + 1) * length) for n in range(2)]


def add_small(ref, row, value):
    ref[row : row + 1] += jnp.sum(value.astype(F32), axis=0, keepdims=True)


def load_halves(src, dst, sems, at):
    loads = [copy(src.at[rows], dst.at[rows], sems.at[at + n]) for n, rows in enumerate(halves_of(src))]
    for load in loads:
        load.start()
    return loads


def rows_of(chip):
    return pl.ds(pl.multiple_of(chip * SHARE, SHARE), SHARE)


def fetch_attn(idx, given, w, sem, cores=(None, None)):
    if len(given) == 1:

        def whole(chip, carry):
            for s in range(2):
                for core in (0, 1) if cores[s] is None else (cores[s],):
                    square = 2 * s + core
                    copy(given[0].at[2 * chip + core, 0, s], w.at[square, rows_of(chip)], sem.at[square]).start()
            return carry

        lax.fori_loop(0, 16, whole, 0)
        return

    def go(block, carry):
        for s in range(2):
            if cores[s] == -1:
                continue
            for side in range(2):
                core = idx[3] ^ side

                def start(s=s, side=side, core=core):
                    for far in range(2):
                        rows = rows_of(place_of(idx, block, far, s == 0))
                        copy(given[4 * s + 2 * side + far].at[block, 0], w.at[2 * s + core, rows], sem.at[2 * s + core]).start()

                if cores[s] is None:
                    start()
                else:
                    pl.when(core == cores[s])(start)
        return carry

    lax.fori_loop(0, 8, go, 0)


def wait_square(w, sem, square):
    copy(w.at[square], w.at[square], sem.at[square]).wait()


def fetch_ffn(idx, given, m, w, sem):
    def place(chip, core, s):
        if m == 0:
            return w.at[2 * core + s, rows_of(chip)]
        return w.at[pl.ds(pl.multiple_of((chip * 4 + core * 2 + s) * SHARE, SHARE), SHARE)]

    def whole(chip, carry):
        for s in range(2):
            for core in range(2):
                copy(given[0].at[2 * chip + core, 1 + m, s], place(chip, core, s), sem.at[2 * core + s]).start()
        return carry

    def go(block, carry):
        for s in range(2):
            for side in range(2):
                core = idx[3] ^ side
                for far in range(2):
                    chip = place_of(idx, block, far, s == 0)
                    copy(given[4 * s + 2 * side + far].at[block, m], place(chip, core, s), sem.at[2 * core + s]).start()
        return carry

    if len(given) == 1:
        lax.fori_loop(0, 16, whole, 0)
    else:
        lax.fori_loop(0, 8, go, 0)


def wait_rows(w, sem):
    quarter = w.shape[0] // 4
    for i in range(4):
        copy(w.at[pl.ds(0, quarter)], w.at[pl.ds(0, quarter)], sem.at[i]).wait()


def call(kernel, name, operands, out_shape, scratch, flops, sems, aliases=None):
    return pl.pallas_call(
        kernel,
        in_specs=[SMEM] + [ANY] * (len(operands) - 1),
        out_specs=[ANY] * len(out_shape),
        out_shape=out_shape,
        scratch_shapes=scratch + [pltpu.SemaphoreType.DMA((n,)) for n in sems],
        input_output_aliases=aliases or {},
        compiler_params=pltpu.CompilerParams(vmem_limit_bytes=LIMIT),
        cost_estimate=pl.CostEstimate(flops=flops, bytes_accessed=30 * 2**20, transcendentals=0),
        name=name,
    )(*operands)


def shape(*dims, dtype=F32):
    return jax.ShapeDtypeStruct(dims, dtype)


def attn_forward_kernel(idx, x_ref, vec_ref, *refs):
    given, refs = refs[:-20], refs[-20:]
    y1_ref, r1_ref, qkv_ref, p_ref, att_ref = refs[:5]
    x, vec, w, qkv, p, att, y1, r1, sem_x, sem_vec, sem_w, sem_y, sem_r, sem_q, sem_p = refs[5:]
    loads = load_halves(x_ref, x, sem_x, 0)
    load_vec = copy(vec_ref, vec, sem_vec.at[0])
    load_vec.start()
    fetch_attn(idx, given, w, sem_w)
    load_vec.wait()
    halves = halves_of(x)
    length = halves[0].stop
    for n, rows in enumerate(halves):
        loads[n].wait()
        xr = x[rows].astype(BF16)
        for i in range(3):
            if n == 0:
                wait_square(w, sem_w, i)
            joined = mm(xr, w[i])
            if i != 1:
                joined = joined + vec[i // 2 : i // 2 + 1]
            qkv[i, rows] = joined.astype(BF16)
    save_qkv = copy(qkv, qkv_ref, sem_q.at[0])
    save_qkv.start()
    pairs = x.shape[1] // (2 * HEAD_DIM)
    places = lax.broadcasted_iota(jnp.int32, (length, 1), 0)
    even = even_lanes()

    def pair(step, carry):
        n, j = step // pairs, step % pairs
        rows = pl.ds(pl.multiple_of(n * length, length), length)
        lanes = pl.ds(pl.multiple_of(j * 2 * HEAD_DIM, 2 * HEAD_DIM), 2 * HEAD_DIM)
        hidden = jnp.where(places < idx[4 + n], 0.0, -1e30)
        q2 = qkv[0, rows, lanes] * jnp.asarray(HEAD_DIM**-0.5, BF16)
        k2 = qkv[1, rows, lanes]
        v2 = qkv[2, rows, lanes].T
        masks = (even, jnp.logical_not(even))
        scores = [nt(k2, jnp.where(mine, q2, jnp.zeros_like(q2))) + hidden for mine in masks]
        parts = []
        for h, s in enumerate(scores):
            e = jnp.exp(s - jnp.max(s, axis=0, keepdims=True))
            soft = (e * (1.0 / jnp.sum(e, axis=0, keepdims=True))).astype(BF16)
            p[2 * step + h] = soft
            parts.append(mm(v2[h * HEAD_DIM : (h + 1) * HEAD_DIM], soft))
        att[rows, lanes] = jnp.concatenate(parts, axis=0).T.astype(BF16)
        copy(p.at[pl.ds(2 * step, 2)], p_ref.at[pl.ds(2 * step, 2)], sem_p.at[0]).start()
        return carry

    lax.fori_loop(0, 2 * pairs, pair, 0, unroll=3)
    save_att = copy(att, att_ref, sem_q.at[1])
    save_att.start()
    wait_square(w, sem_w, 3)
    saves = [save_qkv, save_att]
    for n, rows in enumerate(halves):
        h = x[rows].astype(F32) + (mm(att[rows], w[3]) + vec[2:3])
        normed, inv = norm_rows(h)
        y1[rows] = normed * vec[3:4] + vec[4:5]
        r1[rows] = inv
        saves += [copy(y1.at[rows], y1_ref.at[rows], sem_y.at[n]), copy(r1.at[rows], r1_ref.at[rows], sem_r.at[n])]
        saves[-2].start()
        saves[-1].start()
    for save in saves:
        save.wait()
    copy(p, p_ref, sem_p.at[0]).wait()


def attn_forward(idx, x, vec, pieces):
    t, d = x.shape
    heads = d // HEAD_DIM
    length = t // 2
    return call(
        attn_forward_kernel,
        "attn_forward",
        (idx, x, vec) + tuple(pieces),
        [shape(t, d), shape(t, 1), shape(3, t, d, dtype=BF16), shape(2 * heads, length, length, dtype=BF16), shape(t, d, dtype=BF16)],
        [
            pltpu.VMEM((t, d), x.dtype),
            pltpu.VMEM(vec.shape, F32),
            pltpu.VMEM((4, d, d), BF16),
            pltpu.VMEM((3, t, d), BF16),
            pltpu.VMEM((2 * heads, length, length), BF16),
            pltpu.VMEM((t, d), BF16),
            pltpu.VMEM((t, d), F32),
            pltpu.VMEM((t, 1), F32),
        ],
        8 * t * d * d + 4 * t * length * d,
        (2, 1, 4, 2, 2, 2, 1),
    )


def ffn_forward_kernel(idx, y1_ref, vec_ref, *refs):
    given, refs = refs[:-22], refs[-22:]
    x_ref, r2_ref, ur_ref, gp_ref = refs[:4]
    y1, vec, we, wc, ur, gp, acc, x, r2, sem_y, sem_vec, sem_e, sem_c, sem_x, sem_r, sem_u, sem_g, sem_z = refs[4:]
    del sem_z
    loads = load_halves(y1_ref, y1, sem_y, 0)
    load_vec = copy(vec_ref, vec, sem_vec.at[0])
    load_vec.start()
    fetch_ffn(idx, given, 0, we, sem_e)
    fetch_ffn(idx, given, 1, wc, sem_c)
    load_vec.wait()
    d = y1.shape[1]
    halves = halves_of(y1)
    for j in range(4):
        cols = slice(j * d, (j + 1) * d)
        wait_square(we, sem_e, j)
        for n, rows in enumerate(halves):
            if j == 0:
                loads[n].wait()
            f = mm(y1[rows].astype(BF16), we[j]) + vec[5 + j : 6 + j]
            u, slope = gelu_pair(f)
            u = u.astype(BF16)
            ur[j, rows] = u
            gp[j, rows] = slope.astype(BF16)
            if j == 0 and n == 0:
                wait_rows(wc, sem_c)
            part = mm(u, wc[cols])
            if j == 0:
                acc[rows] = part
            else:
                acc[rows] += part
        copy(ur.at[j], ur_ref.at[j], sem_u.at[0]).start()
        copy(gp.at[j], gp_ref.at[j], sem_g.at[0]).start()
    saves = []
    for n, rows in enumerate(halves):
        normed, inv = norm_rows(y1[rows] + (acc[rows] + vec[9:10]))
        x[rows] = normed * vec[10:11] + vec[11:12]
        r2[rows] = inv
        saves += [copy(x.at[rows], x_ref.at[rows], sem_x.at[n]), copy(r2.at[rows], r2_ref.at[rows], sem_r.at[n])]
        saves[-2].start()
        saves[-1].start()
    for save in saves:
        save.wait()
    copy(ur, ur_ref, sem_u.at[0]).wait()
    copy(gp, gp_ref, sem_g.at[0]).wait()


def ffn_forward(idx, y1, vec, pieces):
    t, d = y1.shape
    return call(
        ffn_forward_kernel,
        "ffn_forward",
        (idx, y1, vec) + tuple(pieces),
        [shape(t, d), shape(t, 1), shape(4, t, d, dtype=BF16), shape(4, t, d, dtype=BF16)],
        [
            pltpu.VMEM((t, d), F32),
            pltpu.VMEM(vec.shape, F32),
            pltpu.VMEM((4, d, d), BF16),
            pltpu.VMEM((4 * d, d), BF16),
            pltpu.VMEM((4, t, d), BF16),
            pltpu.VMEM((4, t, d), BF16),
            pltpu.VMEM((t, d), F32),
            pltpu.VMEM((t, d), F32),
            pltpu.VMEM((t, 1), F32),
        ],
        16 * t * d * d,
        (2, 1, 4, 4, 2, 2, 1, 1, 1),
    )


def send_rows(idx, block, chip, core, s, m, sums, sem):
    if len(sums) == 1:
        copy(block, sums[0].at[2 * chip + core, s, m], sem).start()
        return
    keep, give = sums
    to = jnp.where(s == 1, relative_of(idx, chip, True), relative_of(idx, chip, False))

    @pl.when(core == idx[3])
    def _():
        copy(block, keep.at[s, to, m], sem).start()

    @pl.when(core != idx[3])
    def _():
        copy(block, give.at[s, to, m], sem).start()


def send_square(idx, stage, core, s, m, sums, sem):
    def go(chip, carry):
        send_rows(idx, stage.at[rows_of(chip)], chip, core, s, m, sums, sem)
        return carry

    lax.fori_loop(0, 16, go, 0)


def sums_shapes(d, whole, m=1):
    if whole:
        return [shape(32, 2, m, SHARE, d, dtype=BF16)]
    return [shape(2, 16, m, SHARE, d, dtype=BF16)] * 2


def ffn_backward_kernel(count, idx, g_ref, x_ref, r2_ref, y1_ref, r1_ref, vec_ref, ur_ref, gp_ref, *refs):
    given, refs = refs[: -(30 + count)], refs[-(30 + count) :]
    attn, given = (given[:1], given[:1]) if len(given) < 16 else (given[8:16], given[:8])
    dh1_ref, small_ref, da_ref = refs[:3]
    sums, refs = refs[3 : 3 + count], refs[3 + count :]
    g, x, r2, y1, r1, vec, we, wc, w, ur, gp, acc, e2, y1r, stage, da, small = refs[:17]
    sem_g, sem_x, sem_y, sem_r, sem_e, sem_c, sem_w, sem_u, sem_d, sem_a = refs[17:]
    d = y1.shape[1]
    halves = halves_of(y1)
    load_vec = copy(vec_ref, vec, sem_r.at[4])
    load_vec.start()
    loads = list(zip(load_halves(g_ref, g, sem_g, 0), load_halves(x_ref, x, sem_x, 0), load_halves(r2_ref, r2, sem_r, 0)))
    load_u = [copy(ur_ref.at[j], ur.at[j], sem_u.at[j]) for j in range(4)]
    load_g = [copy(gp_ref.at[j], gp.at[j], sem_u.at[4 + j]) for j in range(4)]
    load_u[0].start()
    fetch_ffn(idx, given, 1, wc, sem_c)
    load_g[0].start()
    load_y = load_halves(y1_ref, y1, sem_y, 0)
    load_r = load_halves(r1_ref, r1, sem_r, 2)
    fetch_ffn(idx, given, 0, we, sem_e)
    for j in range(1, 4):
        load_u[j].start()
        load_g[j].start()
    fetch_attn(idx, attn, w, sem_w, (-1, 1))
    small[...] = jnp.zeros_like(small)
    load_vec.wait()
    inv_gain = 1.0 / vec[10:11]
    for n, rows in enumerate(halves):
        for load in loads[n]:
            load.wait()
        grad = g[rows].astype(F32)
        normed = (x[rows] - vec[11:12]) * inv_gain
        add_small(small, 8, grad * normed)
        add_small(small, 9, grad)
        back = norm_rows_back(grad, normed, r2[rows], vec[10:11])
        low = back.astype(BF16)
        add_small(small, 7, low)
        acc[rows] = back
        e2[rows] = low
    for j in range(4):
        cols = slice(j * d, (j + 1) * d)
        load_u[j].wait()
        stage[4 + j] = tn(ur[j], e2[...]).astype(BF16)

        def go(b, carry):
            send_rows(idx, stage.at[4 + j, rows_of(b)], 4 * j + b // 4, b // 2 % 2, b % 2, 1, sums, sem_a.at[0])
            return carry

        lax.fori_loop(0, 16, go, 0)
        if j == 0:
            wait_rows(wc, sem_c)
            for n, rows in enumerate(halves):
                load_y[n].wait()
                y1r[rows] = y1[rows].astype(BF16)
        load_g[j].wait()
        for rows in halves:
            ef = (nt(e2[rows], wc[cols]) * gp[j, rows].astype(F32)).astype(BF16)
            gp[j, rows] = ef
            add_small(small, 3 + j, ef)
        stage[j] = tn(y1r[...], gp[j]).astype(BF16)
        send_square(idx, stage.at[j], j // 2, j % 2, 0, sums, sem_a.at[1])
        wait_square(we, sem_e, j)
        for rows in halves:
            acc[rows] += nt(gp[j, rows], we[j])
    wait_square(w, sem_w, 3)
    inv_gain = 1.0 / vec[3:4]
    saves = []
    for n, rows in enumerate(halves):
        load_r[n].wait()
        grad, normed = acc[rows], (y1[rows] - vec[4:5]) * inv_gain
        add_small(small, 1, grad * normed)
        add_small(small, 2, grad)
        back = norm_rows_back(grad, normed, r1[rows], vec[3:4])
        x[rows] = back
        low = back.astype(BF16)
        add_small(small, 0, low)
        da[rows] = nt(low, w[3]).astype(BF16)
        saves += [copy(x.at[rows], dh1_ref.at[rows], sem_d.at[n]), copy(da.at[rows], da_ref.at[rows], sem_d.at[2 + n])]
        saves[-2].start()
        saves[-1].start()
    saves.append(copy(small, small_ref, sem_d.at[4]))
    saves[-1].start()
    for save in saves:
        save.wait()
    copy(stage.at[4:8], stage.at[4:8], sem_a.at[0]).wait()
    copy(stage.at[0:4], stage.at[0:4], sem_a.at[1]).wait()


def ffn_backward(whole, idx, g, x, r2, y1, r1, vec, ur, gp, ffn_pieces, attn_pieces):
    t, d = x.shape
    sums = sums_shapes(d, whole, 2)
    pieces = tuple(ffn_pieces) + tuple(attn_pieces) if len(ffn_pieces) == 8 else tuple(ffn_pieces)
    return call(
        partial(ffn_backward_kernel, len(sums)),
        "ffn_backward",
        (idx, g, x, r2, y1, r1, vec, ur, gp) + pieces,
        [shape(t, d), shape(16, d), shape(t, d, dtype=BF16)] + sums,
        [
            pltpu.VMEM((t, d), g.dtype),
            pltpu.VMEM((t, d), F32),
            pltpu.VMEM((t, 1), F32),
            pltpu.VMEM((t, d), F32),
            pltpu.VMEM((t, 1), F32),
            pltpu.VMEM(vec.shape, F32),
            pltpu.VMEM((4, d, d), BF16),
            pltpu.VMEM((4 * d, d), BF16),
            pltpu.VMEM((4, d, d), BF16),
            pltpu.VMEM((4, t, d), BF16),
            pltpu.VMEM((4, t, d), BF16),
            pltpu.VMEM((t, d), F32),
            pltpu.VMEM((t, d), BF16),
            pltpu.VMEM((t, d), BF16),
            pltpu.VMEM((8, d, d), BF16),
            pltpu.VMEM((t, d), BF16),
            pltpu.VMEM((16, d), F32),
        ],
        32 * t * d * d,
        (2, 2, 2, 5, 4, 4, 4, 8, 5, 2),
    )


def ffn_both_kernel(idx, y1_ref, r1_ref, g_ref, vec_ref, *refs):
    given, refs = refs[:-32], refs[-32:]
    attn, given = (given[:1], given[:1]) if len(given) < 16 else (given[8:16], given[:8])
    x_ref, dh1_ref, small_ref, da_ref, sums = refs[:5]
    y1, r1, g, vec, we, wc, w, ur, gp, acc, x, n2, e2, y1r, stage, da, small = refs[5:22]
    sem_y, sem_r, sem_g, sem_vec, sem_e, sem_c, sem_w, sem_x, sem_d, sem_a = refs[22:]
    d = y1.shape[1]
    halves = halves_of(y1)
    load_y = load_halves(y1_ref, y1, sem_y, 0)
    load_vec = copy(vec_ref, vec, sem_vec.at[0])
    load_vec.start()
    fetch_ffn(idx, given, 0, we, sem_e)
    fetch_ffn(idx, given, 1, wc, sem_c)
    load_g = load_halves(g_ref, g, sem_g, 0)
    load_r = load_halves(r1_ref, r1, sem_r, 0)
    fetch_attn(idx, attn, w, sem_w, (-1, 1))
    small[...] = jnp.zeros_like(small)
    load_vec.wait()
    for n, rows in enumerate(halves):
        load_y[n].wait()
        y1r[rows] = y1[rows].astype(BF16)
    for j in range(4):
        cols = slice(j * d, (j + 1) * d)
        wait_square(we, sem_e, j)
        for n, rows in enumerate(halves):
            u, slope = gelu_pair(mm(y1r[rows], we[j]) + vec[5 + j : 6 + j])
            u = u.astype(BF16)
            ur[j, rows] = u
            gp[j, rows] = slope.astype(BF16)
            if j == 0 and n == 0:
                wait_rows(wc, sem_c)
            part = mm(u, wc[cols])
            if j == 0:
                acc[rows] = part
            else:
                acc[rows] += part
    saves = []
    for n, rows in enumerate(halves):
        normed, inv = norm_rows(y1[rows] + (acc[rows] + vec[9:10]))
        x[rows] = normed * vec[10:11] + vec[11:12]
        saves.append(copy(x.at[rows], x_ref.at[rows], sem_x.at[n]))
        saves[-1].start()
        load_g[n].wait()
        grad = g[rows].astype(F32)
        add_small(small, 8, grad * normed)
        add_small(small, 9, grad)
        back = norm_rows_back(grad, normed, inv, vec[10:11])
        low = back.astype(BF16)
        add_small(small, 7, low)
        acc[rows] = back
        e2[rows] = low
    for j in range(4):
        cols = slice(j * d, (j + 1) * d)
        stage[4 + j] = tn(ur[j], e2[...]).astype(BF16)

        def go(b, carry):
            send_rows(idx, stage.at[4 + j, rows_of(b)], 4 * j + b // 4, b // 2 % 2, b % 2, 1, (sums,), sem_a.at[0])
            return carry

        lax.fori_loop(0, 16, go, 0)
        for rows in halves:
            ef = (nt(e2[rows], wc[cols]) * gp[j, rows].astype(F32)).astype(BF16)
            gp[j, rows] = ef
            add_small(small, 3 + j, ef)
        stage[j] = tn(y1r[...], gp[j]).astype(BF16)
        send_square(idx, stage.at[j], j // 2, j % 2, 0, (sums,), sem_a.at[1])
        for rows in halves:
            acc[rows] += nt(gp[j, rows], we[j])
    wait_square(w, sem_w, 3)
    inv_gain = 1.0 / vec[3:4]
    for n, rows in enumerate(halves):
        load_r[n].wait()
        grad, normed = acc[rows], (y1[rows] - vec[4:5]) * inv_gain
        add_small(small, 1, grad * normed)
        add_small(small, 2, grad)
        back = norm_rows_back(grad, normed, r1[rows], vec[3:4])
        n2[rows] = back
        low = back.astype(BF16)
        add_small(small, 0, low)
        da[rows] = nt(low, w[3]).astype(BF16)
        saves += [copy(n2.at[rows], dh1_ref.at[rows], sem_d.at[n]), copy(da.at[rows], da_ref.at[rows], sem_d.at[2 + n])]
        saves[-2].start()
        saves[-1].start()
    saves.append(copy(small, small_ref, sem_d.at[4]))
    saves[-1].start()
    for save in saves:
        save.wait()
    copy(stage.at[4:8], stage.at[4:8], sem_a.at[0]).wait()
    copy(stage.at[0:4], stage.at[0:4], sem_a.at[1]).wait()


def ffn_both(idx, y1, r1, g, vec, ffn_pieces, attn_pieces):
    t, d = y1.shape
    pieces = tuple(ffn_pieces) + tuple(attn_pieces) if len(ffn_pieces) == 8 else tuple(ffn_pieces)
    return call(
        ffn_both_kernel,
        "ffn_both",
        (idx, y1, r1, g, vec) + pieces,
        [shape(t, d), shape(t, d), shape(16, d), shape(t, d, dtype=BF16)] + sums_shapes(d, True, 2),
        [
            pltpu.VMEM((t, d), F32),
            pltpu.VMEM((t, 1), F32),
            pltpu.VMEM((t, d), g.dtype),
            pltpu.VMEM(vec.shape, F32),
            pltpu.VMEM((4, d, d), BF16),
            pltpu.VMEM((4 * d, d), BF16),
            pltpu.VMEM((4, d, d), BF16),
            pltpu.VMEM((4, t, d), BF16),
            pltpu.VMEM((4, t, d), BF16),
            pltpu.VMEM((t, d), F32),
            pltpu.VMEM((t, d), F32),
            pltpu.VMEM((t, d), F32),
            pltpu.VMEM((t, d), BF16),
            pltpu.VMEM((t, d), BF16),
            pltpu.VMEM((8, d, d), BF16),
            pltpu.VMEM((t, d), BF16),
            pltpu.VMEM((16, d), F32),
        ],
        48 * t * d * d,
        (2, 2, 2, 1, 4, 4, 4, 2, 5, 2),
    )


def heads_backward_kernel(idx, da_ref, qkv_ref, p_ref, back_ref, small_ref, da, qkv, back, small, p, sem_in, sem_p, sem_out):
    t, d = da.shape
    length = t // 2
    pairs = d // (2 * HEAD_DIM)
    factor = HEAD_DIM**-0.5
    even = even_lanes()

    def load(step, slot):
        return copy(p_ref.at[pl.ds(2 * step, 2)], p.at[slot], sem_p.at[slot])

    load(0, 0).start()
    loads = load_halves(da_ref, da, sem_in, 0)
    for n, rows in enumerate(halves_of(da)):
        loads.append(copy(qkv_ref.at[:, rows], qkv.at[:, rows], sem_in.at[2 + n]))
        loads[-1].start()
    for n, rows in enumerate(halves_of(da)):
        loads[n].wait()
        loads[2 + n].wait()

        def pair(j, carry, n=n):
            step = n * pairs + j
            slot = step % 2

            @pl.when(step + 1 < 2 * pairs)
            def _():
                load(step + 1, 1 - slot).start()

            load(step, slot).wait()
            lanes = pl.ds(pl.multiple_of(j * 2 * HEAD_DIM, 2 * HEAD_DIM), 2 * HEAD_DIM)
            q2, k2, v2 = (qkv[i, n * length : (n + 1) * length, lanes] for i in range(3))
            da2 = da[n * length : (n + 1) * length, lanes]
            masks = (even, jnp.logical_not(even))
            k2t = k2.T
            dps = [nt(v2, jnp.where(mine, da2, jnp.zeros_like(da2))) for mine in masks]
            softs = [p[slot, h] for h in range(2)]
            dss = []
            for soft, dp in zip(softs, dps):
                soft = soft.astype(F32)
                inner = jnp.sum(soft * dp, axis=0, keepdims=True)
                dss.append((soft * (dp - inner)).astype(BF16))
            dv = jnp.where(even, mm(softs[0], da2), mm(softs[1], da2))
            dk = jnp.where(even, mm(dss[0], q2), mm(dss[1], q2))
            dq = jnp.concatenate([mm(k2t[h * HEAD_DIM : (h + 1) * HEAD_DIM], dss[h]) for h in range(2)], axis=0).T
            back[0, n * length : (n + 1) * length, lanes] = (dq * factor).astype(BF16)
            back[1, n * length : (n + 1) * length, lanes] = (dk * factor).astype(BF16)
            back[2, n * length : (n + 1) * length, lanes] = dv.astype(BF16)
            return carry

        lax.fori_loop(0, pairs, pair, 0)
        copy(back.at[:, rows], back_ref.at[:, rows], sem_out.at[n]).start()
    small[0:1] = jnp.sum(back[0].astype(F32), axis=0, keepdims=True)
    small[1:2] = jnp.sum(back[2].astype(F32), axis=0, keepdims=True)
    save = copy(small, small_ref, sem_out.at[2])
    save.start()
    for n, rows in enumerate(halves_of(da)):
        copy(back.at[:, rows], back_ref.at[:, rows], sem_out.at[n]).wait()
    save.wait()


def heads_backward(idx, da, qkv, p):
    t, d = da.shape
    length = t // 2
    return call(
        heads_backward_kernel,
        "heads_backward",
        (idx, da, qkv, p),
        [shape(3, t, d, dtype=BF16), shape(8, d)],
        [
            pltpu.VMEM((t, d), BF16),
            pltpu.VMEM((3, t, d), BF16),
            pltpu.VMEM((3, t, d), BF16),
            pltpu.VMEM((8, d), F32),
            pltpu.VMEM((2, 2, length, length), BF16),
        ],
        30 * t * length * d,
        (4, 2, 3),
    )


def inward_backward_kernel(count, idx, dh1_ref, x_ref, att_ref, back_ref, *refs):
    given, refs = refs[: -(16 + count)], refs[-(16 + count) :]
    dx_ref = refs[0]
    sums, refs = refs[1 : 1 + count], refs[1 + count :]
    dh1, x, att, back, w, stage, dx, sem_d, sem_x, sem_a, sem_b, sem_w, sem_out, sem_s, _ = refs[:15]
    halves = halves_of(x)
    load_x = load_halves(x_ref, x, sem_x, 0)
    load_b = [copy(back_ref.at[i], back.at[i], sem_b.at[i]) for i in range(3)]
    for load in load_b:
        load.start()
    fetch_attn(idx, given, w, sem_w, (None, 0))
    load_d = load_halves(dh1_ref, dh1, sem_d, 0)
    load_a = copy(att_ref, att, sem_a.at[0])
    load_a.start()
    for load in load_x:
        load.wait()
    xr = x[...].astype(BF16)
    for i, (core, s) in enumerate(((0, 0), (1, 0), (0, 1))):
        load_b[i].wait()
        stage[i] = tn(xr, back[i]).astype(BF16)
        send_square(idx, stage.at[i], core, s, 0, sums, sem_s.at[0])
    for load in load_d:
        load.wait()
    load_a.wait()
    stage[3] = tn(att[...], dh1[...].astype(BF16)).astype(BF16)
    send_square(idx, stage.at[3], 1, 1, 0, sums, sem_s.at[0])
    for i in range(3):
        wait_square(w, sem_w, i)
    saves = []
    for n, rows in enumerate(halves):
        dx[rows] = dh1[rows] + (nt(back[0, rows], w[0]) + nt(back[1, rows], w[1]) + nt(back[2, rows], w[2]))
        saves.append(copy(dx.at[rows], dx_ref.at[rows], sem_out.at[n]))
        saves[-1].start()
    for save in saves:
        save.wait()
    copy(stage, stage, sem_s.at[0]).wait()


def inward_backward(whole, idx, dh1, x, att, back, pieces):
    t, d = dh1.shape
    sums = sums_shapes(d, whole)
    return call(
        partial(inward_backward_kernel, len(sums)),
        "inward_backward",
        (idx, dh1, x, att, back) + tuple(pieces),
        [shape(t, d)] + sums,
        [
            pltpu.VMEM((t, d), F32),
            pltpu.VMEM((t, d), x.dtype),
            pltpu.VMEM((t, d), BF16),
            pltpu.VMEM((3, t, d), BF16),
            pltpu.VMEM((4, d, d), BF16),
            pltpu.VMEM((4, d, d), BF16),
            pltpu.VMEM((t, d), F32),
        ],
        14 * t * d * d,
        (2, 2, 1, 3, 4, 2, 1, 1),
    )


BITS = {"c": 1, "y": 2, "x": 4, "z1": 8, "z2": 16, "z3": 24}


def swap(array, by):
    return lax.ppermute(array, AXES, [(i, i ^ BITS[by]) for i in range(32)])


def tie(values, *others):
    return lax.optimization_barrier((values, others))[0]


def pair_up(share):
    return jnp.stack([share, swap(share, "z3")])


def column_up(pair):
    return jnp.concatenate([pair, swap(pair, "z1")])


def near_up(cols):
    return tuple(jnp.concatenate([col, swap(col, by)]) for col, by in zip(cols, "xy"))


def far_up(near):
    return tuple(swap(piece, by) for piece, by in zip(near, "yx"))


def other_core(pieces):
    return tuple(swap(piece, "c") for piece in pieces)


def in_order(near, far, near_c, far_c):
    return sum(((near[s], far[s], near_c[s], far_c[s]) for s in range(2)), ())


def place_small(qb, vb, ob, ag, ash, eb, cb, fg, fs, width, device):
    layers, rows = qb.shape
    lanes = lax.broadcasted_iota(jnp.int32, (1, 1, width), 2)
    thin = jnp.stack([qb, vb, ob, ag, ash, cb, fg, fs], axis=1).astype(F32)
    thin = jnp.where(lanes // rows == device, jnp.tile(thin, (1, 1, width // rows)), 0.0)
    lines = lax.broadcasted_iota(jnp.int32, (1, 4, width), 1)
    wide = jnp.tile(eb.astype(F32)[:, None], (1, 4, width // eb.shape[1]))
    wide = jnp.where(lines * (width // eb.shape[1]) + lanes // eb.shape[1] == device, wide, 0.0)
    return jnp.concatenate([thin[:, 0:5], wide, thin[:, 5:8], jnp.zeros((layers, 4, width), F32)], axis=1)


def own_small(total, rows, device):
    layers, _, width = total.shape
    thin = lax.dynamic_slice_in_dim(total, device * rows, rows, 2)
    count = width // (4 * rows)
    wide = lax.dynamic_slice(total, (0, 5 + device // count, device % count * 4 * rows), (layers, 1, 4 * rows))
    return [thin[:, i] for i in range(5)] + [wide[:, 0]] + [thin[:, i] for i in range(9, 12)]


def add_swap(array, by):
    return array + swap(array, by)


class Sums:
    def __init__(self, keep, give):
        self.both = [keep]
        self.parts = [[], []]
        self.give = give

    def total(self, s, lo, hi):
        whole = None
        for a in [b[s] for b in self.both] + self.parts[s]:
            a = a[lo:hi].astype(F32)
            whole = a if whole is None else whole + a
        return whole

    def latest(self):
        return self.parts if self.parts[0] else self.both

    def hold(self, *others):
        if self.parts[0]:
            self.parts = tie(self.parts, *others)
        else:
            self.both = tie(self.both, *others)

    def core(self):
        self.both = self.both + [swap(self.give, "c")]

    def plane(self, lo, bys):
        arrived = [swap(self.total(s, lo, 2 * lo).astype(BF16), bys[s]) for s in range(2)]
        for s in range(2):
            self.parts[s] = self.parts[s] + [arrived[s]]

    def first(self):
        self.plane(8, "yx")

    def second(self):
        self.plane(4, "xy")

    def line(self, lo, by):
        arrived = swap(jnp.stack([self.total(s, lo, 2 * lo) for s in range(2)]).astype(BF16), by)
        for s in range(2):
            self.parts[s] = self.parts[s] + [arrived[s]]

    def third(self):
        self.line(2, "z1")

    def fourth(self):
        self.line(1, "z3")

    def result(self):
        return jnp.stack([self.total(s, 0, 1)[0] for s in range(2)])


def front(first, last, rows, width, c, attention):
    layers = first.shape[0]
    first = first.reshape(layers, rows, -1)
    cut = lambda i: first[:, :, i * width : (i + 1) * width]
    if attention:
        zero, one = (cut(0), cut(2)), (cut(1), last.reshape(layers, rows, width))
    else:
        zero, one = (cut(0), cut(1)), (cut(2), cut(3))
    zero, one = jnp.stack(zero, 1), jnp.stack(one, 1)
    return jnp.where(c == 0, zero, one), jnp.where(c == 0, one, zero)


def both_cores(mine, got, c):
    return jnp.where(c == 0, jnp.concatenate([mine, got], 2), jnp.concatenate([got, mine], 2))


def gather_any(w_inward, w_outward, w_expand, w_contract, width):
    whole = lambda m, n: lax.all_gather(m, AXES, axis=0, tiled=True).reshape(-1, n)
    inward, outward = whole(w_inward, 3 * width), whole(w_outward, width)
    expand, contract = whole(w_expand, 4 * width), whole(w_contract, width)
    cut = lambda m, i: m[:, i * width : (i + 1) * width].reshape(16, SHARE, width)
    squares = [cut(inward, i) for i in range(3)] + [cut(outward, 0)] + [cut(expand, i) for i in range(4)]
    down = contract.reshape(16, 2, 2, SHARE, width)
    sides = []
    for core in range(2):
        pick = (core, 2 + core, 4 + 2 * core, 5 + 2 * core)
        pairs = [squares[i] for i in pick] + [down[:, core, s] for s in range(2)]
        sides.append(jnp.stack(pairs, 1).reshape(16, 3, 2, SHARE, width))
    return jnp.stack(sides, 1).reshape(32, 3, 2, SHARE, width)


def collect_any(attn, ffn, width):
    attn = attn.reshape(16, 2, 2, SHARE, width)
    ffn = ffn.reshape(16, 2, 2, 2, SHARE, width)
    expand, contract = ffn[:, :, :, 0], ffn[:, :, :, 1]
    inward = jnp.concatenate([attn[:, 0, 0], attn[:, 1, 0], attn[:, 0, 1]], axis=-1)
    expand = jnp.concatenate([expand[:, core, s] for core in range(2) for s in range(2)], axis=-1)
    return tuple(
        lax.psum_scatter(m.reshape(-1).astype(F32), AXES, scatter_dimension=0, tiled=True)
        for m in (inward, attn[:, 1, 1], expand, contract)
    )


def local(blocked, tokens, lengths, w_inward, qb, vb, w_outward, ob, ag, ash, w_expand, eb, w_contract, cb, fg, fs, cotangent):
    layers = w_inward.shape[0]
    width = tokens.shape[-1]
    rows = qb.shape[1]
    device = lax.axis_index("wide") * lax.axis_size("narrow") + lax.axis_index("narrow")
    me = device if blocked else jnp.int32(0)
    c = me & 1
    place = jnp.stack([me >> 3, (me >> 2) & 1, (me >> 1) & 1, c]).astype(jnp.int32)
    idx = jnp.concatenate([place, lengths.reshape(-1), jnp.zeros((2,), jnp.int32)])
    small = place_small(qb, vb, ob, ag, ash, eb, cb, fg, fs, width, device)
    x = tokens.reshape(-1, width)
    kept = []

    def keep_layer(x, y1, attn, ffn, attn_pieces, ffn_pieces):
        kept.append((x, y1) + tuple(attn[1:]) + tuple(ffn) + (attn_pieces, ffn_pieces))
        return ffn[0]

    if blocked:
        mine, got = front(w_inward, w_outward, rows, width, c, True)
        halves = lambda col: (col[:, 0, None], col[:, 1, None])
        halves2 = lambda col: (col[:, :, 0], col[:, :, 1])
        share_a = both_cores(mine, swap(got, "c"), c)
        small = add_swap(small, "c")
        mine, got = front(w_expand, None, rows, width, c, False)
        share_e = both_cores(mine, swap(got, "c"), c)
        contract = w_contract.reshape(layers, 2, SHARE, width)
        share_f = [jnp.stack([share_e[l], contract[l]]) for l in range(layers)]
        a_pair = pair_up(share_a[0])
        share, a_pair, small = tie((share_f[0], a_pair, small))
        f_pair = pair_up(share)
        a_col = column_up(a_pair)
        small = add_swap(small, "z1")
        f_pair, a_col, small = tie((f_pair, a_col, small))
        f_col = column_up(f_pair)
        a_near = near_up(halves(a_col))
        small = add_swap(small, "z2")
        a_near, small = tie((a_near, small))
        a_far = far_up(a_near)
        a_core = other_core(a_near)
        f_col, a_far, small = tie((f_col, a_far, small))
        f_near = near_up(halves2(f_col))
        small = add_swap(small, "x")
        a1_pair = pair_up(tie((share_a[1], a_far))[0])
        a_core += other_core(a_far)
        x, f_near, a1_pair, small = tie((x, f_near, a1_pair, small))
        f_far = far_up(f_near)
        small = add_swap(small, "y")
        a1_col = column_up(a1_pair)
        f_core = other_core(f_near)
        vecs = [small[l] for l in range(layers)]
        a_pieces = in_order(a_near, a_far, a_core[:2], a_core[2:])
        attn = attn_forward(idx, x, vecs[0], a_pieces)
        f_far, a1_col, f_core, y1, share = tie((f_far, a1_col, f_core, attn[0], share_f[1]))
        f_core += other_core(f_far)
        a1_near = near_up(halves(a1_col))
        f1_pair = pair_up(share)
        y1, a1_near, f1_pair, f_core = tie((y1, a1_near, f1_pair, f_core))
        a1_far = far_up(a1_near)
        f1_col = column_up(f1_pair)
        y1, f1_col = tie((y1, f1_col))
        f1_near = near_up(halves2(f1_col))
        f_pieces = in_order(f_near, f_far, f_core[:2], f_core[2:])
        ffn = ffn_forward(idx, y1, vecs[0], f_pieces)
        x1 = keep_layer(x, y1, attn, ffn, a_pieces, f_pieces)
        a1_far, f1_near, x1 = tie((a1_far, f1_near, x1))
        a1_core = other_core(a1_near + a1_far)
        f1_far = far_up(f1_near)
        f1_core = other_core(f1_near)
        a1_pieces = in_order(a1_near, a1_far, a1_core[:2], a1_core[2:])
        attn = attn_forward(idx, x1, vecs[1], a1_pieces)
        f1_far, f1_core, y1 = tie((f1_far, f1_core, attn[0]))
        f1_core += other_core(f1_far)
        f1_pieces = in_order(f1_near, f1_far, f1_core[:2], f1_core[2:])
        output, dh1, small, da, whole = ffn_both(idx, y1, attn[1], cotangent.reshape(-1, width), vecs[1], f1_pieces, a1_pieces)
        keep_layer(x1, y1, attn, (output, None, None, None), a1_pieces, f1_pieces)
    else:
        small = lax.psum(small, AXES)
        vecs = [small[l] for l in range(layers)]
        for l in range(layers):
            pieces = (gather_any(w_inward[l], w_outward[l], w_expand[l], w_contract[l], width),)
            attn = attn_forward(idx, x, vecs[l], pieces)
            if l + 1 < layers:
                x = keep_layer(x, attn[0], attn, ffn_forward(idx, attn[0], vecs[l], pieces), pieces, pieces)
        output, dh1, small, da, whole = ffn_both(idx, attn[0], attn[1], cotangent.reshape(-1, width), vecs[l], pieces, pieces)
        keep_layer(x, attn[0], attn, (output, None, None, None), pieces, pieces)
    w_sums, smalls = [None] * layers, [None] * layers

    def ffn_back(l, g):
        x, y1, r1, qkv, p, att, out, r2, ur, gp, attn_pieces, ffn_pieces = kept[l]
        return ffn_backward(not blocked, idx, g, out, r2, y1, r1, vecs[l], ur, gp, ffn_pieces, attn_pieces)

    def heads_back(l, da):
        x, y1, r1, qkv, p, att, out, r2, ur, gp, attn_pieces, ffn_pieces = kept[l]
        return heads_backward(idx, da, qkv, p)

    def inward_back(l, dh1, back):
        x, y1, r1, qkv, p, att, out, r2, ur, gp, attn_pieces, ffn_pieces = kept[l]
        return inward_backward(not blocked, idx, dh1, x, att, back, attn_pieces)

    if blocked:
        f1 = lax.psum_scatter(whole, AXES, scatter_dimension=0, tiled=True)
        back, small_h = heads_back(1, da)
        smalls[1] = jnp.concatenate([small_h[0:2], small[0:10]])
        g, *sums = inward_back(1, dh1, back)
        a1 = Sums(*sums)
        a1.core()
        dh1, small, da, *sums = ffn_back(0, g)
        f0 = Sums(*sums)
        da, f0.give, a1.both = tie((da, f0.give, a1.both))
        f0.core()
        a1.first()
        back, small_h = heads_back(0, da)
        smalls[0] = jnp.concatenate([small_h[0:2], small[0:10]])
        back, a1.parts, f0.both = tie((back, a1.parts, f0.both))
        f0.first()
        a1.second()
        g, *sums = inward_back(0, dh1, back)
        a0 = Sums(*sums)
        a0.give, a1.parts, f0.parts = tie((a0.give, a1.parts, f0.parts))
        a0.core()
        f0.second()
        a1.third()
        a0.both, a1.parts = tie((a0.both, a1.parts))
        a0.first()
        a1.fourth()
        small, f0.parts = tie((jnp.stack(smalls), f0.parts))
        f0.third()
        small = add_swap(small, "z2")
        small, a0.parts, f1 = tie((small, a0.parts, f1))
        a0.second()
        small = add_swap(small, "x")
        small, a0.parts, f0.parts = tie((small, a0.parts, f0.parts))
        a0.third()
        f0.fourth()
        small = add_swap(small, "y")
        small, a0.parts, f0.parts = tie((small, a0.parts, f0.parts))
        a0.fourth()
        small = add_swap(small, "z1")
        small, a0.parts = tie((small, a0.parts))
        small = add_swap(small, "c")
        f1 = f1[0].astype(F32)
        f0 = f0.result()
        a0, a1 = (m.result()[:, 0] for m in (a0, a1))
        w_sums = [(a0, f0[:, 0], f0[:, 1]), (a1, f1[:, 0], f1[:, 1])]
    else:
        for l in reversed(range(layers)):
            if l + 1 < layers:
                dh1, small, da, whole = ffn_back(l, g)
            back, small_h = heads_back(l, da)
            g, sums_a = inward_back(l, dh1, back)
            smalls[l] = jnp.concatenate([small_h[0:2], small[0:10]])
            w_sums[l] = collect_any(sums_a, whole, width)
        small = lax.psum(jnp.stack(smalls), AXES)
    names = ("qb", "vb", "ob", "ag", "as", "eb", "cb", "fg", "fs")
    outs = dict(zip(names, own_small(small, rows, device)))
    flat = {"in": [], "out": [], "ex": [], "co": []}
    for l in range(layers):
        if not blocked:
            for name, share in zip(("in", "out", "ex", "co"), w_sums[l]):
                flat[name].append(share)
            continue
        attn, expand, contract = w_sums[l]
        squares = jnp.stack([attn[0], attn[1], expand[0], expand[1]])
        low, high = squares[:, :rows], squares[:, rows:]
        mine = jnp.where(c == 0, low, high)
        got = swap(jnp.where(c == 0, high, low), "c")
        zero, one = jnp.where(c == 0, mine, got), jnp.where(c == 0, got, mine)
        flat["in"].append(jnp.concatenate([zero[0], one[0], zero[1]], axis=1).reshape(-1))
        flat["out"].append(one[1].reshape(-1))
        flat["ex"].append(jnp.concatenate([zero[2], zero[3], one[2], one[3]], axis=1).reshape(-1))
        flat["co"].append(contract.reshape(-1))
    flat = {k: jnp.stack(v) for k, v in flat.items()}
    shape = tokens.shape
    return (
        output.reshape(shape), g.reshape(shape), flat["in"], outs["qb"], outs["vb"], flat["out"], outs["ob"],
        outs["ag"], outs["as"], flat["ex"], outs["eb"], flat["co"], outs["cb"], outs["fg"], outs["fs"],
    )


def solution(mesh):
    flat = P(None, AXES)
    deep = P(None, AXES, None, None)
    blocked = mesh.shape["wide"] == 8 and mesh.shape["narrow"] == 4
    return jax.shard_map(
        partial(local, blocked),
        mesh=mesh,
        in_specs=(deep,) + (flat,) * 14 + (deep,),
        out_specs=(deep, deep) + (flat,) * 13,
        check_vma=False,
    )
```
